256 devices in a mesh: pts: 128 (over y, z, x_hi, core), quad: 2 (over x_lo).
Axes of the slice: x: 4 (x_hi: 2, x_lo: 2; x = x_hi * 2 + x_lo), y: 4, z: 8, core: 2. Of those that a mesh axis runs over, the one named last changes fastest.
Arguments:
- features: bfloat16 [262144, 256], P(('pts', 'quad')), may hold values from -6 to 6
- cotangent: bfloat16 [262144, 256], P(('pts', 'quad')), may hold values from -6 to 6
- morton_target: int32 [262144], P(('pts', 'quad')), may hold values from 0 to 262143, as said below
- morton_source: int32 [262144], P(('pts', 'quad')), may hold values from 0 to 262143, as said below
- counts: int32 [8192], P(('pts', 'quad')), may hold values from 8 to 32
- w_qkv: bfloat16 [256, 768], replicated
- w_proj: bfloat16 [256, 256], replicated, may hold values from -0.375 to 0.375
- w_up: bfloat16 [256, 1024], replicated, may hold values from -0.375 to 0.375
- w_down: bfloat16 [1024, 256], replicated, may hold values from -0.1875 to 0.1875
- gain_one: float32 [256], replicated, may hold values from 0.5 to 1.5
- gain_two: float32 [256], replicated, may hold values from 0.5 to 1.5
Outputs:
- grad_features: bfloat16 [262144, 256], P(('pts', 'quad'))
- grad_qkv: float32 [256, 768], replicated
- grad_proj: float32 [256, 256], replicated
- grad_up: float32 [256, 1024], replicated
- grad_down: float32 [1024, 256], replicated
- grad_gain_one: float32 [256], replicated
- grad_gain_two: float32 [256], replicated
The draws below stay inside these ranges and needn't reach their ends.
Inputs may be any that keep to these rules, and one draw needn't show every extreme that they name: `morton_target`: A permutation of the 262144 Morton positions. A point stored on the device with indices pts = d, quad = q lands on a position held by a device with quad = q, and each device sends exactly 8 of its points to each device with its quad index. The inverse permutation of morton_target: morton_target[morton_source[n]] = n.
All inputs are finite; a program needn't handle non-finite values.
Results may differ from the reference program's by a relative error of at most 0.015.
Values may be sent and summed in bfloat16 or wider, within the bound.
A program may use at most 64 MiB of HBM per device.

```python
import math
import jax
import jax.numpy as jnp
from jax import lax

CHANNELS = 256
HEADS = 8
FFN_WIDTH = 1024
WINDOW = 32
DILATION = 4
POINTS_DEV = 1024
POINTS = 262144
N_PTS = 128
N_QUAD = 2


def shuffle_points(sub_key):
    return jax.random.permutation(sub_key, POINTS_DEV).astype(jnp.int32)


def morton_tables(key):
    share = POINTS_DEV // N_PTS
    block_total = N_PTS * N_QUAD
    send_key, slot_key = jax.random.split(key)
    shuffled = jax.vmap(shuffle_points)(jax.random.split(send_key, block_total))
    grouped = jnp.sort(jnp.argsort(shuffled, axis=1).reshape(block_total, N_PTS, share), axis=2)
    grouped = grouped.reshape(block_total, POINTS_DEV)
    place_in_list = jnp.argsort(grouped, axis=1).astype(jnp.int32)
    target_device = place_in_list // share
    within_rank = place_in_list % share
    sender = jnp.arange(block_total, dtype=jnp.int32)[:, None]
    receiver = target_device * N_QUAD + sender % N_QUAD
    arrival_rank = sender // N_QUAD * share + within_rank
    slot_tables = jax.vmap(shuffle_points)(jax.random.split(slot_key, block_total))
    local_slot = slot_tables[receiver, arrival_rank]
    target = (receiver * POINTS_DEV + local_slot).reshape(-1).astype(jnp.int32)
    source = jnp.zeros((POINTS,), jnp.int32).at[target].set(jnp.arange(POINTS, dtype=jnp.int32))
    return (target, source)


def draw_morton_target(key, part):
    tables = morton_tables(key)
    return tables[0]


def draw_morton_source(key, part):
    tables = morton_tables(key)
    return tables[1]


def draw_w_qkv(key, part):
    key = jax.random.fold_in(key, 11)
    weight_key = jax.random.fold_in(key, 0)
    base = jax.random.normal(weight_key, (CHANNELS, 3 * CHANNELS), jnp.float32) / math.sqrt(CHANNELS)
    return base.astype(jnp.bfloat16)


def plant(array, rng, smallest, top_value):
    dims = array.shape
    spot = [jax.random.randint(jax.random.fold_in(rng, axis), (), 0, dims[axis]) for axis in range(len(dims))]
    array = array.at[tuple(spot)].set(smallest)
    longest = dims.index(max(dims))
    spot[longest] = (spot[longest] + 1) % dims[longest]
    return array.at[tuple(spot)].set(top_value)


def block_levels(rng, extent, cuts, least, high):
    factor_of, own = 1.0, jax.random.fold_in(rng, 6)
    for dim, blocks in cuts:
        draws = jnp.exp(jax.random.uniform(jax.random.fold_in(own, dim), (blocks,), jnp.float32, least / len(cuts), high / len(cuts)))
        factor_of = factor_of * jnp.repeat(draws, extent[dim] // blocks).reshape([-1 if axis == dim else 1 for axis in range(len(extent))])
    return factor_of


def gaussian(own_key, dims, scale, reach, cuts=(), kind=jnp.bfloat16):
    drawn = jax.random.normal(own_key, dims, jnp.float32) * scale
    if len(cuts) > 0:
        drawn = block_levels(own_key, dims, cuts, -0.22, 0.18) * drawn
    return jnp.clip(drawn, min=-reach, max=reach).astype(kind)


def setup_inputs(seed: int = 0) -> dict:
    key_list = jax.random.split(jax.random.key(seed), 12)
    features = gaussian(key_list[0], (POINTS, CHANNELS), 1.0, 6.0, ((0, 256),))
    cotangent = gaussian(key_list[1], (POINTS, CHANNELS), 1.0, 6.0, ((0, 256),))
    morton_target = draw_morton_target(jax.random.fold_in(key_list[11], 71), 0)
    morton_source = draw_morton_source(jax.random.fold_in(key_list[11], 71), 0)
    counts = plant(jax.random.randint(key_list[4], (POINTS // WINDOW,), 8, WINDOW + 1), jax.random.fold_in(key_list[4], 1), 8, WINDOW).astype(jnp.int32)
    w_qkv = draw_w_qkv(jax.random.fold_in(key_list[11], 71), 0)
    w_proj = gaussian(key_list[6], (CHANNELS, CHANNELS), CHANNELS ** -0.5, 0.375)
    w_up = gaussian(key_list[7], (CHANNELS, FFN_WIDTH), CHANNELS ** -0.5, 0.375)
    w_down = gaussian(key_list[8], (FFN_WIDTH, CHANNELS), FFN_WIDTH ** -0.5, 0.1875)
    gain_one = jnp.clip(1.0 + 0.1 * jax.random.normal(key_list[9], (CHANNELS,), jnp.float32), 0.5, 1.5)
    gain_two = jnp.clip(1.0 + 0.1 * jax.random.normal(key_list[10], (CHANNELS,), jnp.float32), 0.5, 1.5)
    return dict(features=features, cotangent=cotangent, morton_target=morton_target, morton_source=morton_source, counts=counts, w_qkv=w_qkv, w_proj=w_proj, w_up=w_up, w_down=w_down, gain_one=gain_one, gain_two=gain_two)


NEG_FILL = -1e+30

def batched(form, left, right):
    return jnp.einsum(form, left.astype(jnp.float32), right.astype(jnp.float32))

def cross_rows(left, right):
    return lax.dot_general(left, right, (((0,), (0,)), ((), ())), preferred_element_type=jnp.float32)

def times_transposed(left, right):
    return lax.dot_general(left, right, (((1,), (1,)), ((), ())), preferred_element_type=jnp.float32)

def layer_norm(values_in):
    centred = values_in - lax.optimization_barrier(jnp.mean(values_in, axis=1, keepdims=True))
    inverse = lax.rsqrt(lax.optimization_barrier(jnp.mean(centred * centred, axis=1, keepdims=True)) + 1e-05)
    return (centred * inverse, inverse)

def norm_back(grad_normed, normed, inverse):
    first_mean = lax.optimization_barrier(jnp.mean(grad_normed, axis=1, keepdims=True))
    second_mean = lax.optimization_barrier(jnp.mean(grad_normed * normed, axis=1, keepdims=True))
    return inverse * (grad_normed - first_mean - normed * second_mean)

def window_masks(counts, row_count):
    span = WINDOW * DILATION
    blocks = row_count // span
    position = jnp.arange(span, dtype=jnp.int32)
    residue = position % DILATION
    slot_index = position // DILATION
    window_count = jnp.tile(counts.reshape(blocks, DILATION), (1, WINDOW))
    live_keys = slot_index[None, :] < window_count
    same_class = residue[:, None] == residue[None, :]
    allowed = same_class[None, None, :, :] & live_keys[:, None, None, :]
    return (live_keys.reshape(row_count, 1), allowed)

def forward_pass(features, counts, w_qkv, w_proj, w_up, gain_one, gain_two):
    row_count, channels = features.shape
    span = WINDOW * DILATION
    blocks = row_count // span
    head_dim = channels // HEADS
    scale = 1.0 / math.sqrt(head_dim)
    live_rows, allowed = window_masks(counts, row_count)
    inputs = features.astype(jnp.float32)
    normed_one, inverse_one = layer_norm(inputs)
    hidden_one = (normed_one * gain_one).astype(jnp.bfloat16)
    projected = jnp.dot(hidden_one, w_qkv, preferred_element_type=jnp.float32).astype(jnp.bfloat16)
    split_heads = projected.reshape(blocks, span, 3, HEADS, head_dim)
    queries = split_heads[:, :, 0]
    keys_all = split_heads[:, :, 1]
    values_all = split_heads[:, :, 2]
    scores = batched('bqhe,bkhe->bhqk', queries, keys_all) * scale
    scores = jnp.where(allowed, scores, NEG_FILL)
    row_max = lax.optimization_barrier(jnp.max(scores, axis=3, keepdims=True))
    powered = jnp.exp(scores - row_max)
    weights = powered / lax.optimization_barrier(jnp.sum(powered, axis=3, keepdims=True))
    weights_low = weights.astype(jnp.bfloat16)
    attended = batched('bhqk,bkhe->bqhe', weights_low, values_all)
    attended = attended.astype(jnp.bfloat16).reshape(row_count, channels)
    branch = jnp.dot(attended, w_proj, preferred_element_type=jnp.float32)
    mixed = (inputs + jnp.where(live_rows, branch, 0.0)).astype(jnp.bfloat16)
    normed_two, inverse_two = layer_norm(mixed.astype(jnp.float32))
    hidden_two = (normed_two * gain_two).astype(jnp.bfloat16)
    before = jnp.dot(hidden_two, w_up, preferred_element_type=jnp.float32)
    cumulative = 0.5 * (1.0 + lax.erf(before * 0.7071067811865476))
    activated = (before * cumulative).astype(jnp.bfloat16)
    return {'live_rows': live_rows, 'normed_one': normed_one, 'inverse_one': inverse_one, 'hidden_one': hidden_one, 'queries': queries, 'keys_all': keys_all, 'values_all': values_all, 'weights': weights, 'weights_low': weights_low, 'attended': attended, 'normed_two': normed_two, 'inverse_two': inverse_two, 'hidden_two': hidden_two, 'before': before, 'cumulative': cumulative, 'activated': activated}

def mlp_back(saved, cotangent, w_up, w_down, gain_two):
    before = saved['before']
    grad_down = cross_rows(saved['activated'], cotangent)
    density = jnp.exp(-0.5 * before * before) * 0.3989422804014327
    grad_before = (times_transposed(cotangent, w_down) * (saved['cumulative'] + before * density)).astype(jnp.bfloat16)
    grad_up = cross_rows(saved['hidden_two'], grad_before)
    grad_hidden = times_transposed(grad_before, w_up)
    grad_gain_two = lax.optimization_barrier(jnp.sum(grad_hidden * saved['normed_two'], axis=0))
    grad_mixed = (cotangent.astype(jnp.float32) + norm_back(grad_hidden * gain_two, saved['normed_two'], saved['inverse_two'])).astype(jnp.bfloat16)
    return (grad_mixed, grad_up, grad_down, grad_gain_two)

def attention_back(saved, grad_mixed, w_qkv, w_proj, gain_one):
    row_count, channels = grad_mixed.shape
    span = WINDOW * DILATION
    blocks = row_count // span
    head_dim = channels // HEADS
    scale = 1.0 / math.sqrt(head_dim)
    grad_branch = jnp.where(saved['live_rows'], grad_mixed, jnp.zeros_like(grad_mixed))
    grad_proj = cross_rows(saved['attended'], grad_branch)
    grad_attended = times_transposed(grad_branch, w_proj).astype(jnp.bfloat16).reshape(blocks, span, HEADS, head_dim)
    grad_values = batched('bhqk,bqhe->bkhe', saved['weights_low'], grad_attended)
    grad_weights = batched('bqhe,bkhe->bhqk', grad_attended, saved['values_all'])
    weights = saved['weights']
    grad_scores = (weights * (grad_weights - lax.optimization_barrier(jnp.sum(weights * grad_weights, axis=3, keepdims=True))) * scale).astype(jnp.bfloat16)
    grad_queries = batched('bhqk,bkhe->bqhe', grad_scores, saved['keys_all'])
    grad_keys = batched('bhqk,bqhe->bkhe', grad_scores, saved['queries'])
    grad_projected = jnp.stack([grad_queries, grad_keys, grad_values], axis=2).astype(jnp.bfloat16).reshape(row_count, 3 * channels)
    grad_qkv = cross_rows(saved['hidden_one'], grad_projected)
    grad_hidden = times_transposed(grad_projected, w_qkv)
    grad_gain_one = lax.optimization_barrier(jnp.sum(grad_hidden * saved['normed_one'], axis=0))
    grad_input = (grad_mixed.astype(jnp.float32) + norm_back(grad_hidden * gain_one, saved['normed_one'], saved['inverse_one'])).astype(jnp.bfloat16)
    return (grad_input, grad_qkv, grad_proj, grad_gain_one)

def reference(features, cotangent, morton_target, morton_source, counts, w_qkv, w_proj, w_up, w_down, gain_one, gain_two):
    steps_total = POINTS // POINTS_DEV
    ordered_features = features[morton_source].reshape(steps_total, POINTS_DEV, CHANNELS)
    ordered_cotangent = cotangent[morton_source].reshape(steps_total, POINTS_DEV, CHANNELS)
    block_counts = counts.reshape(steps_total, POINTS_DEV // WINDOW)

    def one_block(totals, pieces):
        piece_features, piece_cotangent, piece_counts = pieces
        saved = forward_pass(piece_features, piece_counts, w_qkv, w_proj, w_up, gain_one, gain_two)
        grad_mixed, grad_up, grad_down, grad_gain_two = mlp_back(saved, piece_cotangent, w_up, w_down, gain_two)
        grad_input, grad_qkv, grad_proj, grad_gain_one = attention_back(saved, grad_mixed, w_qkv, w_proj, gain_one)
        terms = (grad_qkv, grad_proj, grad_up, grad_down, grad_gain_one, grad_gain_two)
        return (jax.tree.map(jnp.add, totals, terms), grad_input)
    start = (jnp.zeros((CHANNELS, 3 * CHANNELS), jnp.float32), jnp.zeros((CHANNELS, CHANNELS), jnp.float32), jnp.zeros((CHANNELS, FFN_WIDTH), jnp.float32), jnp.zeros((FFN_WIDTH, CHANNELS), jnp.float32), jnp.zeros((CHANNELS,), jnp.float32), jnp.zeros((CHANNELS,), jnp.float32))
    totals, grad_blocks = lax.scan(one_block, start, (ordered_features, ordered_cotangent, block_counts))
    grad_features = grad_blocks.reshape(POINTS, CHANNELS)[morton_target]
    grad_scale = 1.0 / math.sqrt(POINTS)
    grad_qkv, grad_proj, grad_up, grad_down, grad_gain_one, grad_gain_two = jax.tree.map(lambda total: total * grad_scale, totals)
    return (grad_features, grad_qkv, grad_proj, grad_up, grad_down, grad_gain_one, grad_gain_two)
```

```python
import functools
import math

import jax
import jax.numpy as jnp
from jax import lax
from jax.experimental import pallas as pl
from jax.experimental.pallas import tpu as pltpu
from jax.sharding import PartitionSpec as P

HEADS = 8
WINDOW = 32
DILATION = 4
ROWS = 1024
CH = 256
FFN = 1024
HD = 32
BLK = 128
TILE = 256
SHARE = 8
NEG_FILL = -1e30
SCALE = 1.0 / math.sqrt(HD)

F32 = jnp.float32
BF16 = jnp.bfloat16
MESH = pl.DeviceIdType.MESH

NY, NZ, NX, NC = 4, 8, 4, 2


def nn(a, b):
    return lax.dot_general(a, b, (((1,), (0,)), ((), ())), preferred_element_type=F32)


def nt(a, b):
    return lax.dot_general(a, b, (((1,), (1,)), ((), ())), preferred_element_type=F32)


def tn(a, b):
    return lax.dot_general(a, b, (((0,), (0,)), ((), ())), preferred_element_type=F32)


def loop(start, stop, body):
    def step(i, carry):
        body(i)
        return carry

    lax.fori_loop(start, stop, step, 0)


def transposed(a):
    return jnp.transpose(a.astype(F32)).astype(a.dtype)


def tile_at(i, size):
    return pl.ds(pl.multiple_of(i * size, size), size)


def norm_rows(values):
    mean = jnp.mean(values, axis=0, keepdims=True)
    centred = values - mean
    inverse = lax.rsqrt(jnp.mean(centred * centred, axis=0, keepdims=True) + 1e-05)
    return centred * inverse, inverse


def norm_back_rows(grad, normed, inverse):
    first = jnp.mean(grad, axis=0, keepdims=True)
    second = jnp.mean(grad * normed, axis=0, keepdims=True)
    return inverse * (grad - first - normed * second)


def pack_windows(dense, window_of_lane):
    packed = dense[3 * WINDOW :]
    for k in (2, 1, 0):
        packed = jnp.where(window_of_lane == k, dense[k * WINDOW : (k + 1) * WINDOW], packed)
    return packed


def spread_windows(packed, diagonal):
    return jnp.concatenate([packed] * DILATION, axis=0) * diagonal


def to_units(y):
    n = y.shape[0] // SHARE
    left = y[:, :128].reshape(n, SHARE, 128)
    right = y[:, 128:].reshape(n, SHARE, 128)
    return jnp.concatenate([left, right], axis=1).astype(BF16)


def from_units(u):
    r = u.astype(F32)
    n = r.shape[0]
    left = r[:, :SHARE, :].reshape(n * SHARE, 128)
    right = r[:, SHARE:, :].reshape(n * SHARE, 128)
    return left, right


def kernel(
    n_pts,
    grad_scale,
    x_ref,
    g_ref,
    tab_ref,
    gains_ref,
    wqkv_ref,
    wproj_ref,
    wup_ref,
    wdown_ref,
    dx_ref,
    oqkv_ref,
    oproj_ref,
    oup_ref,
    odown_ref,
    ogain_ref,
    sendx,
    recvx,
    sendg,
    recvg,
    sendr,
    recvr,
    rank_rows,
    rank_cols,
    gain_cols,
    wqkv_t,
    wproj_t,
    wup_t,
    r_t,
    x_t,
    n1_t,
    h1_t,
    inv_rows,
    proj_t,
    w_t,
    att_t,
    n2_t,
    h2_t,
    act_t,
    dg_t,
    g_t,
    gb_t,
    gm_t,
    gbr_t,
    ga_t,
    gproj_t,
    dx_t,
    gg_cols,
    grad1,
    core1,
    cur1,
    ra1,
    rb1,
    mid1,
    rc1,
    rd1,
    zin1,
    rz1,
    grad2,
    core2,
    cur2,
    ra2,
    rb2,
    mid2,
    rc2,
    rd2,
    rz2,
    gcore,
    gx,
    gy,
    gz,
    a2a_sems,
    core_sems,
    four_send,
    four_recv,
    z_send,
    z_recv,
    gcore_sems,
    gfour_send,
    gfour_recv,
    gz_send,
    gz_recv,
):
    me = lax.axis_index("pts")
    quad = lax.axis_index("quad")
    core = lax.rem(me, NC)
    x_hi = lax.rem(me // NC, 2)
    z = lax.rem(me // (2 * NC), NZ)
    y = me // (2 * NC * NZ)
    x = x_hi * 2 + quad

    def core_dev():
        return {"pts": me + 1 - 2 * core, "quad": quad}

    def x_dev(other):
        return {"pts": me + (other // 2 - x_hi) * NC, "quad": lax.rem(other, 2)}

    def y_dev(other):
        return {"pts": me + (other - y) * (2 * NC * NZ), "quad": quad}

    def z_dev(other):
        return {"pts": me + (other - z) * (2 * NC), "quad": quad}

    barrier = pltpu.get_barrier_semaphore()

    def greet(k):
        pl.semaphore_signal(
            barrier, inc=1, device_id={"pts": lax.rem(me + k, n_pts), "quad": quad}, device_id_type=MESH
        )

    loop(1, n_pts, greet)
    for hi in range(2):
        pl.semaphore_signal(
            barrier,
            inc=1,
            device_id={"pts": me + (hi - x_hi) * NC, "quad": 1 - quad},
            device_id_type=MESH,
        )

    lane_row = lax.broadcasted_iota(jnp.int32, (1, ROWS), 1)
    target_key = (tab_ref[0:1, :] // (2 * ROWS)) * ROWS + lane_row
    source_key = tab_ref[1:2, :]
    pad = jnp.zeros((6, ROWS), F32)
    rank_rows[...] = jnp.concatenate([target_key.astype(F32), source_key.astype(F32), pad], axis=0)
    rank_cols[...] = jnp.transpose(rank_rows[...])

    keys = rank_rows[...]

    def count(i, carry):
        t, s = carry
        cols = rank_cols[tile_at(i, 64), :]
        t = t + jnp.sum(jnp.where(cols[:, 0:1] < keys[0:1, :], 1.0, 0.0), axis=0, keepdims=True)
        s = s + jnp.sum(jnp.where(cols[:, 1:2] < keys[1:2, :], 1.0, 0.0), axis=0, keepdims=True)
        return t, s

    zero_row = jnp.zeros((1, ROWS), F32)
    rank_target, rank_source = lax.fori_loop(0, ROWS // 64, count, (zero_row, zero_row))
    rank_rows[...] = jnp.concatenate([rank_target, rank_source, pad], axis=0)
    rank_cols[...] = jnp.transpose(rank_rows[...])

    def select_rows(first, size, ranks):
        slot = lax.broadcasted_iota(jnp.int32, (size, ranks.shape[1]), 0).astype(F32)
        return jnp.where(slot + first == ranks, 1.0, 0.0).astype(BF16)

    def place(i, source_ref, out):
        pick = select_rows((i * TILE).astype(F32), TILE, rank_rows[0:1, :])
        out[tile_at(i, TILE // SHARE)] = to_units(nn(pick, source_ref[...]))

    def a2a(send, recv, index, k):
        peer = lax.rem(me + k, n_pts)
        return pltpu.make_async_remote_copy(
            src_ref=send.at[peer],
            dst_ref=recv.at[me],
            send_sem=a2a_sems.at[index],
            recv_sem=a2a_sems.at[index + 1],
            device_id={"pts": peer, "quad": quad},
            device_id_type=MESH,
        )

    def a2a_start(send, recv, index):
        pltpu.make_async_copy(send.at[me], recv.at[me], a2a_sems.at[index + 1]).start()
        loop(1, n_pts, lambda j: a2a(send, recv, index, 1 + lax.rem((j - 1) * 37 , n_pts - 1)).start())

    def a2a_wait_recv(recv, index):
        pltpu.make_async_copy(recv, recv, a2a_sems.at[index + 1]).wait()

    def a2a_wait_send(send, index):
        part = send.at[pl.ds(0, n_pts - 1)]
        pltpu.make_async_copy(part, part, a2a_sems.at[index]).wait()

    tiles = ROWS // TILE
    loop(0, tiles, lambda i: place(i, x_ref, sendx))
    pl.semaphore_wait(barrier, n_pts + 1)
    a2a_start(sendx, recvx, 0)
    loop(0, tiles, lambda i: place(i, g_ref, sendg))
    a2a_start(sendg, recvg, 2)

    wqkv_t[...] = transposed(wqkv_ref[...])
    wproj_t[...] = transposed(wproj_ref[...])
    wup_t[...] = transposed(wup_ref[...])
    gain_cols[...] = jnp.transpose(gains_ref[...])
    gain_one = gain_cols[:, 0:1]
    gain_two = gain_cols[:, 1:2]

    sub = lax.broadcasted_iota(jnp.int32, (WINDOW, BLK), 0)
    window_of_lane = lax.broadcasted_iota(jnp.int32, (WINDOW, BLK), 1) // WINDOW
    diagonal = jnp.where(
        lax.broadcasted_iota(jnp.int32, (BLK, BLK), 0) // WINDOW
        == lax.broadcasted_iota(jnp.int32, (BLK, BLK), 1) // WINDOW,
        1.0,
        0.0,
    ).astype(BF16)

    def live_tile(at, size):
        slot = lax.rem(lax.broadcasted_iota(jnp.int32, (1, size), 1), WINDOW)
        return slot < tab_ref[2:3, at]

    def arrive(recv, out):
        left, right = from_units(recv[...])
        r_t[0:128, :] = jnp.transpose(left).astype(BF16)
        r_t[128:256, :] = jnp.transpose(right).astype(BF16)

        def one(i):
            at = tile_at(i, TILE)
            out[:, at] = nn(r_t[...], select_rows(0.0, ROWS, rank_rows[1:2, at])).astype(BF16)

        loop(0, tiles, one)

    a2a_wait_recv(recvx, 0)
    arrive(recvx, x_t)

    def first_norm(i):
        at = tile_at(i, TILE)
        normed, inverse = norm_rows(x_t[:, at].astype(F32))
        n1_t[:, at] = normed
        inv_rows[0:1, at] = inverse
        hidden = (normed * gain_one).astype(BF16)
        h1_t[:, at] = hidden
        proj_t[:, at] = nn(wqkv_t[...], hidden).astype(BF16)

    loop(0, tiles, first_norm)

    def heads_of(ref, at, part, h):
        return ref[part * CH + h * HD : part * CH + (h + 1) * HD, at]

    def attend(b):
        at = tile_at(b, BLK)
        admitted = sub < tab_ref[2:3, at]
        for h in range(HEADS):
            q = heads_of(proj_t, at, 0, h)
            k = heads_of(proj_t, at, 1, h)
            v = heads_of(proj_t, at, 2, h)
            scores = pack_windows(tn(k, q), window_of_lane) * SCALE
            scores = jnp.where(admitted, scores, NEG_FILL)
            powered = jnp.exp(scores - jnp.max(scores, axis=0, keepdims=True))
            weights = powered / jnp.sum(powered, axis=0, keepdims=True)
            w_t[b * HEADS + h] = weights
            wide = spread_windows(weights.astype(BF16), diagonal)
            att_t[h * HD : (h + 1) * HD, at] = nn(v, wide).astype(BF16)

    loop(0, ROWS // BLK, attend)

    def forward_mlp(i):
        at = tile_at(i, TILE)
        branch = nn(wproj_t[...], att_t[:, at])
        mixed = x_t[:, at].astype(F32) + jnp.where(live_tile(at, TILE), branch, 0.0)
        normed, inverse = norm_rows(mixed.astype(BF16).astype(F32))
        n2_t[:, at] = normed
        inv_rows[1:2, at] = inverse
        hidden = (normed * gain_two).astype(BF16)
        h2_t[:, at] = hidden

        def part(f):
            rows = tile_at(f, TILE)
            before = nn(wup_t[rows, :], hidden)
            cumulative = 0.5 * (1.0 + lax.erf(before * 0.7071067811865476))
            act_t[rows, at] = (before * cumulative).astype(BF16)
            density = jnp.exp(-0.5 * before * before) * 0.3989422804014327
            dg_t[rows, at] = cumulative + before * density

        loop(0, FFN // TILE, part)

    loop(0, tiles, forward_mlp)

    a2a_wait_recv(recvg, 2)
    arrive(recvg, g_t)

    def back_act(i):
        at = tile_at(i, TILE)

        def part(f):
            rows = tile_at(f, TILE)
            gb_t[rows, at] = (nn(wdown_ref[rows, :], g_t[:, at]) * dg_t[rows, at]).astype(BF16)

        loop(0, FFN // TILE, part)

    loop(0, tiles, back_act)

    def tiles_of(y, lanes):
        return [y[:, l * 128 : (l + 1) * 128].reshape(16, 16, 128).astype(BF16) for l in range(lanes)]

    def up_down(f):
        rows = tile_at(f, TILE)
        down = nt(act_t[rows, :], g_t[...])
        for l, u in enumerate(tiles_of(down, 2)):
            grad1[pl.ds(128 + f * 32 + l * 16, 16)] = u
        up = nt(h2_t[...], gb_t[rows, :])
        for l, u in enumerate(tiles_of(up, 2)):
            grad1[pl.ds(f * 32 + l * 16, 16)] = u

    loop(0, FFN // TILE, up_down)

    def four_copies(src, dst_of, which, mine, dev, sem_base):
        copies = []
        for d in range(1, 4):
            other = lax.rem(mine + d, 4)
            copies.append(
                pltpu.make_async_remote_copy(
                    src_ref=src(other),
                    dst_ref=dst_of,
                    send_sem=four_send.at[sem_base + which, d],
                    recv_sem=four_recv.at[sem_base + which, mine],
                    device_id=dev(other),
                    device_id_type=MESH,
                )
            )
        return copies

    def four_wait(src, dst, which, mine, dev, sem_base):
        for d in range(1, 4):
            other = lax.rem(mine + d, 4)
            got = pltpu.make_async_remote_copy(
                src_ref=src(other),
                dst_ref=dst(other),
                send_sem=four_send.at[sem_base + which, d],
                recv_sem=four_recv.at[sem_base + which, other],
                device_id=dev(other),
                device_id_type=MESH,
            )
            got.wait_recv()
            got.wait_send()

    def group(index, grad, from_core, cur, ra, rb, mid, rc, rd, nk):
        half = nk * 32
        part = half // 2
        quarter = part // 4
        base = index * 4
        cbase = index * 4

        def core_copy(src, dst, sem):
            return pltpu.make_async_remote_copy(
                src_ref=src,
                dst_ref=dst,
                send_sem=core_sems.at[cbase + sem],
                recv_sem=core_sems.at[cbase + sem + 1],
                device_id=core_dev(),
                device_id_type=MESH,
            )

        def first_core():
            return core_copy(grad.at[pl.ds((1 - core) * half, half)], from_core, 0)

        def s0():
            first_core().start()

        def cur_a(o):
            return cur.at[pl.ds(o * quarter, quarter)]

        def cur_b(o):
            return cur.at[pl.ds(part + o * quarter, quarter)]

        def s1():
            first_core().wait()
            total = grad[pl.ds(core * half, half)].astype(F32) + from_core[...].astype(F32)
            cur[...] = total.astype(BF16)
            for c in four_copies(cur_a, ra.at[x], 0, x, x_dev, base):
                c.start()
            for c in four_copies(cur_b, rb.at[y], 1, y, y_dev, base):
                c.start()

        def mid_a(o):
            return mid.at[pl.ds(o * nk, nk)]

        def mid_b(o):
            return mid.at[pl.ds(quarter + o * nk, nk)]

        def add_four(own, slots, mine):
            total = own.astype(F32)
            for d in range(1, 4):
                total = total + slots[lax.rem(mine + d, 4)].astype(F32)
            return total.astype(BF16)

        def s2():
            four_wait(cur_a, lambda o: ra.at[o], 0, x, x_dev, base)
            four_wait(cur_b, lambda o: rb.at[o], 1, y, y_dev, base)
            mid[pl.ds(0, quarter)] = add_four(cur[pl.ds(x * quarter, quarter)], ra, x)
            mid[pl.ds(quarter, quarter)] = add_four(cur[pl.ds(part + y * quarter, quarter)], rb, y)
            for c in four_copies(mid_a, rc.at[y], 2, y, y_dev, base):
                c.start()
            for c in four_copies(mid_b, rd.at[x], 3, x, x_dev, base):
                c.start()

        def s3():
            four_wait(mid_a, lambda o: rc.at[o], 2, y, y_dev, base)
            four_wait(mid_b, lambda o: rd.at[o], 3, x, x_dev, base)
            a = add_four(mid[pl.ds(y * nk, nk)], rc, y)
            b = add_four(mid[pl.ds(quarter + x * nk, nk)], rd, x)
            return a, b

        mine = core * half

        def out_a(xx, yy):
            return grad.at[pl.ds(mine + xx * quarter + yy * nk, nk)]

        def out_b(xx, yy):
            return grad.at[pl.ds(mine + part + yy * quarter + xx * nk, nk)]

        def whole_a(xx):
            return grad.at[pl.ds(mine + xx * quarter, quarter)]

        def whole_b(yy):
            return grad.at[pl.ds(mine + part + yy * quarter, quarter)]

        gbase = 8 + index * 4

        def s5():
            for c in four_copies(lambda o: out_a(x, y), out_a(x, y), 0, y, y_dev, gbase):
                c.start()
            for c in four_copies(lambda o: out_b(x, y), out_b(x, y), 1, x, x_dev, gbase):
                c.start()

        def s6():
            four_wait(lambda o: out_a(x, y), lambda o: out_a(x, o), 0, y, y_dev, gbase)
            four_wait(lambda o: out_b(x, y), lambda o: out_b(o, y), 1, x, x_dev, gbase)
            for c in four_copies(lambda o: whole_a(x), whole_a(x), 2, x, x_dev, gbase):
                c.start()
            for c in four_copies(lambda o: whole_b(y), whole_b(y), 3, y, y_dev, gbase):
                c.start()

        def last_core():
            at = grad.at[pl.ds(mine, half)]
            return core_copy(at, at, 2)

        def s7():
            four_wait(lambda o: whole_a(x), lambda o: whole_a(o), 2, x, x_dev, gbase)
            four_wait(lambda o: whole_b(y), lambda o: whole_b(o), 3, y, y_dev, gbase)
            last_core().start()

        def s8():
            last_core().wait()

        def put(a, b):
            grad[pl.ds(mine + x * quarter + y * nk, nk)] = a
            grad[pl.ds(mine + part + y * quarter + x * nk, nk)] = b

        return s0, s1, s2, s3, put, s5, s6, s7, s8

    def z_copy(src, dst, sems, d, slot):
        other = lax.rem(z + d, NZ)
        return pltpu.make_async_remote_copy(
            src_ref=src,
            dst_ref=dst,
            send_sem=z_send.at[sems, d],
            recv_sem=z_recv.at[sems, slot],
            device_id=z_dev(other),
            device_id_type=MESH,
        )

    one = group(0, grad1, core1, cur1, ra1, rb1, mid1, rc1, rd1, 4)
    two = group(1, grad2, core2, cur2, ra2, rb2, mid2, rc2, rd2, 2)

    def one_s3():
        a, b = one[3]()
        zin1[0:4] = a
        zin1[4:8] = b
        for d in range(1, NZ):
            z_copy(zin1.at[lax.rem(z + d, NZ)], rz1.at[z], 0, d, z).start()

    def one_out(zz):
        p = zz // 4
        k = lax.rem(zz, 4)
        first = x + p * (y - x)
        second = y + p * (x - y)
        return core * 128 + p * 64 + first * 16 + second * 4 + k

    def one_s4():
        total = zin1[z].astype(F32)
        for d in range(1, NZ):
            other = lax.rem(z + d, NZ)
            got = z_copy(zin1.at[other], rz1.at[other], 0, d, other)
            got.wait_recv()
            got.wait_send()
            total = total + rz1[other].astype(F32)
        grad1[one_out(z)] = total.astype(BF16)
        for d in range(1, NZ):
            z_copy(grad1.at[one_out(z)], grad1.at[one_out(z)], 1, d, z).start()

    def one_s5():
        for d in range(1, NZ):
            other = lax.rem(z + d, NZ)
            got = z_copy(grad1.at[one_out(z)], grad1.at[one_out(other)], 1, d, other)
            got.wait_recv()
            got.wait_send()
        one[5]()

    def two_s3():
        a, b = two[3]()
        rz2[z, 0:2] = a
        rz2[z, 2:4] = b
        for d in range(1, NZ):
            z_copy(rz2.at[z], rz2.at[z], 2, d, z).start()

    def two_s5():
        for d in range(1, NZ):
            other = lax.rem(z + d, NZ)
            got = z_copy(rz2.at[z], rz2.at[other], 2, d, other)
            got.wait_recv()
            got.wait_send()
        total = rz2[0].astype(F32)
        for k in range(1, NZ):
            total = total + rz2[k].astype(F32)
        total = total.astype(BF16)
        two[4](total[0:2], total[2:4])
        two[5]()

    def gain_copies(buf, count, mine, dev, send_sem, recv_sem, wait):
        for d in range(1, count):
            other = lax.rem(mine + d, count)
            c = pltpu.make_async_remote_copy(
                src_ref=buf.at[mine],
                dst_ref=buf.at[other] if wait else buf.at[mine],
                send_sem=send_sem(d),
                recv_sem=recv_sem(other) if wait else recv_sem(mine),
                device_id=dev(other),
                device_id_type=MESH,
            )
            if wait:
                c.wait_recv()
                c.wait_send()
            else:
                c.start()

    def add_slots(buf, count):
        total = buf[0]
        for k in range(1, count):
            total = total + buf[k]
        return total

    gain_steps = (
        (gcore, NC, core, lambda o: core_dev(), lambda d: gcore_sems.at[0], lambda o: gcore_sems.at[1]),
        (gx, NX, x, x_dev, lambda d: gfour_send.at[0, d], lambda o: gfour_recv.at[0, o]),
        (gy, NY, y, y_dev, lambda d: gfour_send.at[1, d], lambda o: gfour_recv.at[1, o]),
        (gz, NZ, z, z_dev, lambda d: gz_send.at[d], lambda o: gz_recv.at[o]),
    )

    def gain_start(step, values):
        buf, count, mine, dev, ssem, rsem = gain_steps[step]
        buf[mine] = values
        gain_copies(buf, count, mine, dev, ssem, rsem, False)

    def gain_wait(step):
        buf, count, mine, dev, ssem, rsem = gain_steps[step]
        gain_copies(buf, count, mine, dev, ssem, rsem, True)
        return add_slots(buf, count)

    one[0]()

    gg_cols[...] = jnp.zeros_like(gg_cols)

    def back_norm_two(i):
        at = tile_at(i, TILE)
        grad = nn(wup_ref[...], gb_t[:, at])
        normed = n2_t[:, at]
        gg_cols[:, 1:2] += jnp.sum(grad * normed, axis=1, keepdims=True)
        back = norm_back_rows(grad * gain_two, normed, inv_rows[1:2, at])
        mixed = (g_t[:, at].astype(F32) + back).astype(BF16)
        gm_t[:, at] = mixed
        kept = jnp.where(live_tile(at, TILE), mixed.astype(F32), 0.0).astype(BF16)
        gbr_t[:, at] = kept
        ga_t[:, at] = nn(wproj_ref[...], kept).astype(BF16)

    loop(0, tiles, back_norm_two)
    for l, u in enumerate(tiles_of(nt(att_t[...], gbr_t[...]), 2)):
        grad2[96 + l * 16 : 112 + l * 16] = u

    one[1]()

    def back_attend(b):
        at = tile_at(b, BLK)
        for h in range(HEADS):
            q = heads_of(proj_t, at, 0, h)
            k = heads_of(proj_t, at, 1, h)
            v = heads_of(proj_t, at, 2, h)
            ga = heads_of(ga_t, at, 0, h)
            weights = w_t[b * HEADS + h]
            wide = spread_windows(weights.astype(BF16), diagonal)
            grad_v = nt(ga, wide)
            grad_w = pack_windows(tn(v, ga), window_of_lane)
            inner = jnp.sum(weights * grad_w, axis=0, keepdims=True)
            grad_s = (weights * (grad_w - inner) * SCALE).astype(BF16)
            wide_s = spread_windows(grad_s, diagonal)
            gproj_t[h * HD : (h + 1) * HD, at] = nn(k, wide_s).astype(BF16)
            gproj_t[CH + h * HD : CH + (h + 1) * HD, at] = nt(q, wide_s).astype(BF16)
            gproj_t[2 * CH + h * HD : 2 * CH + (h + 1) * HD, at] = grad_v.astype(BF16)

        pl.when(b == 1)(one[2])
        pl.when(b == 3)(one_s3)
        pl.when(b == 5)(one_s4)
        pl.when(b == 7)(one_s5)

    loop(0, ROWS // BLK, back_attend)

    def qkv_part(p):
        rows = tile_at(p, TILE)
        for l, u in enumerate(tiles_of(nt(h1_t[...], gproj_t[rows, :]), 2)):
            grad2[pl.ds(p * 32 + l * 16, 16)] = u

    loop(0, 3, qkv_part)
    two[0]()
    one[6]()

    def back_norm_one(i):
        at = tile_at(i, TILE)
        grad = nn(wqkv_ref[...], gproj_t[:, at])
        normed = n1_t[:, at]
        gg_cols[:, 0:1] += jnp.sum(grad * normed, axis=1, keepdims=True)
        back = norm_back_rows(grad * gain_one, normed, inv_rows[0:1, at])
        dx_t[:, at] = (gm_t[:, at].astype(F32) + back).astype(BF16)

    loop(0, tiles, back_norm_one)
    two[1]()
    gain_start(0, jnp.transpose(gg_cols[...]))

    def give_back(i):
        pick = select_rows((i * TILE).astype(F32), TILE, rank_rows[1:2, :])
        sendr[tile_at(i, TILE // SHARE)] = to_units(nt(pick, dx_t[...]))

    loop(0, tiles, give_back)
    a2a_start(sendr, recvr, 4)

    one[7]()
    two[2]()
    gain_start(1, gain_wait(0))
    two_s3()
    gain_start(2, gain_wait(1))
    two_s5()
    gain_start(3, gain_wait(2))
    one[8]()

    def split_units(first, lanes, out, grad):
        for l in range(lanes):
            block = grad[first + l * 16 : first + (l + 1) * 16].reshape(256, 128)
            out[:, l * 128 : (l + 1) * 128] = block.astype(F32) * grad_scale

    split_units(0, 8, oup_ref, grad1)

    def down_rows(f):
        rows = tile_at(f, TILE)
        for l in range(2):
            block = grad1[pl.ds(128 + f * 32 + l * 16, 16)].reshape(256, 128)
            odown_ref[rows, l * 128 : (l + 1) * 128] = block.astype(F32) * grad_scale

    loop(0, 4, down_rows)
    two[6]()
    ogain_ref[...] = gain_wait(3) * grad_scale
    two[7]()
    two[8]()
    split_units(0, 6, oqkv_ref, grad2)
    split_units(96, 2, oproj_ref, grad2)

    a2a_wait_recv(recvr, 4)
    left, right = from_units(recvr[...])
    r_t2 = jnp.concatenate([left, right], axis=1).astype(BF16)

    def home(i):
        rows = tile_at(i, TILE)
        slot = lax.broadcasted_iota(jnp.int32, (TILE, ROWS), 1).astype(F32)
        pick = jnp.where(rank_cols[rows, 0:1] == slot, 1.0, 0.0).astype(BF16)
        dx_ref[rows, :] = nn(pick, r_t2).astype(BF16)

    loop(0, tiles, home)
    a2a_wait_send(sendx, 0)
    a2a_wait_send(sendg, 2)
    a2a_wait_send(sendr, 4)


def units(n):
    return pltpu.VMEM((n, 16, 128), BF16)


def shards(
    features,
    cotangent,
    morton_target,
    morton_source,
    counts,
    w_qkv,
    w_proj,
    w_up,
    w_down,
    gain_one,
    gain_two,
):
    n_pts = lax.axis_size("pts")
    grad_scale = 1.0 / math.sqrt(features.shape[0] * n_pts * lax.axis_size("quad"))
    source = morton_source.reshape(ROWS // BLK, WINDOW, DILATION).transpose(0, 2, 1).reshape(ROWS)
    count_row = jnp.repeat(counts, WINDOW)
    table = jnp.concatenate(
        [jnp.stack([morton_target, source, count_row]), jnp.zeros((5, ROWS), jnp.int32)]
    )
    gains = jnp.concatenate([jnp.stack([gain_one, gain_two]), jnp.zeros((6, CH), F32)])
    rows = lambda n, kind: pltpu.VMEM((n, ROWS), kind)
    sem = pltpu.SemaphoreType.DMA
    out = pl.pallas_call(
        functools.partial(kernel, n_pts, grad_scale),
        out_shape=(
            jax.ShapeDtypeStruct((ROWS, CH), BF16),
            jax.ShapeDtypeStruct((CH, 3 * CH), F32),
            jax.ShapeDtypeStruct((CH, CH), F32),
            jax.ShapeDtypeStruct((CH, FFN), F32),
            jax.ShapeDtypeStruct((FFN, CH), F32),
            jax.ShapeDtypeStruct((8, CH), F32),
        ),
        in_specs=[pl.BlockSpec(memory_space=pltpu.VMEM)] * 8,
        out_specs=[pl.BlockSpec(memory_space=pltpu.VMEM)] * 6,
        scratch_shapes=[units(n_pts)] * 6
        + [
            rows(8, F32),
            pltpu.VMEM((ROWS, 8), F32),
            pltpu.VMEM((CH, 8), F32),
            pltpu.VMEM((3 * CH, CH), BF16),
            pltpu.VMEM((CH, CH), BF16),
            pltpu.VMEM((FFN, CH), BF16),
            rows(CH, BF16),
            rows(CH, BF16),
            rows(CH, F32),
            rows(CH, BF16),
            rows(8, F32),
            rows(3 * CH, BF16),
            pltpu.VMEM((ROWS // BLK * HEADS, WINDOW, BLK), F32),
            rows(CH, BF16),
            rows(CH, F32),
            rows(CH, BF16),
            rows(FFN, BF16),
            rows(FFN, F32),
            rows(CH, BF16),
            rows(FFN, BF16),
            rows(CH, BF16),
            rows(CH, BF16),
            rows(CH, BF16),
            rows(3 * CH, BF16),
            rows(CH, BF16),
            pltpu.VMEM((CH, 8), F32),
            units(256),
            units(128),
            units(128),
            pltpu.VMEM((4, 16, 16, 128), BF16),
            pltpu.VMEM((4, 16, 16, 128), BF16),
            units(32),
            pltpu.VMEM((4, 4, 16, 128), BF16),
            pltpu.VMEM((4, 4, 16, 128), BF16),
            units(8),
            units(8),
            units(128),
            units(64),
            units(64),
            pltpu.VMEM((4, 8, 16, 128), BF16),
            pltpu.VMEM((4, 8, 16, 128), BF16),
            units(16),
            pltpu.VMEM((4, 2, 16, 128), BF16),
            pltpu.VMEM((4, 2, 16, 128), BF16),
            pltpu.VMEM((8, 4, 16, 128), BF16),
            pltpu.VMEM((2, 8, CH), F32),
            pltpu.VMEM((4, 8, CH), F32),
            pltpu.VMEM((4, 8, CH), F32),
            pltpu.VMEM((8, 8, CH), F32),
            sem((6,)),
            sem((8,)),
            sem((16, 4)),
            sem((16, 4)),
            sem((3, 8)),
            sem((3, 8)),
            sem((2,)),
            sem((2, 4)),
            sem((2, 4)),
            sem((8,)),
            sem((8,)),
        ],
        compiler_params=pltpu.CompilerParams(
            collective_id=0, has_side_effects=True, vmem_limit_bytes=56 * 1024 * 1024
        ),
    )(features, cotangent, table, gains, w_qkv, w_proj, w_up, w_down)
    dx, grad_qkv, grad_proj, grad_up, grad_down, gain_grads = out
    return dx, grad_qkv, grad_proj, grad_up, grad_down, gain_grads[0], gain_grads[1]


def solution(mesh):
    placed = (
        P(("pts", "quad"), None),
        P(("pts", "quad"), None),
        P(("pts", "quad")),
        P(("pts", "quad")),
        P(("pts", "quad")),
        P(),
        P(),
        P(),
        P(),
        P(),
        P(),
    )
    return jax.shard_map(
        shards,
        mesh=mesh,
        in_specs=placed,
        out_specs=(P(("pts", "quad"), None), P(), P(), P(), P(), P(), P()),
        check_vma=False,
    )
```

```python
import functools
import math

import jax
import jax.numpy as jnp
from jax import lax
from jax.experimental import pallas as pl
from jax.experimental.pallas import tpu as pltpu
from jax.sharding import PartitionSpec as P

HEADS = 8
WINDOW = 32
DILATION = 4
ROWS = 1024
CH = 256
FFN = 1024
HD = 32
BLK = 128
TILE = 256
SHARE = 8
NEG_FILL = -1e30
SCALE = 1.0 / math.sqrt(HD)

F32 = jnp.float32
BF16 = jnp.bfloat16
MESH = pl.DeviceIdType.MESH

NY, NZ, NX, NC = 4, 8, 4, 2


def nn(a, b):
    return lax.dot_general(a, b, (((1,), (0,)), ((), ())), preferred_element_type=F32)


def nt(a, b):
    return lax.dot_general(a, b, (((1,), (1,)), ((), ())), preferred_element_type=F32)


def tn(a, b):
    return lax.dot_general(a, b, (((0,), (0,)), ((), ())), preferred_element_type=F32)


def loop(start, stop, body):
    def step(i, carry):
        body(i)
        return carry

    lax.fori_loop(start, stop, step, 0)


def transposed(a):
    return jnp.transpose(a.astype(F32)).astype(a.dtype)


def tile_at(i, size):
    return pl.ds(pl.multiple_of(i * size, size), size)


def norm_rows(values):
    mean = jnp.mean(values, axis=0, keepdims=True)
    centred = values - mean
    inverse = lax.rsqrt(jnp.mean(centred * centred, axis=0, keepdims=True) + 1e-05)
    return centred * inverse, inverse


def norm_back_rows(grad, normed, inverse):
    first = jnp.mean(grad, axis=0, keepdims=True)
    second = jnp.mean(grad * normed, axis=0, keepdims=True)
    return inverse * (grad - first - normed * second)


def pack_windows(dense, window_of_lane):
    packed = dense[3 * WINDOW :]
    for k in (2, 1, 0):
        packed = jnp.where(window_of_lane == k, dense[k * WINDOW : (k + 1) * WINDOW], packed)
    return packed


def spread_windows(packed, diagonal):
    return jnp.concatenate([packed] * DILATION, axis=0) * diagonal


def to_units(y):
    n = y.shape[0] // SHARE
    left = y[:, :128].reshape(n, SHARE, 128)
    right = y[:, 128:].reshape(n, SHARE, 128)
    return jnp.concatenate([left, right], axis=1).astype(BF16)


def from_units(u):
    r = u.astype(F32)
    n = r.shape[0]
    left = r[:, :SHARE, :].reshape(n * SHARE, 128)
    right = r[:, SHARE:, :].reshape(n * SHARE, 128)
    return left, right


def head_columns(t):
    blocks = []
    for h in range(HEADS):
        own = t[h * HD : (h + 1) * HD]
        pieces = [own]
        if h > 0:
            pieces.insert(0, jnp.zeros((h * HD, BLK), t.dtype))
        if h < HEADS - 1:
            pieces.append(jnp.zeros(((HEADS - 1 - h) * HD, BLK), t.dtype))
        blocks.append(jnp.concatenate(pieces, axis=0))
    return jnp.concatenate(blocks, axis=1)


def head_rows(r):
    head = lax.broadcasted_iota(jnp.int32, (1, CH), 1) // HD
    return jnp.concatenate(
        [r * jnp.where(head == h, 1.0, 0.0).astype(r.dtype) for h in range(HEADS)], axis=0
    )


def flip(a):
    return jnp.transpose(a.astype(F32)).astype(BF16)


def kernel(
    n_pts,
    target_ref,
    source_ref,
    counts_ref,
    gain_one_ref,
    gain_two_ref,
    x_hbm,
    g_hbm,
    wqkv_hbm,
    wproj_hbm,
    wup_hbm,
    wdown_hbm,
    out1_ref,
    out2_ref,
    outr_ref,
    ranks_ref,
    ogain_ref,
    x_ref,
    g_ref,
    wqkv_ref,
    wproj_ref,
    wup_ref,
    wdown_ref,
    sendx,
    recvx,
    sendg,
    recvg,
    sendr,
    recvr,
    rank_rows,
    rank_cols,
    count_rows,
    gain_cols,
    wqkv_t,
    wproj_t,
    wup_t,
    x_t,
    n1_t,
    h1_t,
    h1_r,
    inv_rows,
    proj_t,
    proj_r,
    w_t,
    att_t,
    n2_t,
    h2_t,
    h2_r,
    act_t,
    dg_t,
    g_t,
    g_r,
    gb_t,
    gm_t,
    gbr_r,
    ga_t,
    ga_r,
    gq_t,
    gkv_r,
    dx_r,
    gg_cols,
    grad1,
    core1,
    cur1,
    ra1,
    rb1,
    mid1,
    rc1,
    rd1,
    zin1,
    rz1,
    grad2,
    core2,
    cur2,
    ra2,
    rb2,
    mid2,
    rc2,
    rd2,
    rz2,
    gcore,
    gx,
    gy,
    gz,
    gsum,
    a2a_sems,
    core_sems,
    four_send,
    four_recv,
    z_send,
    z_recv,
    gcore_sems,
    gfour_send,
    gfour_recv,
    gz_send,
    gz_recv,
    load_sems,
    store_sems,
):
    me = lax.axis_index("pts")
    quad = lax.axis_index("quad")
    core = lax.rem(me, NC)
    x_hi = lax.rem(me // NC, 2)
    z = lax.rem(me // (2 * NC), NZ)
    y = me // (2 * NC * NZ)
    x = x_hi * 2 + quad

    def core_dev():
        return {"pts": me + 1 - 2 * core, "quad": quad}

    def x_dev(other):
        return {"pts": me + (other // 2 - x_hi) * NC, "quad": lax.rem(other, 2)}

    def y_dev(other):
        return {"pts": me + (other - y) * (2 * NC * NZ), "quad": quad}

    def z_dev(other):
        return {"pts": me + (other - z) * (2 * NC), "quad": quad}

    loads = [
        pltpu.make_async_copy(src, dst, load_sems.at[k])
        for k, (src, dst) in enumerate(
            (
                (x_hbm, x_ref),
                (g_hbm, g_ref),
                (wqkv_hbm, wqkv_ref),
                (wproj_hbm, wproj_ref),
                (wup_hbm, wup_ref),
                (wdown_hbm, wdown_ref),
            )
        )
    ]
    for load in loads:
        load.start()

    barrier = pltpu.get_barrier_semaphore()

    def greet(k):
        pl.semaphore_signal(
            barrier, inc=1, device_id={"pts": lax.rem(me + k, n_pts), "quad": quad}, device_id_type=MESH
        )

    loop(1, n_pts, greet)
    for hi in range(2):
        pl.semaphore_signal(
            barrier,
            inc=1,
            device_id={"pts": me + (hi - x_hi) * NC, "quad": 1 - quad},
            device_id_type=MESH,
        )

    def one_row(a):
        return jnp.concatenate([a[r : r + 1, :] for r in range(8)], axis=1)

    stored = lax.broadcasted_iota(jnp.int32, (8, 128), 0) * 128 + lax.broadcasted_iota(
        jnp.int32, (8, 128), 1
    )
    target_key = one_row(((target_ref[...] >> 11) * ROWS + stored).astype(F32))
    to_lane = lax.broadcasted_iota(jnp.int32, (BLK, BLK), 1)
    from_lane = lax.broadcasted_iota(jnp.int32, (BLK, BLK), 0)
    moved = jnp.where(
        from_lane == lax.rem(to_lane, WINDOW) * DILATION + to_lane // WINDOW, 1.0, 0.0
    ).astype(BF16)
    src = source_ref[...]
    digits = jnp.concatenate([src & 63, (src >> 6) & 63, src >> 12], axis=0)
    digits = nn(digits.astype(F32).astype(BF16), moved)
    source_key = one_row(digits[0:8] + 64.0 * digits[8:16] + 4096.0 * digits[16:24])
    spread = jnp.where(
        lax.broadcasted_iota(jnp.int32, (WINDOW, ROWS), 1) // WINDOW
        == lax.broadcasted_iota(jnp.int32, (WINDOW, ROWS), 0),
        1.0,
        0.0,
    ).astype(BF16)
    wide_counts = jnp.broadcast_to(counts_ref[...].astype(F32), (8, WINDOW)).astype(BF16)
    count_rows[...] = nn(wide_counts, spread)
    pad = jnp.zeros((6, ROWS), F32)
    rank_rows[...] = jnp.concatenate([target_key, source_key, pad], axis=0)
    rank_cols[...] = jnp.transpose(rank_rows[...])

    keys = rank_rows[...]

    def count(i, carry):
        t, s = carry
        cols = rank_cols[tile_at(i, 64), :]
        t = t + jnp.sum(jnp.where(cols[:, 0:1] < keys[0:1, :], 1.0, 0.0), axis=0, keepdims=True)
        s = s + jnp.sum(jnp.where(cols[:, 1:2] < keys[1:2, :], 1.0, 0.0), axis=0, keepdims=True)
        return t, s

    zero_row = jnp.zeros((1, ROWS), F32)
    rank_target, rank_source = lax.fori_loop(0, ROWS // 64, count, (zero_row, zero_row))
    rank_rows[...] = jnp.concatenate([rank_target, rank_source, pad], axis=0)
    rank_cols[...] = jnp.transpose(rank_rows[...])

    def select_rows(first, size, ranks):
        slot = lax.broadcasted_iota(jnp.int32, (size, ranks.shape[1]), 0).astype(F32)
        return jnp.where(slot + first == ranks, 1.0, 0.0).astype(BF16)

    def place(i, source_ref, out):
        pick = select_rows((i * TILE).astype(F32), TILE, rank_rows[0:1, :])
        out[tile_at(i, TILE // SHARE)] = to_units(nn(pick, source_ref[...]))

    def a2a(send, recv, index, k):
        peer = lax.rem(me + k, n_pts)
        return pltpu.make_async_remote_copy(
            src_ref=send.at[peer],
            dst_ref=recv.at[me],
            send_sem=a2a_sems.at[index],
            recv_sem=a2a_sems.at[index + 1],
            device_id={"pts": peer, "quad": quad},
            device_id_type=MESH,
        )

    def a2a_start(send, recv, index):
        pltpu.make_async_copy(send.at[me], recv.at[me], a2a_sems.at[index + 1]).start()
        loop(1, n_pts, lambda j: a2a(send, recv, index, 1 + lax.rem((j - 1) * 37 , n_pts - 1)).start())

    def a2a_wait_recv(recv, index):
        pltpu.make_async_copy(recv, recv, a2a_sems.at[index + 1]).wait()

    def a2a_wait_send(send, index):
        part = send.at[pl.ds(0, n_pts - 1)]
        pltpu.make_async_copy(part, part, a2a_sems.at[index]).wait()

    keep_ranks = pltpu.make_async_copy(rank_rows, ranks_ref, store_sems.at[3])
    keep_ranks.start()
    tiles = ROWS // TILE
    loads[0].wait()
    loop(0, tiles, lambda i: place(i, x_ref, sendx))
    pl.semaphore_wait(barrier, n_pts + 1)
    a2a_start(sendx, recvx, 0)
    loads[1].wait()
    loop(0, tiles, lambda i: place(i, g_ref, sendg))
    a2a_start(sendg, recvg, 2)

    for load in loads[2:]:
        load.wait()
    wqkv_t[...] = transposed(wqkv_ref[...])
    wproj_t[...] = transposed(wproj_ref[...])
    wup_t[...] = transposed(wup_ref[...])
    gain_cols[...] = jnp.transpose(
        jnp.concatenate([gain_one_ref[...], gain_two_ref[...], jnp.zeros((6, CH), F32)], axis=0)
    )
    gain_one = gain_cols[:, 0:1]
    gain_two = gain_cols[:, 1:2]

    span = HEADS * BLK
    sub = lax.broadcasted_iota(jnp.int32, (WINDOW, span), 0).astype(F32)
    window_of_lane = lax.rem(lax.broadcasted_iota(jnp.int32, (WINDOW, span), 1), BLK) // WINDOW
    diagonal = jnp.where(
        lax.broadcasted_iota(jnp.int32, (BLK, span), 0) // WINDOW
        == lax.rem(lax.broadcasted_iota(jnp.int32, (BLK, span), 1), BLK) // WINDOW,
        1.0,
        0.0,
    ).astype(BF16)

    def live_tile(at, size):
        slot = lax.rem(lax.broadcasted_iota(jnp.int32, (1, size), 1), WINDOW).astype(F32)
        return slot < count_rows[0:1, at]

    def arrive(recv, out, out_rows):
        left, right = from_units(recv[...])
        arrived = jnp.concatenate([left, right], axis=1).astype(BF16)

        def one(i):
            at = tile_at(i, TILE)
            slot = lax.broadcasted_iota(jnp.int32, (TILE, ROWS), 1).astype(F32)
            pick = jnp.where(rank_cols[at, 1:2] == slot, 1.0, 0.0).astype(BF16)
            points = nn(pick, arrived)
            out[:, at] = jnp.transpose(points).astype(BF16)
            if out_rows is not None:
                out_rows[at, :] = points.astype(BF16)

        loop(0, tiles, one)

    a2a_wait_recv(recvx, 0)
    arrive(recvx, x_t, None)

    def first_norm(i):
        at = tile_at(i, TILE)
        normed, inverse = norm_rows(x_t[:, at].astype(F32))
        n1_t[:, at] = normed
        inv_rows[0:1, at] = inverse
        scaled = normed * gain_one
        hidden = scaled.astype(BF16)
        hidden_rows = jnp.transpose(scaled).astype(BF16)
        h1_t[:, at] = hidden
        h1_r[at, :] = hidden_rows
        proj_t[:, at] = nn(wqkv_t[...], hidden).astype(BF16)
        proj_r[at, :] = nn(hidden_rows, wqkv_ref[...]).astype(BF16)

    loop(0, tiles, first_norm)

    def attend(b):
        at = tile_at(b, BLK)
        counted = jnp.concatenate([count_rows[0:1, at]] * HEADS, axis=1)
        dense = nn(proj_r[at, CH : 2 * CH], head_columns(proj_t[0:CH, at]))
        scores = pack_windows(dense, window_of_lane) * SCALE
        scores = jnp.where(sub < counted, scores, NEG_FILL)
        powered = jnp.exp(scores - jnp.max(scores, axis=0, keepdims=True))
        weights = powered / jnp.sum(powered, axis=0, keepdims=True)
        w_t[b] = weights
        wide = spread_windows(weights.astype(BF16), diagonal)
        for h in range(HEADS):
            v = proj_t[2 * CH + h * HD : 2 * CH + (h + 1) * HD, at]
            att_t[h * HD : (h + 1) * HD, at] = nn(v, wide[:, h * BLK : (h + 1) * BLK]).astype(BF16)

    loop(0, ROWS // BLK, attend)

    def forward_mlp(i):
        at = tile_at(i, TILE)
        branch = nn(wproj_t[...], att_t[:, at])
        mixed = x_t[:, at].astype(F32) + jnp.where(live_tile(at, TILE), branch, 0.0)
        normed, inverse = norm_rows(mixed.astype(BF16).astype(F32))
        n2_t[:, at] = normed
        inv_rows[1:2, at] = inverse
        scaled = normed * gain_two
        hidden = scaled.astype(BF16)
        h2_t[:, at] = hidden
        h2_r[at, :] = jnp.transpose(scaled).astype(BF16)
        for f in range(FFN // TILE):
            rows = pl.ds(f * TILE, TILE)
            before = nn(wup_t[rows, :], hidden)
            cumulative = 0.5 * (1.0 + lax.erf(before * 0.7071067811865476))
            act_t[rows, at] = (before * cumulative).astype(BF16)
            density = jnp.exp(-0.5 * before * before) * 0.3989422804014327
            dg_t[rows, at] = cumulative + before * density

    loop(0, tiles, forward_mlp)

    a2a_wait_recv(recvg, 2)
    arrive(recvg, g_t, g_r)

    def back_act(i):
        at = tile_at(i, TILE)
        for f in range(FFN // TILE):
            rows = pl.ds(f * TILE, TILE)
            gb_t[rows, at] = (nn(wdown_ref[rows, :], g_t[:, at]) * dg_t[rows, at]).astype(BF16)

    loop(0, tiles, back_act)

    def tiles_of(y, lanes):
        return [y[:, l * 128 : (l + 1) * 128].reshape(16, 16, 128).astype(BF16) for l in range(lanes)]

    def up_down(f):
        rows = tile_at(f, TILE)
        for l, u in enumerate(tiles_of(nn(act_t[rows, :], g_r[...]), 2)):
            grad1[pl.ds(128 + f * 32 + l * 16, 16)] = u
        for l, u in enumerate(tiles_of(nn(gb_t[rows, :], h2_r[...]), 2)):
            grad1[pl.ds(f * 32 + l * 16, 16)] = u

    loop(0, FFN // TILE, up_down)

    def four_copies(src, dst_of, which, mine, dev, sem_base):
        copies = []
        for d in range(1, 4):
            other = lax.rem(mine + d, 4)
            copies.append(
                pltpu.make_async_remote_copy(
                    src_ref=src(other),
                    dst_ref=dst_of,
                    send_sem=four_send.at[sem_base + which, d],
                    recv_sem=four_recv.at[sem_base + which, mine],
                    device_id=dev(other),
                    device_id_type=MESH,
                )
            )
        return copies

    def four_wait(src, dst, which, mine, dev, sem_base):
        for d in range(1, 4):
            other = lax.rem(mine + d, 4)
            got = pltpu.make_async_remote_copy(
                src_ref=src(other),
                dst_ref=dst(other),
                send_sem=four_send.at[sem_base + which, d],
                recv_sem=four_recv.at[sem_base + which, other],
                device_id=dev(other),
                device_id_type=MESH,
            )
            got.wait_recv()
            got.wait_send()

    def group(index, grad, from_core, cur, ra, rb, mid, rc, rd, nk):
        half = nk * 32
        part = half // 2
        quarter = part // 4
        base = index * 4
        cbase = index * 4

        def core_copy(src, dst, sem):
            return pltpu.make_async_remote_copy(
                src_ref=src,
                dst_ref=dst,
                send_sem=core_sems.at[cbase + sem],
                recv_sem=core_sems.at[cbase + sem + 1],
                device_id=core_dev(),
                device_id_type=MESH,
            )

        def first_core():
            return core_copy(grad.at[pl.ds((1 - core) * half, half)], from_core, 0)

        def s0():
            first_core().start()

        def cur_a(o):
            return cur.at[pl.ds(o * quarter, quarter)]

        def cur_b(o):
            return cur.at[pl.ds(part + o * quarter, quarter)]

        def s1():
            first_core().wait()
            total = grad[pl.ds(core * half, half)].astype(F32) + from_core[...].astype(F32)
            cur[...] = total.astype(BF16)
            for c in four_copies(cur_a, ra.at[x], 0, x, x_dev, base):
                c.start()
            for c in four_copies(cur_b, rb.at[y], 1, y, y_dev, base):
                c.start()

        def mid_a(o):
            return mid.at[pl.ds(o * nk, nk)]

        def mid_b(o):
            return mid.at[pl.ds(quarter + o * nk, nk)]

        def add_four(own, slots, mine):
            total = own.astype(F32)
            for d in range(1, 4):
                total = total + slots[lax.rem(mine + d, 4)].astype(F32)
            return total.astype(BF16)

        def s2():
            four_wait(cur_a, lambda o: ra.at[o], 0, x, x_dev, base)
            four_wait(cur_b, lambda o: rb.at[o], 1, y, y_dev, base)
            mid[pl.ds(0, quarter)] = add_four(cur[pl.ds(x * quarter, quarter)], ra, x)
            mid[pl.ds(quarter, quarter)] = add_four(cur[pl.ds(part + y * quarter, quarter)], rb, y)
            for c in four_copies(mid_a, rc.at[y], 2, y, y_dev, base):
                c.start()
            for c in four_copies(mid_b, rd.at[x], 3, x, x_dev, base):
                c.start()

        def s3():
            four_wait(mid_a, lambda o: rc.at[o], 2, y, y_dev, base)
            four_wait(mid_b, lambda o: rd.at[o], 3, x, x_dev, base)
            a = add_four(mid[pl.ds(y * nk, nk)], rc, y)
            b = add_four(mid[pl.ds(quarter + x * nk, nk)], rd, x)
            return a, b

        mine = core * half

        def out_a(xx, yy):
            return grad.at[pl.ds(mine + xx * quarter + yy * nk, nk)]

        def out_b(xx, yy):
            return grad.at[pl.ds(mine + part + yy * quarter + xx * nk, nk)]

        def whole_a(xx):
            return grad.at[pl.ds(mine + xx * quarter, quarter)]

        def whole_b(yy):
            return grad.at[pl.ds(mine + part + yy * quarter, quarter)]

        gbase = 8 + index * 4

        def s5():
            for c in four_copies(lambda o: out_a(x, y), out_a(x, y), 0, y, y_dev, gbase):
                c.start()
            for c in four_copies(lambda o: out_b(x, y), out_b(x, y), 1, x, x_dev, gbase):
                c.start()

        def s6():
            four_wait(lambda o: out_a(x, y), lambda o: out_a(x, o), 0, y, y_dev, gbase)
            four_wait(lambda o: out_b(x, y), lambda o: out_b(o, y), 1, x, x_dev, gbase)
            for c in four_copies(lambda o: whole_a(x), whole_a(x), 2, x, x_dev, gbase):
                c.start()
            for c in four_copies(lambda o: whole_b(y), whole_b(y), 3, y, y_dev, gbase):
                c.start()

        def last_core():
            at = grad.at[pl.ds(mine, half)]
            return core_copy(at, at, 2)

        def s7():
            four_wait(lambda o: whole_a(x), lambda o: whole_a(o), 2, x, x_dev, gbase)
            four_wait(lambda o: whole_b(y), lambda o: whole_b(o), 3, y, y_dev, gbase)
            last_core().start()

        def s8():
            last_core().wait()

        def put(a, b):
            grad[pl.ds(mine + x * quarter + y * nk, nk)] = a
            grad[pl.ds(mine + part + y * quarter + x * nk, nk)] = b

        return s0, s1, s2, s3, put, s5, s6, s7, s8

    def z_copy(src, dst, sems, d, slot):
        other = lax.rem(z + d, NZ)
        return pltpu.make_async_remote_copy(
            src_ref=src,
            dst_ref=dst,
            send_sem=z_send.at[sems, d],
            recv_sem=z_recv.at[sems, slot],
            device_id=z_dev(other),
            device_id_type=MESH,
        )

    one = group(0, grad1, core1, cur1, ra1, rb1, mid1, rc1, rd1, 4)
    two = group(1, grad2, core2, cur2, ra2, rb2, mid2, rc2, rd2, 2)

    def one_s3():
        a, b = one[3]()
        zin1[0:4] = a
        zin1[4:8] = b
        for d in range(1, NZ):
            z_copy(zin1.at[lax.rem(z + d, NZ)], rz1.at[z], 0, d, z).start()

    def one_out(zz):
        p = zz // 4
        k = lax.rem(zz, 4)
        first = x + p * (y - x)
        second = y + p * (x - y)
        return core * 128 + p * 64 + first * 16 + second * 4 + k

    def one_s4():
        total = zin1[z].astype(F32)
        for d in range(1, NZ):
            other = lax.rem(z + d, NZ)
            got = z_copy(zin1.at[other], rz1.at[other], 0, d, other)
            got.wait_recv()
            got.wait_send()
            total = total + rz1[other].astype(F32)
        grad1[one_out(z)] = total.astype(BF16)
        for d in range(1, NZ):
            z_copy(grad1.at[one_out(z)], grad1.at[one_out(z)], 1, d, z).start()

    def one_s5():
        for d in range(1, NZ):
            other = lax.rem(z + d, NZ)
            got = z_copy(grad1.at[one_out(z)], grad1.at[one_out(other)], 1, d, other)
            got.wait_recv()
            got.wait_send()
        one[5]()

    def two_s3():
        a, b = two[3]()
        rz2[z, 0:2] = a
        rz2[z, 2:4] = b
        for d in range(1, NZ):
            z_copy(rz2.at[z], rz2.at[z], 2, d, z).start()

    def two_s5():
        for d in range(1, NZ):
            other = lax.rem(z + d, NZ)
            got = z_copy(rz2.at[z], rz2.at[other], 2, d, other)
            got.wait_recv()
            got.wait_send()
        total = rz2[0].astype(F32)
        for k in range(1, NZ):
            total = total + rz2[k].astype(F32)
        total = total.astype(BF16)
        two[4](total[0:2], total[2:4])
        two[5]()

    def gain_copies(buf, count, mine, dev, send_sem, recv_sem, wait):
        for d in range(1, count):
            other = lax.rem(mine + d, count)
            c = pltpu.make_async_remote_copy(
                src_ref=buf.at[mine],
                dst_ref=buf.at[other] if wait else buf.at[mine],
                send_sem=send_sem(d),
                recv_sem=recv_sem(other) if wait else recv_sem(mine),
                device_id=dev(other),
                device_id_type=MESH,
            )
            if wait:
                c.wait_recv()
                c.wait_send()
            else:
                c.start()

    def add_slots(buf, count):
        total = buf[0]
        for k in range(1, count):
            total = total + buf[k]
        return total

    gain_steps = (
        (gcore, NC, core, lambda o: core_dev(), lambda d: gcore_sems.at[0], lambda o: gcore_sems.at[1]),
        (gx, NX, x, x_dev, lambda d: gfour_send.at[0, d], lambda o: gfour_recv.at[0, o]),
        (gy, NY, y, y_dev, lambda d: gfour_send.at[1, d], lambda o: gfour_recv.at[1, o]),
        (gz, NZ, z, z_dev, lambda d: gz_send.at[d], lambda o: gz_recv.at[o]),
    )

    def gain_start(step, values):
        buf, count, mine, dev, ssem, rsem = gain_steps[step]
        buf[mine] = values
        gain_copies(buf, count, mine, dev, ssem, rsem, False)

    def gain_wait(step):
        buf, count, mine, dev, ssem, rsem = gain_steps[step]
        gain_copies(buf, count, mine, dev, ssem, rsem, True)
        return add_slots(buf, count)

    one[0]()

    gg_cols[...] = jnp.zeros_like(gg_cols)

    def back_norm_two(i):
        at = tile_at(i, TILE)
        grad = nn(wup_ref[...], gb_t[:, at])
        normed = n2_t[:, at]
        gg_cols[:, 1:2] += jnp.sum(grad * normed, axis=1, keepdims=True)
        back = norm_back_rows(grad * gain_two, normed, inv_rows[1:2, at])
        mixed = (g_t[:, at].astype(F32) + back).astype(BF16)
        gm_t[:, at] = mixed
        kept = jnp.where(live_tile(at, TILE), mixed.astype(F32), 0.0)
        kept_rows = jnp.transpose(kept).astype(BF16)
        gbr_r[at, :] = kept_rows
        ga_t[:, at] = nn(wproj_ref[...], kept.astype(BF16)).astype(BF16)
        ga_r[at, :] = nn(kept_rows, wproj_t[...]).astype(BF16)

    loop(0, tiles, back_norm_two)
    for l, u in enumerate(tiles_of(nn(att_t[...], gbr_r[...]), 2)):
        grad2[96 + l * 16 : 112 + l * 16] = u

    one[1]()

    def back_attend(b):
        at = tile_at(b, BLK)
        weights = w_t[b]
        wide = spread_windows(weights.astype(BF16), diagonal)
        gkv_r[at, CH : 2 * CH] = nn(wide, head_rows(ga_r[at, :])).astype(BF16)
        dense = nn(proj_r[at, 2 * CH : 3 * CH], head_columns(ga_t[:, at]))
        grad_w = pack_windows(dense, window_of_lane)
        inner = jnp.sum(weights * grad_w, axis=0, keepdims=True)
        grad_s = (weights * (grad_w - inner) * SCALE).astype(BF16)
        wide_s = spread_windows(grad_s, diagonal)
        gkv_r[at, 0:CH] = nn(wide_s, head_rows(proj_r[at, 0:CH])).astype(BF16)
        for h in range(HEADS):
            k = proj_t[CH + h * HD : CH + (h + 1) * HD, at]
            gq_t[h * HD : (h + 1) * HD, at] = nn(k, wide_s[:, h * BLK : (h + 1) * BLK]).astype(BF16)

        pl.when(b == 1)(one[2])
        pl.when(b == 3)(one_s3)
        pl.when(b == 5)(one_s4)
        pl.when(b == 7)(one_s5)

    loop(0, ROWS // BLK, back_attend)

    for l, u in enumerate(tiles_of(nn(gq_t[...], h1_r[...]), 2)):
        grad2[l * 16 : (l + 1) * 16] = u
    for p in range(2):
        for l, u in enumerate(tiles_of(nn(h1_t[...], gkv_r[:, p * CH : (p + 1) * CH]), 2)):
            grad2[(p + 1) * 32 + l * 16 : (p + 1) * 32 + (l + 1) * 16] = u
    two[0]()
    one[6]()

    def back_norm_one(i):
        at = tile_at(i, TILE)
        grad = nn(wqkv_ref[:, 0:CH], gq_t[:, at]) + jnp.transpose(
            nn(gkv_r[at, :], wqkv_t[CH : 3 * CH, :])
        )
        normed = n1_t[:, at]
        gg_cols[:, 0:1] += jnp.sum(grad * normed, axis=1, keepdims=True)
        back = norm_back_rows(grad * gain_one, normed, inv_rows[0:1, at])
        dx_r[at, :] = jnp.transpose(gm_t[:, at].astype(F32) + back).astype(BF16)

    loop(0, tiles, back_norm_one)
    two[1]()
    gain_start(0, jnp.transpose(gg_cols[...]))

    def give_back(i):
        pick = select_rows((i * TILE).astype(F32), TILE, rank_rows[1:2, :])
        sendr[tile_at(i, TILE // SHARE)] = to_units(nn(pick, dx_r[...]))

    loop(0, tiles, give_back)
    a2a_start(sendr, recvr, 4)

    one[7]()
    two[2]()
    gain_start(1, gain_wait(0))
    two_s3()
    gain_start(2, gain_wait(1))
    two_s5()
    gain_start(3, gain_wait(2))
    one[8]()

    stores = [
        pltpu.make_async_copy(src, dst, store_sems.at[k])
        for k, (src, dst) in enumerate(
            ((grad1, out1_ref), (grad2, out2_ref), (recvr, outr_ref))
        )
    ]
    stores[0].start()
    two[6]()
    gsum[...] = gain_wait(3)
    keep_gains = pltpu.make_async_copy(gsum, ogain_ref, store_sems.at[4])
    keep_gains.start()
    two[7]()
    two[8]()
    stores[1].start()
    a2a_wait_recv(recvr, 4)
    stores[2].start()
    a2a_wait_send(sendx, 0)
    a2a_wait_send(sendg, 2)
    a2a_wait_send(sendr, 4)
    for store in stores:
        store.wait()
    keep_ranks.wait()
    keep_gains.wait()


def finish(
    grad_scale,
    u1_ref,
    u2_ref,
    ur_ref,
    ranks_ref,
    gains_ref,
    dx_hbm,
    qkv_hbm,
    proj_hbm,
    up_hbm,
    down_hbm,
    gain_one_ref,
    gain_two_ref,
    dx_ref,
    oqkv_ref,
    oproj_ref,
    oup_ref,
    odown_ref,
    sems,
):
    stores = [
        pltpu.make_async_copy(src, dst, sems.at[k])
        for k, (src, dst) in enumerate(
            (
                (oup_ref, up_hbm),
                (odown_ref, down_hbm),
                (oqkv_ref, qkv_hbm),
                (oproj_ref, proj_hbm),
                (dx_ref, dx_hbm),
            )
        )
    ]

    def block(ref, first):
        left = ref[first : first + 16].reshape(TILE, 128).astype(F32)
        right = ref[first + 16 : first + 32].reshape(TILE, 128).astype(F32)
        return jnp.concatenate([left, right], axis=1) * grad_scale

    for f in range(FFN // TILE):
        at = slice(f * TILE, (f + 1) * TILE)
        oup_ref[:, at] = jnp.transpose(block(u1_ref, f * 32))
    stores[0].start()
    for f in range(FFN // TILE):
        odown_ref[f * TILE : (f + 1) * TILE, :] = block(u1_ref, 128 + f * 32)
    stores[1].start()
    oqkv_ref[:, 0:CH] = jnp.transpose(block(u2_ref, 0))
    oqkv_ref[:, CH : 2 * CH] = block(u2_ref, 32)
    oqkv_ref[:, 2 * CH : 3 * CH] = block(u2_ref, 64)
    stores[2].start()
    oproj_ref[...] = block(u2_ref, 96)
    stores[3].start()
    gain_one_ref[...] = gains_ref[0:1, :] * grad_scale
    gain_two_ref[...] = gains_ref[1:2, :] * grad_scale
    left, right = from_units(ur_ref[...])
    arrived = jnp.concatenate([left, right], axis=1).astype(BF16)
    ranks = jnp.transpose(ranks_ref[...])
    for i in range(ROWS // TILE):
        slot = lax.broadcasted_iota(jnp.int32, (TILE, ROWS), 1).astype(F32)
        pick = jnp.where(ranks[i * TILE : (i + 1) * TILE, 0:1] == slot, 1.0, 0.0).astype(BF16)
        dx_ref[i * TILE : (i + 1) * TILE, :] = nn(pick, arrived).astype(BF16)
    stores[4].start()
    for store in stores:
        store.wait()


def units(n):
    return pltpu.VMEM((n, 16, 128), BF16)


def shards(
    features,
    cotangent,
    morton_target,
    morton_source,
    counts,
    w_qkv,
    w_proj,
    w_up,
    w_down,
    gain_one,
    gain_two,
):
    n_pts = lax.axis_size("pts")
    grad_scale = 1.0 / math.sqrt(features.shape[0] * n_pts * lax.axis_size("quad"))
    rows = lambda n, kind: pltpu.VMEM((n, ROWS), kind)
    wide = lambda n: pltpu.VMEM((ROWS, n), BF16)
    sem = pltpu.SemaphoreType.DMA
    vmem = pl.BlockSpec(memory_space=pltpu.VMEM)
    anywhere = pl.BlockSpec(memory_space=pl.ANY)
    parts = pl.pallas_call(
        functools.partial(kernel, n_pts),
        out_shape=(
            jax.ShapeDtypeStruct((256, 16, 128), BF16),
            jax.ShapeDtypeStruct((128, 16, 128), BF16),
            jax.ShapeDtypeStruct((n_pts, 16, 128), BF16),
            jax.ShapeDtypeStruct((8, ROWS), F32),
            jax.ShapeDtypeStruct((8, CH), F32),
        ),
        in_specs=[vmem] * 5 + [anywhere] * 6,
        out_specs=[anywhere] * 5,
        scratch_shapes=[
            wide(CH),
            wide(CH),
            pltpu.VMEM((CH, 3 * CH), BF16),
            pltpu.VMEM((CH, CH), BF16),
            pltpu.VMEM((CH, FFN), BF16),
            pltpu.VMEM((FFN, CH), BF16),
        ]
        + [units(n_pts)] * 6
        + [
            rows(8, F32),
            pltpu.VMEM((ROWS, 8), F32),
            rows(8, F32),
            pltpu.VMEM((CH, 8), F32),
            pltpu.VMEM((3 * CH, CH), BF16),
            pltpu.VMEM((CH, CH), BF16),
            pltpu.VMEM((FFN, CH), BF16),
            rows(CH, BF16),
            rows(CH, F32),
            rows(CH, BF16),
            wide(CH),
            rows(8, F32),
            rows(3 * CH, BF16),
            wide(3 * CH),
            pltpu.VMEM((ROWS // BLK, WINDOW, HEADS * BLK), F32),
            rows(CH, BF16),
            rows(CH, F32),
            rows(CH, BF16),
            wide(CH),
            rows(FFN, BF16),
            rows(FFN, F32),
            rows(CH, BF16),
            wide(CH),
            rows(FFN, BF16),
            rows(CH, BF16),
            wide(CH),
            rows(CH, BF16),
            wide(CH),
            rows(CH, BF16),
            wide(2 * CH),
            wide(CH),
            pltpu.VMEM((CH, 8), F32),
            units(256),
            units(128),
            units(128),
            pltpu.VMEM((4, 16, 16, 128), BF16),
            pltpu.VMEM((4, 16, 16, 128), BF16),
            units(32),
            pltpu.VMEM((4, 4, 16, 128), BF16),
            pltpu.VMEM((4, 4, 16, 128), BF16),
            units(8),
            units(8),
            units(128),
            units(64),
            units(64),
            pltpu.VMEM((4, 8, 16, 128), BF16),
            pltpu.VMEM((4, 8, 16, 128), BF16),
            units(16),
            pltpu.VMEM((4, 2, 16, 128), BF16),
            pltpu.VMEM((4, 2, 16, 128), BF16),
            pltpu.VMEM((8, 4, 16, 128), BF16),
            pltpu.VMEM((2, 8, CH), F32),
            pltpu.VMEM((4, 8, CH), F32),
            pltpu.VMEM((4, 8, CH), F32),
            pltpu.VMEM((8, 8, CH), F32),
            pltpu.VMEM((8, CH), F32),
            sem((6,)),
            sem((8,)),
            sem((16, 4)),
            sem((16, 4)),
            sem((3, 8)),
            sem((3, 8)),
            sem((2,)),
            sem((2, 4)),
            sem((2, 4)),
            sem((8,)),
            sem((8,)),
            sem((6,)),
            sem((5,)),
        ],
        compiler_params=pltpu.CompilerParams(
            collective_id=0, has_side_effects=True, vmem_limit_bytes=44 * 1024 * 1024
        ),
    )(
        morton_target.reshape(8, 128),
        morton_source.reshape(8, 128),
        counts.reshape(1, WINDOW),
        gain_one.reshape(1, CH),
        gain_two.reshape(1, CH),
        features,
        cotangent,
        w_qkv,
        w_proj,
        w_up,
        w_down,
    )
    shapes = (
        ((ROWS, CH), BF16),
        ((CH, 3 * CH), F32),
        ((CH, CH), F32),
        ((CH, FFN), F32),
        ((FFN, CH), F32),
    )
    out = pl.pallas_call(
        functools.partial(finish, grad_scale),
        out_shape=tuple(jax.ShapeDtypeStruct(*shape) for shape in shapes)
        + (jax.ShapeDtypeStruct((1, CH), F32),) * 2,
        in_specs=[vmem] * 5,
        out_specs=[anywhere] * 5 + [vmem] * 2,
        scratch_shapes=[pltpu.VMEM(*shape) for shape in shapes] + [sem((5,))],
        compiler_params=pltpu.CompilerParams(vmem_limit_bytes=24 * 1024 * 1024),
    )(*parts)
    dx, grad_qkv, grad_proj, grad_up, grad_down, gain_one_grad, gain_two_grad = out
    return (
        dx,
        grad_qkv,
        grad_proj,
        grad_up,
        grad_down,
        gain_one_grad.reshape(CH),
        gain_two_grad.reshape(CH),
    )


def solution(mesh):
    placed = (
        P(("pts", "quad"), None),
        P(("pts", "quad"), None),
        P(("pts", "quad")),
        P(("pts", "quad")),
        P(("pts", "quad")),
        P(),
        P(),
        P(),
        P(),
        P(),
        P(),
    )
    return jax.shard_map(
        shards,
        mesh=mesh,
        in_specs=placed,
        out_specs=(P(("pts", "quad"), None), P(), P(), P(), P(), P(), P()),
        check_vma=False,
    )
```

```python
import functools
import math

import jax
import jax.numpy as jnp
from jax import lax
from jax.experimental import pallas as pl
from jax.experimental.pallas import tpu as pltpu
from jax.sharding import PartitionSpec as P

HEADS = 8
WINDOW = 32
DILATION = 4
ROWS = 1024
CH = 256
FFN = 1024
HD = 32
BLK = 128
TILE = 256
SHARE = 8
NEG_FILL = -1e30
SCALE = 1.0 / math.sqrt(HD)

F32 = jnp.float32
BF16 = jnp.bfloat16
MESH = pl.DeviceIdType.MESH

NY, NZ, NX, NC = 4, 8, 4, 2


def nn(a, b):
    return lax.dot_general(a, b, (((1,), (0,)), ((), ())), preferred_element_type=F32)


def nt(a, b):
    return lax.dot_general(a, b, (((1,), (1,)), ((), ())), preferred_element_type=F32)


def tn(a, b):
    return lax.dot_general(a, b, (((0,), (0,)), ((), ())), preferred_element_type=F32)


def loop(start, stop, body, unroll=1):
    def step(i, carry):
        for k in range(unroll):
            body(i * unroll + k)
        return carry

    lax.fori_loop(start // unroll, stop // unroll, step, 0)


def transposed(a):
    return jnp.transpose(a.astype(F32)).astype(a.dtype)


def tile_at(i, size):
    return pl.ds(pl.multiple_of(i * size, size), size)


def norm_rows(values):
    mean = jnp.mean(values, axis=0, keepdims=True)
    centred = values - mean
    inverse = lax.rsqrt(jnp.mean(centred * centred, axis=0, keepdims=True) + 1e-05)
    return centred * inverse, inverse


def norm_back_rows(grad, normed, inverse):
    first = jnp.mean(grad, axis=0, keepdims=True)
    second = jnp.mean(grad * normed, axis=0, keepdims=True)
    return inverse * (grad - first - normed * second)


def pack_windows(dense, window_of_lane):
    packed = dense[3 * WINDOW :]
    for k in (2, 1, 0):
        packed = jnp.where(window_of_lane == k, dense[k * WINDOW : (k + 1) * WINDOW], packed)
    return packed


def spread_windows(packed, diagonal):
    return jnp.concatenate([packed] * DILATION, axis=0) * diagonal


def to_units(y):
    n = y.shape[0] // SHARE
    left = y[:, :128].reshape(n, SHARE, 128)
    right = y[:, 128:].reshape(n, SHARE, 128)
    return jnp.concatenate([left, right], axis=1).astype(BF16)


def from_units(u):
    r = u.astype(F32)
    n = r.shape[0]
    left = r[:, :SHARE, :].reshape(n * SHARE, 128)
    right = r[:, SHARE:, :].reshape(n * SHARE, 128)
    return left, right


def head_columns(t):
    blocks = []
    for h in range(HEADS):
        own = t[h * HD : (h + 1) * HD]
        pieces = [own]
        if h > 0:
            pieces.insert(0, jnp.zeros((h * HD, BLK), t.dtype))
        if h < HEADS - 1:
            pieces.append(jnp.zeros(((HEADS - 1 - h) * HD, BLK), t.dtype))
        blocks.append(jnp.concatenate(pieces, axis=0))
    return jnp.concatenate(blocks, axis=1)


def head_rows(r):
    head = lax.broadcasted_iota(jnp.int32, (1, CH), 1) // HD
    return jnp.concatenate(
        [r * jnp.where(head == h, 1.0, 0.0).astype(r.dtype) for h in range(HEADS)], axis=0
    )


def flip(a):
    return jnp.transpose(a.astype(F32)).astype(BF16)


def kernel(
    n_pts,
    target_hbm,
    source_hbm,
    counts_hbm,
    gain_one_hbm,
    gain_two_hbm,
    x_hbm,
    g_hbm,
    wqkv_hbm,
    wproj_hbm,
    wup_hbm,
    wdown_hbm,
    out1_ref,
    out2_ref,
    outr_ref,
    ranks_ref,
    ogain_ref,
    target_ref,
    source_ref,
    counts_ref,
    gain_one_ref,
    gain_two_ref,
    x_ref,
    g_ref,
    wqkv_ref,
    wproj_ref,
    wup_ref,
    wdown_ref,
    sendx,
    recvx,
    sendg,
    recvg,
    sendr,
    rank_rows,
    rank_cols,
    count_rows,
    gain_cols,
    wqkv_t,
    wproj_t,
    wup_t,
    x_t,
    n1_t,
    h1_t,
    h1_r,
    inv_rows,
    proj_t,
    proj_r,
    w_t,
    att_t,
    n2_t,
    h2_t,
    h2_r,
    act_t,
    dg_t,
    g_t,
    g_r,
    gb_t,
    gm_t,
    gbr_r,
    ga_t,
    ga_r,
    gq_t,
    gkv_r,
    dx_r,
    gg_cols,
    grad1,
    core1,
    cur1,
    ra1,
    rb1,
    mid1,
    rc1,
    rd1,
    zin1,
    rz1,
    grad2,
    core2,
    cur2,
    ra2,
    rb2,
    mid2,
    rc2,
    rd2,
    rz2,
    gcore,
    gx,
    gy,
    gz,
    gsum,
    a2a_sems,
    core_sems,
    four_send,
    four_recv,
    z_send,
    z_recv,
    gcore_sems,
    gfour_send,
    gfour_recv,
    gz_send,
    gz_recv,
    load_sems,
    store_sems,
):
    me = lax.axis_index("pts")
    quad = lax.axis_index("quad")
    core = lax.rem(me, NC)
    x_hi = lax.rem(me // NC, 2)
    z = lax.rem(me // (2 * NC), NZ)
    y = me // (2 * NC * NZ)
    x = x_hi * 2 + quad

    def core_dev():
        return {"pts": me + 1 - 2 * core, "quad": quad}

    def x_dev(other):
        return {"pts": me + (other // 2 - x_hi) * NC, "quad": lax.rem(other, 2)}

    def y_dev(other):
        return {"pts": me + (other - y) * (2 * NC * NZ), "quad": quad}

    def z_dev(other):
        return {"pts": me + (other - z) * (2 * NC), "quad": quad}

    loads = [
        pltpu.make_async_copy(src, dst, load_sems.at[k])
        for k, (src, dst) in enumerate(
            (
                (target_hbm, target_ref),
                (source_hbm, source_ref),
                (counts_hbm, counts_ref),
                (gain_one_hbm, gain_one_ref),
                (gain_two_hbm, gain_two_ref),
                (x_hbm, x_ref),
                (g_hbm, g_ref),
                (wqkv_hbm, wqkv_ref),
                (wproj_hbm, wproj_ref),
                (wup_hbm, wup_ref),
                (wdown_hbm, wdown_ref),
            )
        )
    ]
    for load in loads:
        load.start()

    barrier = pltpu.get_barrier_semaphore()

    def greet(k):
        pl.semaphore_signal(
            barrier, inc=1, device_id={"pts": lax.rem(me + k, n_pts), "quad": quad}, device_id_type=MESH
        )

    loop(1, n_pts, greet)
    for hi in range(2):
        pl.semaphore_signal(
            barrier,
            inc=1,
            device_id={"pts": me + (hi - x_hi) * NC, "quad": 1 - quad},
            device_id_type=MESH,
        )

    for load in loads[:5]:
        load.wait()

    def one_row(a):
        return jnp.concatenate([a[r : r + 1, :] for r in range(8)], axis=1)

    stored = lax.broadcasted_iota(jnp.int32, (8, 128), 0) * 128 + lax.broadcasted_iota(
        jnp.int32, (8, 128), 1
    )
    target_key = one_row(((target_ref[...] >> 11) * ROWS + stored).astype(F32))
    to_lane = lax.broadcasted_iota(jnp.int32, (BLK, BLK), 1)
    from_lane = lax.broadcasted_iota(jnp.int32, (BLK, BLK), 0)
    moved = jnp.where(
        from_lane == lax.rem(to_lane, WINDOW) * DILATION + to_lane // WINDOW, 1.0, 0.0
    ).astype(BF16)
    src = source_ref[...]
    digits = jnp.concatenate([src & 63, (src >> 6) & 63, src >> 12], axis=0)
    digits = nn(digits.astype(F32).astype(BF16), moved)
    source_key = one_row(digits[0:8] + 64.0 * digits[8:16] + 4096.0 * digits[16:24])
    spread = jnp.where(
        lax.broadcasted_iota(jnp.int32, (WINDOW, ROWS), 1) // WINDOW
        == lax.broadcasted_iota(jnp.int32, (WINDOW, ROWS), 0),
        1.0,
        0.0,
    ).astype(BF16)
    wide_counts = jnp.broadcast_to(counts_ref[...].astype(F32), (8, WINDOW)).astype(BF16)
    count_rows[...] = nn(wide_counts, spread)
    pad = jnp.zeros((6, ROWS), F32)
    rank_rows[...] = jnp.concatenate([target_key, source_key, pad], axis=0)
    rank_cols[...] = jnp.transpose(rank_rows[...])

    keys = rank_rows[...]

    def count(i, carry):
        t, s = carry
        cols = rank_cols[tile_at(i, 64), :]
        t = t + jnp.sum(jnp.where(cols[:, 0:1] < keys[0:1, :], 1.0, 0.0), axis=0, keepdims=True)
        s = s + jnp.sum(jnp.where(cols[:, 1:2] < keys[1:2, :], 1.0, 0.0), axis=0, keepdims=True)
        return t, s

    zero_row = jnp.zeros((1, ROWS), F32)
    rank_target, rank_source = lax.fori_loop(0, ROWS // 64, count, (zero_row, zero_row))
    rank_rows[...] = jnp.concatenate([rank_target, rank_source, pad], axis=0)
    rank_cols[...] = jnp.transpose(rank_rows[...])

    def select_rows(first, size, ranks):
        slot = lax.broadcasted_iota(jnp.int32, (size, ranks.shape[1]), 0).astype(F32)
        return jnp.where(slot + first == ranks, 1.0, 0.0).astype(BF16)

    def place(i, source_ref, out):
        pick = select_rows((i * TILE).astype(F32), TILE, rank_rows[0:1, :])
        out[tile_at(i, TILE // SHARE)] = to_units(nn(pick, source_ref[...]))

    def a2a(send, recv, index, k):
        peer = lax.rem(me + k, n_pts)
        return pltpu.make_async_remote_copy(
            src_ref=send.at[peer],
            dst_ref=recv.at[me],
            send_sem=a2a_sems.at[index],
            recv_sem=a2a_sems.at[index + 1],
            device_id={"pts": peer, "quad": quad},
            device_id_type=MESH,
        )

    def a2a_some(send, recv, index, first, stop):
        loop(first, stop, lambda j: a2a(send, recv, index, 1 + lax.rem((j - 1) * 37, n_pts - 1)).start())

    def a2a_own(send, recv, index):
        pltpu.make_async_copy(send.at[me], recv.at[me], a2a_sems.at[index + 1]).start()

    def a2a_start(send, recv, index):
        a2a_own(send, recv, index)
        a2a_some(send, recv, index, 1, n_pts)

    def a2a_wait_recv(recv, index):
        pltpu.make_async_copy(recv, recv, a2a_sems.at[index + 1]).wait()

    def a2a_wait_send(send, index):
        part = send.at[pl.ds(0, n_pts - 1)]
        pltpu.make_async_copy(part, part, a2a_sems.at[index]).wait()

    keep_ranks = pltpu.make_async_copy(rank_rows, ranks_ref, store_sems.at[2])
    keep_ranks.start()
    tiles = ROWS // TILE
    loads[5].wait()
    loop(0, tiles, lambda i: place(i, x_ref, sendx))
    pl.semaphore_wait(barrier, n_pts + 1)
    a2a_start(sendx, recvx, 0)
    loads[6].wait()
    loop(0, tiles, lambda i: place(i, g_ref, sendg))
    a2a_start(sendg, recvg, 2)

    for load in loads[7:]:
        load.wait()
    wqkv_t[...] = transposed(wqkv_ref[...])
    wproj_t[...] = transposed(wproj_ref[...])
    wup_t[...] = transposed(wup_ref[...])
    gain_cols[...] = jnp.transpose(
        jnp.concatenate([gain_one_ref[...], gain_two_ref[...], jnp.zeros((6, CH), F32)], axis=0)
    )
    gain_one = gain_cols[:, 0:1]
    gain_two = gain_cols[:, 1:2]

    span = HEADS * BLK
    sub = lax.broadcasted_iota(jnp.int32, (WINDOW, span), 0).astype(F32)
    window_of_lane = lax.rem(lax.broadcasted_iota(jnp.int32, (WINDOW, span), 1), BLK) // WINDOW
    diagonal = jnp.where(
        lax.broadcasted_iota(jnp.int32, (BLK, span), 0) // WINDOW
        == lax.rem(lax.broadcasted_iota(jnp.int32, (BLK, span), 1), BLK) // WINDOW,
        1.0,
        0.0,
    ).astype(BF16)

    def live_tile(at, size):
        slot = lax.rem(lax.broadcasted_iota(jnp.int32, (1, size), 1), WINDOW).astype(F32)
        return slot < count_rows[0:1, at]

    def arrive(recv, out, out_rows):
        left, right = from_units(recv[...])
        arrived = jnp.concatenate([left, right], axis=1).astype(BF16)

        def one(i):
            at = tile_at(i, TILE)
            slot = lax.broadcasted_iota(jnp.int32, (TILE, ROWS), 1).astype(F32)
            pick = jnp.where(rank_cols[at, 1:2] == slot, 1.0, 0.0).astype(BF16)
            points = nn(pick, arrived)
            out[:, at] = jnp.transpose(points).astype(BF16)
            if out_rows is not None:
                out_rows[at, :] = points.astype(BF16)

        loop(0, tiles, one, 4)

    a2a_wait_recv(recvx, 0)
    arrive(recvx, x_t, None)

    def first_norm(i):
        at = tile_at(i, TILE)
        normed, inverse = norm_rows(x_t[:, at].astype(F32))
        n1_t[:, at] = normed
        inv_rows[0:1, at] = inverse
        scaled = normed * gain_one
        hidden = scaled.astype(BF16)
        hidden_rows = jnp.transpose(scaled).astype(BF16)
        h1_t[:, at] = hidden
        h1_r[at, :] = hidden_rows
        proj_t[:, at] = nn(wqkv_t[...], hidden).astype(BF16)
        proj_r[at, :] = nn(hidden_rows, wqkv_ref[...]).astype(BF16)

    loop(0, tiles, first_norm, 4)

    def attend(b):
        at = tile_at(b, BLK)
        counted = jnp.concatenate([count_rows[0:1, at]] * HEADS, axis=1)
        dense = nn(proj_r[at, CH : 2 * CH], head_columns(proj_t[0:CH, at]))
        scores = pack_windows(dense, window_of_lane) * SCALE
        scores = jnp.where(sub < counted, scores, NEG_FILL)
        powered = jnp.exp(scores - jnp.max(scores, axis=0, keepdims=True))
        weights = powered / jnp.sum(powered, axis=0, keepdims=True)
        w_t[b] = weights
        wide = spread_windows(weights.astype(BF16), diagonal)
        for h in range(HEADS):
            v = proj_t[2 * CH + h * HD : 2 * CH + (h + 1) * HD, at]
            att_t[h * HD : (h + 1) * HD, at] = nn(v, wide[:, h * BLK : (h + 1) * BLK]).astype(BF16)

    loop(0, ROWS // BLK, attend, 8)

    def forward_mlp(i):
        at = tile_at(i, TILE)
        branch = nn(wproj_t[...], att_t[:, at])
        mixed = x_t[:, at].astype(F32) + jnp.where(live_tile(at, TILE), branch, 0.0)
        normed, inverse = norm_rows(mixed.astype(BF16).astype(F32))
        n2_t[:, at] = normed
        inv_rows[1:2, at] = inverse
        scaled = normed * gain_two
        hidden = scaled.astype(BF16)
        h2_t[:, at] = hidden
        h2_r[at, :] = jnp.transpose(scaled).astype(BF16)
        for f in range(FFN // TILE):
            rows = pl.ds(f * TILE, TILE)
            before = nn(wup_t[rows, :], hidden)
            cumulative = 0.5 * (1.0 + lax.erf(before * 0.7071067811865476))
            act_t[rows, at] = (before * cumulative).astype(BF16)
            density = jnp.exp(-0.5 * before * before) * 0.3989422804014327
            dg_t[rows, at] = cumulative + before * density

    loop(0, tiles, forward_mlp)

    a2a_wait_recv(recvg, 2)
    arrive(recvg, g_t, g_r)

    def back_act(i):
        at = tile_at(i, TILE)
        for f in range(FFN // TILE):
            rows = pl.ds(f * TILE, TILE)
            gb_t[rows, at] = (nn(wdown_ref[rows, :], g_t[:, at]) * dg_t[rows, at]).astype(BF16)

    loop(0, tiles, back_act, 4)

    def tiles_of(y, lanes):
        return [y[:, l * 128 : (l + 1) * 128].reshape(16, 16, 128).astype(BF16) for l in range(lanes)]

    def up_down(f):
        rows = tile_at(f, TILE)
        for l, u in enumerate(tiles_of(nn(act_t[rows, :], g_r[...]), 2)):
            grad1[pl.ds(128 + f * 32 + l * 16, 16)] = u
        for l, u in enumerate(tiles_of(nn(gb_t[rows, :], h2_r[...]), 2)):
            grad1[pl.ds(f * 32 + l * 16, 16)] = u

    loop(0, FFN // TILE, up_down, 4)

    def four_copies(src, dst_of, which, mine, dev, sem_base):
        copies = []
        for d in range(1, 4):
            other = lax.rem(mine + d, 4)
            copies.append(
                pltpu.make_async_remote_copy(
                    src_ref=src(other),
                    dst_ref=dst_of,
                    send_sem=four_send.at[sem_base + which, d],
                    recv_sem=four_recv.at[sem_base + which, mine],
                    device_id=dev(other),
                    device_id_type=MESH,
                )
            )
        return copies

    def four_wait(src, dst, which, mine, dev, sem_base):
        for d in range(1, 4):
            other = lax.rem(mine + d, 4)
            got = pltpu.make_async_remote_copy(
                src_ref=src(other),
                dst_ref=dst(other),
                send_sem=four_send.at[sem_base + which, d],
                recv_sem=four_recv.at[sem_base + which, other],
                device_id=dev(other),
                device_id_type=MESH,
            )
            got.wait_recv()
            got.wait_send()

    def group(index, grad, from_core, cur, ra, rb, mid, rc, rd, nk):
        half = nk * 32
        part = half // 2
        quarter = part // 4
        base = index * 4
        cbase = index * 4

        def core_copy(src, dst, sem):
            return pltpu.make_async_remote_copy(
                src_ref=src,
                dst_ref=dst,
                send_sem=core_sems.at[cbase + sem],
                recv_sem=core_sems.at[cbase + sem + 1],
                device_id=core_dev(),
                device_id_type=MESH,
            )

        def first_core():
            return core_copy(grad.at[pl.ds((1 - core) * half, half)], from_core, 0)

        def s0():
            first_core().start()

        def cur_a(o):
            return cur.at[pl.ds(o * quarter, quarter)]

        def cur_b(o):
            return cur.at[pl.ds(part + o * quarter, quarter)]

        def s1():
            first_core().wait()
            total = grad[pl.ds(core * half, half)].astype(F32) + from_core[...].astype(F32)
            cur[...] = total.astype(BF16)
            for c in four_copies(cur_a, ra.at[x], 0, x, x_dev, base):
                c.start()
            for c in four_copies(cur_b, rb.at[y], 1, y, y_dev, base):
                c.start()

        def mid_a(o):
            return mid.at[pl.ds(o * nk, nk)]

        def mid_b(o):
            return mid.at[pl.ds(quarter + o * nk, nk)]

        def add_four(own, slots, mine):
            total = own.astype(F32)
            for d in range(1, 4):
                total = total + slots[lax.rem(mine + d, 4)].astype(F32)
            return total.astype(BF16)

        def s2():
            four_wait(cur_a, lambda o: ra.at[o], 0, x, x_dev, base)
            four_wait(cur_b, lambda o: rb.at[o], 1, y, y_dev, base)
            mid[pl.ds(0, quarter)] = add_four(cur[pl.ds(x * quarter, quarter)], ra, x)
            mid[pl.ds(quarter, quarter)] = add_four(cur[pl.ds(part + y * quarter, quarter)], rb, y)
            for c in four_copies(mid_a, rc.at[y], 2, y, y_dev, base):
                c.start()
            for c in four_copies(mid_b, rd.at[x], 3, x, x_dev, base):
                c.start()

        def s3():
            four_wait(mid_a, lambda o: rc.at[o], 2, y, y_dev, base)
            four_wait(mid_b, lambda o: rd.at[o], 3, x, x_dev, base)
            a = add_four(mid[pl.ds(y * nk, nk)], rc, y)
            b = add_four(mid[pl.ds(quarter + x * nk, nk)], rd, x)
            return a, b

        mine = core * half

        def out_a(xx, yy):
            return grad.at[pl.ds(mine + xx * quarter + yy * nk, nk)]

        def out_b(xx, yy):
            return grad.at[pl.ds(mine + part + yy * quarter + xx * nk, nk)]

        def whole_a(xx):
            return grad.at[pl.ds(mine + xx * quarter, quarter)]

        def whole_b(yy):
            return grad.at[pl.ds(mine + part + yy * quarter, quarter)]

        gbase = 8 + index * 4

        def s5():
            for c in four_copies(lambda o: out_a(x, y), out_a(x, y), 0, y, y_dev, gbase):
                c.start()
            for c in four_copies(lambda o: out_b(x, y), out_b(x, y), 1, x, x_dev, gbase):
                c.start()

        def s6():
            four_wait(lambda o: out_a(x, y), lambda o: out_a(x, o), 0, y, y_dev, gbase)
            four_wait(lambda o: out_b(x, y), lambda o: out_b(o, y), 1, x, x_dev, gbase)
            for c in four_copies(lambda o: whole_a(x), whole_a(x), 2, x, x_dev, gbase):
                c.start()
            for c in four_copies(lambda o: whole_b(y), whole_b(y), 3, y, y_dev, gbase):
                c.start()

        def last_core():
            at = grad.at[pl.ds(mine, half)]
            return core_copy(at, at, 2)

        def s7():
            four_wait(lambda o: whole_a(x), lambda o: whole_a(o), 2, x, x_dev, gbase)
            four_wait(lambda o: whole_b(y), lambda o: whole_b(o), 3, y, y_dev, gbase)
            last_core().start()

        def s8():
            last_core().wait()

        def put(a, b):
            grad[pl.ds(mine + x * quarter + y * nk, nk)] = a
            grad[pl.ds(mine + part + y * quarter + x * nk, nk)] = b

        return s0, s1, s2, s3, put, s5, s6, s7, s8

    def z_copy(src, dst, sems, d, slot):
        other = lax.rem(z + d, NZ)
        return pltpu.make_async_remote_copy(
            src_ref=src,
            dst_ref=dst,
            send_sem=z_send.at[sems, d],
            recv_sem=z_recv.at[sems, slot],
            device_id=z_dev(other),
            device_id_type=MESH,
        )

    one = group(0, grad1, core1, cur1, ra1, rb1, mid1, rc1, rd1, 4)
    two = group(1, grad2, core2, cur2, ra2, rb2, mid2, rc2, rd2, 2)

    def one_s3():
        a, b = one[3]()
        zin1[0:4] = a
        zin1[4:8] = b
        for d in range(1, NZ):
            z_copy(zin1.at[lax.rem(z + d, NZ)], rz1.at[z], 0, d, z).start()

    def one_out(zz):
        p = zz // 4
        k = lax.rem(zz, 4)
        first = x + p * (y - x)
        second = y + p * (x - y)
        return core * 128 + p * 64 + first * 16 + second * 4 + k

    def one_s4():
        total = zin1[z].astype(F32)
        for d in range(1, NZ):
            other = lax.rem(z + d, NZ)
            got = z_copy(zin1.at[other], rz1.at[other], 0, d, other)
            got.wait_recv()
            got.wait_send()
            total = total + rz1[other].astype(F32)
        grad1[one_out(z)] = total.astype(BF16)
        for d in range(1, NZ):
            z_copy(grad1.at[one_out(z)], grad1.at[one_out(z)], 1, d, z).start()

    def one_s5():
        for d in range(1, NZ):
            other = lax.rem(z + d, NZ)
            got = z_copy(grad1.at[one_out(z)], grad1.at[one_out(other)], 1, d, other)
            got.wait_recv()
            got.wait_send()
        one[5]()

    def two_s3():
        a, b = two[3]()
        rz2[z, 0:2] = a
        rz2[z, 2:4] = b
        for d in range(1, NZ):
            z_copy(rz2.at[z], rz2.at[z], 2, d, z).start()

    def two_s5():
        for d in range(1, NZ):
            other = lax.rem(z + d, NZ)
            got = z_copy(rz2.at[z], rz2.at[other], 2, d, other)
            got.wait_recv()
            got.wait_send()
        total = rz2[0].astype(F32)
        for k in range(1, NZ):
            total = total + rz2[k].astype(F32)
        total = total.astype(BF16)
        two[4](total[0:2], total[2:4])
        two[5]()

    def gain_copies(buf, count, mine, dev, send_sem, recv_sem, wait):
        for d in range(1, count):
            other = lax.rem(mine + d, count)
            c = pltpu.make_async_remote_copy(
                src_ref=buf.at[mine],
                dst_ref=buf.at[other] if wait else buf.at[mine],
                send_sem=send_sem(d),
                recv_sem=recv_sem(other) if wait else recv_sem(mine),
                device_id=dev(other),
                device_id_type=MESH,
            )
            if wait:
                c.wait_recv()
                c.wait_send()
            else:
                c.start()

    def add_slots(buf, count):
        total = buf[0]
        for k in range(1, count):
            total = total + buf[k]
        return total

    gain_steps = (
        (gcore, NC, core, lambda o: core_dev(), lambda d: gcore_sems.at[0], lambda o: gcore_sems.at[1]),
        (gx, NX, x, x_dev, lambda d: gfour_send.at[0, d], lambda o: gfour_recv.at[0, o]),
        (gy, NY, y, y_dev, lambda d: gfour_send.at[1, d], lambda o: gfour_recv.at[1, o]),
        (gz, NZ, z, z_dev, lambda d: gz_send.at[d], lambda o: gz_recv.at[o]),
    )

    def gain_start(step, values):
        buf, count, mine, dev, ssem, rsem = gain_steps[step]
        buf[mine] = values
        gain_copies(buf, count, mine, dev, ssem, rsem, False)

    def gain_wait(step):
        buf, count, mine, dev, ssem, rsem = gain_steps[step]
        gain_copies(buf, count, mine, dev, ssem, rsem, True)
        return add_slots(buf, count)

    one[0]()

    gg_cols[...] = jnp.zeros_like(gg_cols)

    def back_norm_two(i):
        at = tile_at(i, TILE)
        grad = nn(wup_ref[...], gb_t[:, at])
        normed = n2_t[:, at]
        gg_cols[:, 1:2] += jnp.sum(grad * normed, axis=1, keepdims=True)
        back = norm_back_rows(grad * gain_two, normed, inv_rows[1:2, at])
        mixed = (g_t[:, at].astype(F32) + back).astype(BF16)
        gm_t[:, at] = mixed
        kept = jnp.where(live_tile(at, TILE), mixed.astype(F32), 0.0)
        kept_rows = jnp.transpose(kept).astype(BF16)
        gbr_r[at, :] = kept_rows
        ga_t[:, at] = nn(wproj_ref[...], kept.astype(BF16)).astype(BF16)
        ga_r[at, :] = nn(kept_rows, wproj_t[...]).astype(BF16)

    loop(0, tiles, back_norm_two, 4)
    for l, u in enumerate(tiles_of(nn(att_t[...], gbr_r[...]), 2)):
        grad2[96 + l * 16 : 112 + l * 16] = u

    one[1]()

    def back_attend(b):
        at = tile_at(b, BLK)
        weights = w_t[b]
        wide = spread_windows(weights.astype(BF16), diagonal)
        gkv_r[at, CH : 2 * CH] = nn(wide, head_rows(ga_r[at, :])).astype(BF16)
        dense = nn(proj_r[at, 2 * CH : 3 * CH], head_columns(ga_t[:, at]))
        grad_w = pack_windows(dense, window_of_lane)
        inner = jnp.sum(weights * grad_w, axis=0, keepdims=True)
        grad_s = (weights * (grad_w - inner) * SCALE).astype(BF16)
        wide_s = spread_windows(grad_s, diagonal)
        gkv_r[at, 0:CH] = nn(wide_s, head_rows(proj_r[at, 0:CH])).astype(BF16)
        for h in range(HEADS):
            k = proj_t[CH + h * HD : CH + (h + 1) * HD, at]
            gq_t[h * HD : (h + 1) * HD, at] = nn(k, wide_s[:, h * BLK : (h + 1) * BLK]).astype(BF16)

    loop(0, ROWS // BLK, back_attend, 8)
    one[2]()

    for l, u in enumerate(tiles_of(nn(gq_t[...], h1_r[...]), 2)):
        grad2[l * 16 : (l + 1) * 16] = u
    for p in range(2):
        for l, u in enumerate(tiles_of(nn(h1_t[...], gkv_r[:, p * CH : (p + 1) * CH]), 2)):
            grad2[(p + 1) * 32 + l * 16 : (p + 1) * 32 + (l + 1) * 16] = u
    two[0]()

    def back_norm_one(i):
        at = tile_at(i, TILE)
        grad = nn(wqkv_ref[:, 0:CH], gq_t[:, at]) + jnp.transpose(
            nn(gkv_r[at, :], wqkv_t[CH : 3 * CH, :])
        )
        normed = n1_t[:, at]
        gg_cols[:, 0:1] += jnp.sum(grad * normed, axis=1, keepdims=True)
        back = norm_back_rows(grad * gain_one, normed, inv_rows[0:1, at])
        dx_r[at, :] = jnp.transpose(gm_t[:, at].astype(F32) + back).astype(BF16)

    loop(0, tiles, back_norm_one, 4)
    one_s3()
    two[1]()
    gain_start(0, jnp.transpose(gg_cols[...]))

    def give_back(i):
        pick = select_rows((i * TILE).astype(F32), TILE, rank_rows[1:2, :])
        sendr[tile_at(i, TILE // SHARE)] = to_units(nn(pick, dx_r[...]))

    loop(0, tiles, give_back, 4)
    stores = [
        pltpu.make_async_copy(src, dst, store_sems.at[k])
        for k, (src, dst) in enumerate(
            ((grad1, out1_ref), (grad2, out2_ref))
        )
    ]
    a2a_own(sendr, outr_ref, 4)
    cuts = (1, 32, 64, 96)
    a2a_some(sendr, outr_ref, 4, cuts[0], cuts[1])
    two[2]()
    one_s4()
    a2a_some(sendr, outr_ref, 4, cuts[1], cuts[2])
    gain_start(1, gain_wait(0))
    two_s3()
    one_s5()
    a2a_some(sendr, outr_ref, 4, cuts[2], cuts[3])
    gain_start(2, gain_wait(1))
    two_s5()
    one[6]()
    a2a_some(sendr, outr_ref, 4, cuts[3], n_pts)
    gain_start(3, gain_wait(2))
    two[6]()
    one[7]()
    two[7]()
    one[8]()
    stores[0].start()
    gsum[...] = gain_wait(3)
    keep_gains = pltpu.make_async_copy(gsum, ogain_ref, store_sems.at[3])
    keep_gains.start()
    two[8]()
    stores[1].start()
    a2a_wait_recv(outr_ref, 4)
    a2a_wait_send(sendx, 0)
    a2a_wait_send(sendg, 2)
    a2a_wait_send(sendr, 4)
    for store in stores:
        store.wait()
    keep_ranks.wait()
    keep_gains.wait()


def finish(
    grad_scale,
    u1_hbm,
    u2_hbm,
    ur_hbm,
    ranks_hbm,
    gains_hbm,
    dx_hbm,
    qkv_hbm,
    proj_hbm,
    up_hbm,
    down_hbm,
    gain_one_ref,
    gain_two_ref,
    u1_ref,
    u2_ref,
    ur_ref,
    ranks_ref,
    gains_ref,
    dx_ref,
    oqkv_ref,
    oproj_ref,
    oup_ref,
    odown_ref,
    load_sems,
    sems,
):
    half = 128
    pairs = (
        (u1_hbm.at[pl.ds(half, half)], u1_ref.at[pl.ds(half, half)]),
        (ur_hbm, ur_ref),
        (ranks_hbm, ranks_ref),
        (u1_hbm.at[pl.ds(0, half)], u1_ref.at[pl.ds(0, half)]),
        (u2_hbm, u2_ref),
        (gains_hbm, gains_ref),
    )
    loads = [pltpu.make_async_copy(a, b, load_sems.at[k]) for k, (a, b) in enumerate(pairs)]
    for load in loads:
        load.start()
    stores = [
        pltpu.make_async_copy(src, dst, sems.at[k])
        for k, (src, dst) in enumerate(
            (
                (oup_ref, up_hbm),
                (odown_ref, down_hbm),
                (oqkv_ref, qkv_hbm),
                (oproj_ref, proj_hbm),
                (dx_ref, dx_hbm),
            )
        )
    ]

    def block(ref, first):
        left = ref[first : first + 16].reshape(TILE, 128).astype(F32)
        right = ref[first + 16 : first + 32].reshape(TILE, 128).astype(F32)
        return jnp.concatenate([left, right], axis=1) * grad_scale

    loads[0].wait()
    for f in range(FFN // TILE):
        odown_ref[f * TILE : (f + 1) * TILE, :] = block(u1_ref, 128 + f * 32)
    stores[1].start()
    loads[1].wait()
    loads[2].wait()
    left, right = from_units(ur_ref[...])
    arrived = jnp.concatenate([left, right], axis=1).astype(BF16)
    ranks = jnp.transpose(ranks_ref[...])
    for i in range(ROWS // TILE):
        slot = lax.broadcasted_iota(jnp.int32, (TILE, ROWS), 1).astype(F32)
        pick = jnp.where(ranks[i * TILE : (i + 1) * TILE, 0:1] == slot, 1.0, 0.0).astype(BF16)
        dx_ref[i * TILE : (i + 1) * TILE, :] = nn(pick, arrived).astype(BF16)
    stores[4].start()
    loads[3].wait()
    for f in range(FFN // TILE):
        at = slice(f * TILE, (f + 1) * TILE)
        oup_ref[:, at] = jnp.transpose(block(u1_ref, f * 32))
    stores[0].start()
    loads[4].wait()
    oqkv_ref[:, 0:CH] = jnp.transpose(block(u2_ref, 0))
    oqkv_ref[:, CH : 2 * CH] = block(u2_ref, 32)
    oqkv_ref[:, 2 * CH : 3 * CH] = block(u2_ref, 64)
    stores[2].start()
    oproj_ref[...] = block(u2_ref, 96)
    stores[3].start()
    loads[5].wait()
    gain_one_ref[...] = gains_ref[0:1, :] * grad_scale
    gain_two_ref[...] = gains_ref[1:2, :] * grad_scale
    for store in stores:
        store.wait()


def units(n):
    return pltpu.VMEM((n, 16, 128), BF16)


def shards(
    features,
    cotangent,
    morton_target,
    morton_source,
    counts,
    w_qkv,
    w_proj,
    w_up,
    w_down,
    gain_one,
    gain_two,
):
    n_pts = lax.axis_size("pts")
    grad_scale = 1.0 / math.sqrt(features.shape[0] * n_pts * lax.axis_size("quad"))
    rows = lambda n, kind: pltpu.VMEM((n, ROWS), kind)
    wide = lambda n: pltpu.VMEM((ROWS, n), BF16)
    sem = pltpu.SemaphoreType.DMA
    vmem = pl.BlockSpec(memory_space=pltpu.VMEM)
    anywhere = pl.BlockSpec(memory_space=pl.ANY)
    hbm = pl.BlockSpec(memory_space=pltpu.HBM)
    parts = pl.pallas_call(
        functools.partial(kernel, n_pts),
        out_shape=(
            jax.ShapeDtypeStruct((256, 16, 128), BF16),
            jax.ShapeDtypeStruct((128, 16, 128), BF16),
            jax.ShapeDtypeStruct((n_pts, 16, 128), BF16),
            jax.ShapeDtypeStruct((8, ROWS), F32),
            jax.ShapeDtypeStruct((8, CH), F32),
        ),
        in_specs=[hbm] * 11,
        out_specs=[anywhere] * 5,
        scratch_shapes=[
            pltpu.VMEM((8, 128), jnp.int32),
            pltpu.VMEM((8, 128), jnp.int32),
            pltpu.VMEM((1, WINDOW), jnp.int32),
            pltpu.VMEM((1, CH), F32),
            pltpu.VMEM((1, CH), F32),
            wide(CH),
            wide(CH),
            pltpu.VMEM((CH, 3 * CH), BF16),
            pltpu.VMEM((CH, CH), BF16),
            pltpu.VMEM((CH, FFN), BF16),
            pltpu.VMEM((FFN, CH), BF16),
        ]
        + [units(n_pts)] * 5
        + [
            rows(8, F32),
            pltpu.VMEM((ROWS, 8), F32),
            rows(8, F32),
            pltpu.VMEM((CH, 8), F32),
            pltpu.VMEM((3 * CH, CH), BF16),
            pltpu.VMEM((CH, CH), BF16),
            pltpu.VMEM((FFN, CH), BF16),
            rows(CH, BF16),
            rows(CH, F32),
            rows(CH, BF16),
            wide(CH),
            rows(8, F32),
            rows(3 * CH, BF16),
            wide(3 * CH),
            pltpu.VMEM((ROWS // BLK, WINDOW, HEADS * BLK), F32),
            rows(CH, BF16),
            rows(CH, F32),
            rows(CH, BF16),
            wide(CH),
            rows(FFN, BF16),
            rows(FFN, F32),
            rows(CH, BF16),
            wide(CH),
            rows(FFN, BF16),
            rows(CH, BF16),
            wide(CH),
            rows(CH, BF16),
            wide(CH),
            rows(CH, BF16),
            wide(2 * CH),
            wide(CH),
            pltpu.VMEM((CH, 8), F32),
            units(256),
            units(128),
            units(128),
            pltpu.VMEM((4, 16, 16, 128), BF16),
            pltpu.VMEM((4, 16, 16, 128), BF16),
            units(32),
            pltpu.VMEM((4, 4, 16, 128), BF16),
            pltpu.VMEM((4, 4, 16, 128), BF16),
            units(8),
            units(8),
            units(128),
            units(64),
            units(64),
            pltpu.VMEM((4, 8, 16, 128), BF16),
            pltpu.VMEM((4, 8, 16, 128), BF16),
            units(16),
            pltpu.VMEM((4, 2, 16, 128), BF16),
            pltpu.VMEM((4, 2, 16, 128), BF16),
            pltpu.VMEM((8, 4, 16, 128), BF16),
            pltpu.VMEM((2, 8, CH), F32),
            pltpu.VMEM((4, 8, CH), F32),
            pltpu.VMEM((4, 8, CH), F32),
            pltpu.VMEM((8, 8, CH), F32),
            pltpu.VMEM((8, CH), F32),
            sem((6,)),
            sem((8,)),
            sem((16, 4)),
            sem((16, 4)),
            sem((3, 8)),
            sem((3, 8)),
            sem((2,)),
            sem((2, 4)),
            sem((2, 4)),
            sem((8,)),
            sem((8,)),
            sem((11,)),
            sem((4,)),
        ],
        compiler_params=pltpu.CompilerParams(
            collective_id=0, has_side_effects=True, vmem_limit_bytes=60 * 1024 * 1024
        ),
    )(
        morton_target.reshape(8, 128),
        morton_source.reshape(8, 128),
        counts.reshape(1, WINDOW),
        gain_one.reshape(1, CH),
        gain_two.reshape(1, CH),
        features,
        cotangent,
        w_qkv,
        w_proj,
        w_up,
        w_down,
    )
    shapes = (
        ((ROWS, CH), BF16),
        ((CH, 3 * CH), F32),
        ((CH, CH), F32),
        ((CH, FFN), F32),
        ((FFN, CH), F32),
    )
    out = pl.pallas_call(
        functools.partial(finish, grad_scale),
        out_shape=tuple(jax.ShapeDtypeStruct(*shape) for shape in shapes)
        + (jax.ShapeDtypeStruct((1, CH), F32),) * 2,
        in_specs=[hbm] * 5,
        out_specs=[anywhere] * 5 + [vmem] * 2,
        scratch_shapes=[
            units(256),
            units(128),
            units(n_pts),
            rows(8, F32),
            pltpu.VMEM((8, CH), F32),
        ]
        + [pltpu.VMEM(*shape) for shape in shapes]
        + [sem((6,)), sem((5,))],
        compiler_params=pltpu.CompilerParams(vmem_limit_bytes=60 * 1024 * 1024),
    )(*parts)
    dx, grad_qkv, grad_proj, grad_up, grad_down, gain_one_grad, gain_two_grad = out
    return (
        dx,
        grad_qkv,
        grad_proj,
        grad_up,
        grad_down,
        gain_one_grad.reshape(CH),
        gain_two_grad.reshape(CH),
    )


def solution(mesh):
    placed = (
        P(("pts", "quad"), None),
        P(("pts", "quad"), None),
        P(("pts", "quad")),
        P(("pts", "quad")),
        P(("pts", "quad")),
        P(),
        P(),
        P(),
        P(),
        P(),
        P(),
    )
    return jax.shard_map(
        shards,
        mesh=mesh,
        in_specs=placed,
        out_specs=(P(("pts", "quad"), None), P(), P(), P(), P(), P(), P()),
        check_vma=False,
    )
```

```python
import functools
import math

import jax
import jax.numpy as jnp
from jax import lax
from jax.experimental import pallas as pl
from jax.experimental.pallas import tpu as pltpu
from jax.sharding import PartitionSpec as P

HEADS = 8
WINDOW = 32
DILATION = 4
ROWS = 1024
CH = 256
FFN = 1024
HD = 32
BLK = 128
TILE = 256
SHARE = 8
NEG_FILL = -1e30
SCALE = 1.0 / math.sqrt(HD)

F32 = jnp.float32
BF16 = jnp.bfloat16
MESH = pl.DeviceIdType.MESH

NY, NZ, NX, NC = 4, 8, 4, 2


def nn(a, b):
    return lax.dot_general(a, b, (((1,), (0,)), ((), ())), preferred_element_type=F32)


def nt(a, b):
    return lax.dot_general(a, b, (((1,), (1,)), ((), ())), preferred_element_type=F32)


def tn(a, b):
    return lax.dot_general(a, b, (((0,), (0,)), ((), ())), preferred_element_type=F32)


def loop(start, stop, body, unroll=1):
    def step(i, carry):
        for k in range(unroll):
            body(i * unroll + k)
        return carry

    lax.fori_loop(start // unroll, stop // unroll, step, 0)


def transposed(a):
    return jnp.transpose(a.astype(F32)).astype(a.dtype)


def tile_at(i, size):
    return pl.ds(pl.multiple_of(i * size, size), size)


def norm_rows(values):
    mean = jnp.mean(values, axis=0, keepdims=True)
    centred = values - mean
    inverse = lax.rsqrt(jnp.mean(centred * centred, axis=0, keepdims=True) + 1e-05)
    return centred * inverse, inverse


def norm_back_rows(grad, normed, inverse):
    first = jnp.mean(grad, axis=0, keepdims=True)
    second = jnp.mean(grad * normed, axis=0, keepdims=True)
    return inverse * (grad - first - normed * second)


def pack_windows(dense, window_of_lane):
    packed = dense[3 * WINDOW :]
    for k in (2, 1, 0):
        packed = jnp.where(window_of_lane == k, dense[k * WINDOW : (k + 1) * WINDOW], packed)
    return packed


def spread_windows(packed, diagonal):
    return jnp.concatenate([packed] * DILATION, axis=0) * diagonal


def to_units(y):
    n = y.shape[0] // SHARE
    left = y[:, :128].reshape(n, SHARE, 128)
    right = y[:, 128:].reshape(n, SHARE, 128)
    return jnp.concatenate([left, right], axis=1).astype(BF16)


def from_units(u):
    r = u.astype(F32)
    n = r.shape[0]
    left = r[:, :SHARE, :].reshape(n * SHARE, 128)
    right = r[:, SHARE:, :].reshape(n * SHARE, 128)
    return left, right


def head_columns(t):
    blocks = []
    for h in range(HEADS):
        own = t[h * HD : (h + 1) * HD]
        pieces = [own]
        if h > 0:
            pieces.insert(0, jnp.zeros((h * HD, BLK), t.dtype))
        if h < HEADS - 1:
            pieces.append(jnp.zeros(((HEADS - 1 - h) * HD, BLK), t.dtype))
        blocks.append(jnp.concatenate(pieces, axis=0))
    return jnp.concatenate(blocks, axis=1)


def head_rows(r):
    head = lax.broadcasted_iota(jnp.int32, (1, CH), 1) // HD
    return jnp.concatenate(
        [r * jnp.where(head == h, 1.0, 0.0).astype(r.dtype) for h in range(HEADS)], axis=0
    )


def flip(a):
    return jnp.transpose(a.astype(F32)).astype(BF16)


def kernel(
    n_pts,
    target_hbm,
    source_hbm,
    counts_hbm,
    gain_one_hbm,
    gain_two_hbm,
    x_hbm,
    g_hbm,
    wqkv_hbm,
    wproj_hbm,
    wup_hbm,
    wdown_hbm,
    out1_ref,
    out2_ref,
    outr_ref,
    ranks_ref,
    ogain_ref,
    target_ref,
    source_ref,
    counts_ref,
    gain_one_ref,
    gain_two_ref,
    x_ref,
    g_ref,
    wqkv_ref,
    wproj_ref,
    wup_ref,
    wdown_ref,
    sendx,
    recvx,
    sendg,
    recvg,
    sendr,
    rank_rows,
    rank_cols,
    count_rows,
    gain_cols,
    wqkv_t,
    wproj_t,
    wup_t,
    x_t,
    n1_t,
    h1_t,
    h1_r,
    inv_rows,
    proj_t,
    proj_r,
    w_t,
    att_t,
    n2_t,
    h2_t,
    h2_r,
    act_t,
    dg_t,
    g_t,
    g_r,
    gb_t,
    gm_t,
    gbr_r,
    ga_t,
    ga_r,
    gq_t,
    gkv_r,
    dx_r,
    gg_cols,
    grad1,
    core1,
    cur1,
    ra1,
    rb1,
    mid1,
    rc1,
    rd1,
    zin1,
    rz1,
    grad2,
    core2,
    cur2,
    ra2,
    rb2,
    mid2,
    rc2,
    rd2,
    rz2,
    gcore,
    gx,
    gy,
    gz,
    gsum,
    a2a_sems,
    core_sems,
    four_send,
    four_recv,
    z_send,
    z_recv,
    gcore_sems,
    gfour_send,
    gfour_recv,
    gz_send,
    gz_recv,
    load_sems,
    store_sems,
):
    me = lax.axis_index("pts")
    quad = lax.axis_index("quad")
    core = lax.rem(me, NC)
    x_hi = lax.rem(me // NC, 2)
    z = lax.rem(me // (2 * NC), NZ)
    y = me // (2 * NC * NZ)
    x = x_hi * 2 + quad

    def core_dev():
        return {"pts": me + 1 - 2 * core, "quad": quad}

    def x_dev(other):
        return {"pts": me + (other // 2 - x_hi) * NC, "quad": lax.rem(other, 2)}

    def y_dev(other):
        return {"pts": me + (other - y) * (2 * NC * NZ), "quad": quad}

    def z_dev(other):
        return {"pts": me + (other - z) * (2 * NC), "quad": quad}

    loads = [
        pltpu.make_async_copy(src, dst, load_sems.at[k])
        for k, (src, dst) in enumerate(
            (
                (target_hbm, target_ref),
                (source_hbm, source_ref),
                (counts_hbm, counts_ref),
                (gain_one_hbm, gain_one_ref),
                (gain_two_hbm, gain_two_ref),
                (x_hbm, x_ref),
                (g_hbm, g_ref),
                (wqkv_hbm, wqkv_ref),
                (wproj_hbm, wproj_ref),
                (wup_hbm, wup_ref),
                (wdown_hbm, wdown_ref),
            )
        )
    ]
    for load in loads:
        load.start()

    barrier = pltpu.get_barrier_semaphore()

    def greet(k):
        pl.semaphore_signal(
            barrier, inc=1, device_id={"pts": lax.rem(me + k, n_pts), "quad": quad}, device_id_type=MESH
        )

    loop(1, n_pts, greet)
    for hi in range(2):
        pl.semaphore_signal(
            barrier,
            inc=1,
            device_id={"pts": me + (hi - x_hi) * NC, "quad": 1 - quad},
            device_id_type=MESH,
        )

    for load in loads[:5]:
        load.wait()

    def one_row(a):
        return jnp.concatenate([a[r : r + 1, :] for r in range(8)], axis=1)

    stored = lax.broadcasted_iota(jnp.int32, (8, 128), 0) * 128 + lax.broadcasted_iota(
        jnp.int32, (8, 128), 1
    )
    target_key = one_row(((target_ref[...] >> 11) * ROWS + stored).astype(F32))
    to_lane = lax.broadcasted_iota(jnp.int32, (BLK, BLK), 1)
    from_lane = lax.broadcasted_iota(jnp.int32, (BLK, BLK), 0)
    moved = jnp.where(
        from_lane == lax.rem(to_lane, WINDOW) * DILATION + to_lane // WINDOW, 1.0, 0.0
    ).astype(BF16)
    src = source_ref[...]
    digits = jnp.concatenate([src & 63, (src >> 6) & 63, src >> 12], axis=0)
    digits = nn(digits.astype(F32).astype(BF16), moved)
    source_key = one_row(digits[0:8] + 64.0 * digits[8:16] + 4096.0 * digits[16:24])
    spread = jnp.where(
        lax.broadcasted_iota(jnp.int32, (WINDOW, ROWS), 1) // WINDOW
        == lax.broadcasted_iota(jnp.int32, (WINDOW, ROWS), 0),
        1.0,
        0.0,
    ).astype(BF16)
    wide_counts = jnp.broadcast_to(counts_ref[...].astype(F32), (8, WINDOW)).astype(BF16)
    count_rows[...] = nn(wide_counts, spread)
    pad = jnp.zeros((6, ROWS), F32)
    rank_rows[...] = jnp.concatenate([target_key, source_key, pad], axis=0)
    rank_cols[...] = jnp.transpose(rank_rows[...])

    keys = rank_rows[...]

    def count(i, carry):
        t, s = carry
        cols = rank_cols[tile_at(i, 64), :]
        t = t + jnp.sum(jnp.where(cols[:, 0:1] < keys[0:1, :], 1.0, 0.0), axis=0, keepdims=True)
        s = s + jnp.sum(jnp.where(cols[:, 1:2] < keys[1:2, :], 1.0, 0.0), axis=0, keepdims=True)
        return t, s

    zero_row = jnp.zeros((1, ROWS), F32)
    rank_target, rank_source = lax.fori_loop(0, ROWS // 64, count, (zero_row, zero_row))
    rank_rows[...] = jnp.concatenate([rank_target, rank_source, pad], axis=0)
    rank_cols[...] = jnp.transpose(rank_rows[...])

    def select_rows(first, size, ranks):
        slot = lax.broadcasted_iota(jnp.int32, (size, ranks.shape[1]), 0).astype(F32)
        return jnp.where(slot + first == ranks, 1.0, 0.0).astype(BF16)

    def place(i, source_ref, out):
        pick = select_rows((i * TILE).astype(F32), TILE, rank_rows[0:1, :])
        out[tile_at(i, TILE // SHARE)] = to_units(nn(pick, source_ref[...]))

    def a2a(send, recv, index, k):
        peer = lax.rem(me + k, n_pts)
        return pltpu.make_async_remote_copy(
            src_ref=send.at[peer],
            dst_ref=recv.at[me],
            send_sem=a2a_sems.at[index],
            recv_sem=a2a_sems.at[index + 1],
            device_id={"pts": peer, "quad": quad},
            device_id_type=MESH,
        )

    def a2a_some(send, recv, index, first, stop):
        loop(first, stop, lambda j: a2a(send, recv, index, 1 + lax.rem((j - 1) * 37, n_pts - 1)).start())

    def a2a_own(send, recv, index):
        pltpu.make_async_copy(send.at[me], recv.at[me], a2a_sems.at[index + 1]).start()

    def a2a_start(send, recv, index):
        a2a_own(send, recv, index)
        a2a_some(send, recv, index, 1, n_pts)

    def a2a_wait_recv(recv, index):
        pltpu.make_async_copy(recv, recv, a2a_sems.at[index + 1]).wait()

    def a2a_wait_send(send, index):
        part = send.at[pl.ds(0, n_pts - 1)]
        pltpu.make_async_copy(part, part, a2a_sems.at[index]).wait()

    keep_ranks = pltpu.make_async_copy(rank_rows, ranks_ref, store_sems.at[2])
    keep_ranks.start()
    tiles = ROWS // TILE
    loads[5].wait()
    loop(0, tiles, lambda i: place(i, x_ref, sendx))
    pl.semaphore_wait(barrier, n_pts + 1)
    a2a_start(sendx, recvx, 0)
    loads[6].wait()
    loop(0, tiles, lambda i: place(i, g_ref, sendg))
    a2a_start(sendg, recvg, 2)

    for load in loads[7:]:
        load.wait()
    wqkv_t[...] = transposed(wqkv_ref[...])
    wproj_t[...] = transposed(wproj_ref[...])
    wup_t[...] = transposed(wup_ref[...])
    gain_cols[...] = jnp.transpose(
        jnp.concatenate([gain_one_ref[...], gain_two_ref[...], jnp.zeros((6, CH), F32)], axis=0)
    )
    gain_one = gain_cols[:, 0:1]
    gain_two = gain_cols[:, 1:2]

    span = HEADS * BLK
    sub = lax.broadcasted_iota(jnp.int32, (WINDOW, span), 0).astype(F32)
    window_of_lane = lax.rem(lax.broadcasted_iota(jnp.int32, (WINDOW, span), 1), BLK) // WINDOW
    diagonal = jnp.where(
        lax.broadcasted_iota(jnp.int32, (BLK, span), 0) // WINDOW
        == lax.rem(lax.broadcasted_iota(jnp.int32, (BLK, span), 1), BLK) // WINDOW,
        1.0,
        0.0,
    ).astype(BF16)

    def live_tile(at, size):
        slot = lax.rem(lax.broadcasted_iota(jnp.int32, (1, size), 1), WINDOW).astype(F32)
        return slot < count_rows[0:1, at]

    def arrive(recv, out, out_rows):
        left, right = from_units(recv[...])
        arrived = jnp.concatenate([left, right], axis=1).astype(BF16)

        def one(i):
            at = tile_at(i, TILE)
            slot = lax.broadcasted_iota(jnp.int32, (TILE, ROWS), 1).astype(F32)
            pick = jnp.where(rank_cols[at, 1:2] == slot, 1.0, 0.0).astype(BF16)
            points = nn(pick, arrived)
            out[:, at] = jnp.transpose(points).astype(BF16)
            if out_rows is not None:
                out_rows[at, :] = points.astype(BF16)

        loop(0, tiles, one, 4)

    a2a_wait_recv(recvx, 0)
    arrive(recvx, x_t, None)

    def first_norm(i):
        at = tile_at(i, TILE)
        normed, inverse = norm_rows(x_t[:, at].astype(F32))
        n1_t[:, at] = normed
        inv_rows[0:1, at] = inverse
        scaled = normed * gain_one
        hidden = scaled.astype(BF16)
        hidden_rows = jnp.transpose(scaled).astype(BF16)
        h1_t[:, at] = hidden
        h1_r[at, :] = hidden_rows
        proj_t[:, at] = nn(wqkv_t[...], hidden).astype(BF16)
        proj_r[at, :] = nn(hidden_rows, wqkv_ref[...]).astype(BF16)

    loop(0, tiles, first_norm, 4)

    def attend(b):
        at = tile_at(b, BLK)
        counted = jnp.concatenate([count_rows[0:1, at]] * HEADS, axis=1)
        dense = nn(proj_r[at, CH : 2 * CH], head_columns(proj_t[0:CH, at]))
        scores = pack_windows(dense, window_of_lane) * SCALE
        scores = jnp.where(sub < counted, scores, NEG_FILL)
        powered = jnp.exp(scores - jnp.max(scores, axis=0, keepdims=True))
        weights = powered / jnp.sum(powered, axis=0, keepdims=True)
        w_t[b] = weights
        wide = spread_windows(weights.astype(BF16), diagonal)
        for h in range(HEADS):
            v = proj_t[2 * CH + h * HD : 2 * CH + (h + 1) * HD, at]
            att_t[h * HD : (h + 1) * HD, at] = nn(v, wide[:, h * BLK : (h + 1) * BLK]).astype(BF16)

    loop(0, ROWS // BLK, attend, 8)

    def forward_mlp(i):
        at = tile_at(i, TILE)
        branch = nn(wproj_t[...], att_t[:, at])
        mixed = x_t[:, at].astype(F32) + jnp.where(live_tile(at, TILE), branch, 0.0)
        normed, inverse = norm_rows(mixed.astype(BF16).astype(F32))
        n2_t[:, at] = normed
        inv_rows[1:2, at] = inverse
        scaled = normed * gain_two
        hidden = scaled.astype(BF16)
        h2_t[:, at] = hidden
        h2_r[at, :] = jnp.transpose(scaled).astype(BF16)
        for f in range(FFN // TILE):
            rows = pl.ds(f * TILE, TILE)
            before = nn(wup_t[rows, :], hidden)
            cumulative = 0.5 * (1.0 + lax.erf(before * 0.7071067811865476))
            act_t[rows, at] = (before * cumulative).astype(BF16)
            density = jnp.exp(-0.5 * before * before) * 0.3989422804014327
            dg_t[rows, at] = cumulative + before * density

    loop(0, tiles, forward_mlp)

    a2a_wait_recv(recvg, 2)
    arrive(recvg, g_t, g_r)

    def back_act(i):
        at = tile_at(i, TILE)
        for f in range(FFN // TILE):
            rows = pl.ds(f * TILE, TILE)
            gb_t[rows, at] = (nn(wdown_ref[rows, :], g_t[:, at]) * dg_t[rows, at]).astype(BF16)

    loop(0, tiles, back_act, 4)

    def tiles_of(y, lanes):
        return [y[:, l * 128 : (l + 1) * 128].reshape(16, 16, 128).astype(BF16) for l in range(lanes)]

    def up_down(f):
        rows = tile_at(f, TILE)
        for l, u in enumerate(tiles_of(nn(act_t[rows, :], g_r[...]), 2)):
            grad1[pl.ds(128 + f * 32 + l * 16, 16)] = u
        for l, u in enumerate(tiles_of(nn(gb_t[rows, :], h2_r[...]), 2)):
            grad1[pl.ds(f * 32 + l * 16, 16)] = u

    loop(0, FFN // TILE, up_down, 4)

    def four_copies(src, dst_of, which, mine, dev, sem_base):
        copies = []
        for d in range(1, 4):
            other = lax.rem(mine + d, 4)
            copies.append(
                pltpu.make_async_remote_copy(
                    src_ref=src(other),
                    dst_ref=dst_of,
                    send_sem=four_send.at[sem_base + which, d],
                    recv_sem=four_recv.at[sem_base + which, mine],
                    device_id=dev(other),
                    device_id_type=MESH,
                )
            )
        return copies

    def four_wait(src, dst, which, mine, dev, sem_base):
        for d in range(1, 4):
            other = lax.rem(mine + d, 4)
            got = pltpu.make_async_remote_copy(
                src_ref=src(other),
                dst_ref=dst(other),
                send_sem=four_send.at[sem_base + which, d],
                recv_sem=four_recv.at[sem_base + which, other],
                device_id=dev(other),
                device_id_type=MESH,
            )
            got.wait_recv()
            got.wait_send()

    def group(index, grad, from_core, cur, ra, rb, mid, rc, rd, nk):
        half = nk * 32
        part = half // 2
        quarter = part // 4
        base = index * 4
        cbase = index * 4

        def core_copy(src, dst, sem):
            return pltpu.make_async_remote_copy(
                src_ref=src,
                dst_ref=dst,
                send_sem=core_sems.at[cbase + sem],
                recv_sem=core_sems.at[cbase + sem + 1],
                device_id=core_dev(),
                device_id_type=MESH,
            )

        def first_core():
            return core_copy(grad.at[pl.ds((1 - core) * half, half)], from_core, 0)

        def s0():
            first_core().start()

        def cur_a(o):
            return cur.at[pl.ds(o * quarter, quarter)]

        def cur_b(o):
            return cur.at[pl.ds(part + o * quarter, quarter)]

        def s1():
            first_core().wait()
            total = grad[pl.ds(core * half, half)].astype(F32) + from_core[...].astype(F32)
            cur[...] = total.astype(BF16)
            for c in four_copies(cur_a, ra.at[x], 0, x, x_dev, base):
                c.start()
            for c in four_copies(cur_b, rb.at[y], 1, y, y_dev, base):
                c.start()

        def mid_a(o):
            return mid.at[pl.ds(o * nk, nk)]

        def mid_b(o):
            return mid.at[pl.ds(quarter + o * nk, nk)]

        def add_four(own, slots, mine):
            total = own.astype(F32)
            for d in range(1, 4):
                total = total + slots[lax.rem(mine + d, 4)].astype(F32)
            return total.astype(BF16)

        def s2():
            four_wait(cur_a, lambda o: ra.at[o], 0, x, x_dev, base)
            four_wait(cur_b, lambda o: rb.at[o], 1, y, y_dev, base)
            mid[pl.ds(0, quarter)] = add_four(cur[pl.ds(x * quarter, quarter)], ra, x)
            mid[pl.ds(quarter, quarter)] = add_four(cur[pl.ds(part + y * quarter, quarter)], rb, y)
            for c in four_copies(mid_a, rc.at[y], 2, y, y_dev, base):
                c.start()
            for c in four_copies(mid_b, rd.at[x], 3, x, x_dev, base):
                c.start()

        def s3():
            four_wait(mid_a, lambda o: rc.at[o], 2, y, y_dev, base)
            four_wait(mid_b, lambda o: rd.at[o], 3, x, x_dev, base)
            a = add_four(mid[pl.ds(y * nk, nk)], rc, y)
            b = add_four(mid[pl.ds(quarter + x * nk, nk)], rd, x)
            return a, b

        mine = core * half

        def out_a(xx, yy):
            return grad.at[pl.ds(mine + xx * quarter + yy * nk, nk)]

        def out_b(xx, yy):
            return grad.at[pl.ds(mine + part + yy * quarter + xx * nk, nk)]

        def whole_a(xx):
            return grad.at[pl.ds(mine + xx * quarter, quarter)]

        def whole_b(yy):
            return grad.at[pl.ds(mine + part + yy * quarter, quarter)]

        gbase = 8 + index * 4

        def s5():
            for c in four_copies(lambda o: out_a(x, y), out_a(x, y), 0, y, y_dev, gbase):
                c.start()
            for c in four_copies(lambda o: out_b(x, y), out_b(x, y), 1, x, x_dev, gbase):
                c.start()

        def s6():
            four_wait(lambda o: out_a(x, y), lambda o: out_a(x, o), 0, y, y_dev, gbase)
            four_wait(lambda o: out_b(x, y), lambda o: out_b(o, y), 1, x, x_dev, gbase)
            for c in four_copies(lambda o: whole_a(x), whole_a(x), 2, x, x_dev, gbase):
                c.start()
            for c in four_copies(lambda o: whole_b(y), whole_b(y), 3, y, y_dev, gbase):
                c.start()

        def last_core():
            at = grad.at[pl.ds(mine, half)]
            return core_copy(at, at, 2)

        def s7():
            four_wait(lambda o: whole_a(x), lambda o: whole_a(o), 2, x, x_dev, gbase)
            four_wait(lambda o: whole_b(y), lambda o: whole_b(o), 3, y, y_dev, gbase)
            last_core().start()

        def s8():
            last_core().wait()

        def put(a, b):
            grad[pl.ds(mine + x * quarter + y * nk, nk)] = a
            grad[pl.ds(mine + part + y * quarter + x * nk, nk)] = b

        return s0, s1, s2, s3, put, s5, s6, s7, s8

    def z_copy(src, dst, sems, d, slot):
        other = lax.rem(z + d, NZ)
        return pltpu.make_async_remote_copy(
            src_ref=src,
            dst_ref=dst,
            send_sem=z_send.at[sems, d],
            recv_sem=z_recv.at[sems, slot],
            device_id=z_dev(other),
            device_id_type=MESH,
        )

    one = group(0, grad1, core1, cur1, ra1, rb1, mid1, rc1, rd1, 4)
    two = group(1, grad2, core2, cur2, ra2, rb2, mid2, rc2, rd2, 2)

    def one_s3():
        a, b = one[3]()
        zin1[0:4] = a
        zin1[4:8] = b
        for d in range(1, NZ):
            z_copy(zin1.at[lax.rem(z + d, NZ)], rz1.at[z], 0, d, z).start()

    def one_out(zz):
        p = zz // 4
        k = lax.rem(zz, 4)
        first = x + p * (y - x)
        second = y + p * (x - y)
        return core * 128 + p * 64 + first * 16 + second * 4 + k

    def one_s4():
        total = zin1[z].astype(F32)
        for d in range(1, NZ):
            other = lax.rem(z + d, NZ)
            got = z_copy(zin1.at[other], rz1.at[other], 0, d, other)
            got.wait_recv()
            got.wait_send()
            total = total + rz1[other].astype(F32)
        grad1[one_out(z)] = total.astype(BF16)
        for d in range(1, NZ):
            z_copy(grad1.at[one_out(z)], grad1.at[one_out(z)], 1, d, z).start()

    def one_s5():
        for d in range(1, NZ):
            other = lax.rem(z + d, NZ)
            got = z_copy(grad1.at[one_out(z)], grad1.at[one_out(other)], 1, d, other)
            got.wait_recv()
            got.wait_send()
        one[5]()

    def two_s3():
        a, b = two[3]()
        rz2[z, 0:2] = a
        rz2[z, 2:4] = b
        for d in range(1, NZ):
            z_copy(rz2.at[z], rz2.at[z], 2, d, z).start()

    def two_s5():
        for d in range(1, NZ):
            other = lax.rem(z + d, NZ)
            got = z_copy(rz2.at[z], rz2.at[other], 2, d, other)
            got.wait_recv()
            got.wait_send()
        total = rz2[0].astype(F32)
        for k in range(1, NZ):
            total = total + rz2[k].astype(F32)
        total = total.astype(BF16)
        two[4](total[0:2], total[2:4])
        two[5]()

    def gain_copies(buf, count, mine, dev, send_sem, recv_sem, wait):
        for d in range(1, count):
            other = lax.rem(mine + d, count)
            c = pltpu.make_async_remote_copy(
                src_ref=buf.at[mine],
                dst_ref=buf.at[other] if wait else buf.at[mine],
                send_sem=send_sem(d),
                recv_sem=recv_sem(other) if wait else recv_sem(mine),
                device_id=dev(other),
                device_id_type=MESH,
            )
            if wait:
                c.wait_recv()
                c.wait_send()
            else:
                c.start()

    def add_slots(buf, count):
        total = buf[0]
        for k in range(1, count):
            total = total + buf[k]
        return total

    gain_steps = (
        (gcore, NC, core, lambda o: core_dev(), lambda d: gcore_sems.at[0], lambda o: gcore_sems.at[1]),
        (gx, NX, x, x_dev, lambda d: gfour_send.at[0, d], lambda o: gfour_recv.at[0, o]),
        (gy, NY, y, y_dev, lambda d: gfour_send.at[1, d], lambda o: gfour_recv.at[1, o]),
        (gz, NZ, z, z_dev, lambda d: gz_send.at[d], lambda o: gz_recv.at[o]),
    )

    def gain_start(step, values):
        buf, count, mine, dev, ssem, rsem = gain_steps[step]
        buf[mine] = values
        gain_copies(buf, count, mine, dev, ssem, rsem, False)

    def gain_wait(step):
        buf, count, mine, dev, ssem, rsem = gain_steps[step]
        gain_copies(buf, count, mine, dev, ssem, rsem, True)
        return add_slots(buf, count)

    one[0]()

    gg_cols[...] = jnp.zeros_like(gg_cols)

    def back_norm_two(i):
        at = tile_at(i, TILE)
        grad = nn(wup_ref[...], gb_t[:, at])
        normed = n2_t[:, at]
        gg_cols[:, 1:2] += jnp.sum(grad * normed, axis=1, keepdims=True)
        back = norm_back_rows(grad * gain_two, normed, inv_rows[1:2, at])
        mixed = (g_t[:, at].astype(F32) + back).astype(BF16)
        gm_t[:, at] = mixed
        kept = jnp.where(live_tile(at, TILE), mixed.astype(F32), 0.0)
        kept_rows = jnp.transpose(kept).astype(BF16)
        gbr_r[at, :] = kept_rows
        ga_t[:, at] = nn(wproj_ref[...], kept.astype(BF16)).astype(BF16)
        ga_r[at, :] = nn(kept_rows, wproj_t[...]).astype(BF16)

    loop(0, tiles, back_norm_two, 4)
    one[1]()
    for l, u in enumerate(tiles_of(nn(att_t[...], gbr_r[...]), 2)):
        grad2[96 + l * 16 : 112 + l * 16] = u


    def back_attend(b):
        at = tile_at(b, BLK)
        weights = w_t[b]
        wide = spread_windows(weights.astype(BF16), diagonal)
        gkv_r[at, CH : 2 * CH] = nn(wide, head_rows(ga_r[at, :])).astype(BF16)
        dense = nn(proj_r[at, 2 * CH : 3 * CH], head_columns(ga_t[:, at]))
        grad_w = pack_windows(dense, window_of_lane)
        inner = jnp.sum(weights * grad_w, axis=0, keepdims=True)
        grad_s = (weights * (grad_w - inner) * SCALE).astype(BF16)
        wide_s = spread_windows(grad_s, diagonal)
        gkv_r[at, 0:CH] = nn(wide_s, head_rows(proj_r[at, 0:CH])).astype(BF16)
        for h in range(HEADS):
            k = proj_t[CH + h * HD : CH + (h + 1) * HD, at]
            gq_t[h * HD : (h + 1) * HD, at] = nn(k, wide_s[:, h * BLK : (h + 1) * BLK]).astype(BF16)

    loop(0, ROWS // BLK, back_attend, 8)

    for l, u in enumerate(tiles_of(nn(gq_t[...], h1_r[...]), 2)):
        grad2[l * 16 : (l + 1) * 16] = u
    for p in range(2):
        for l, u in enumerate(tiles_of(nn(h1_t[...], gkv_r[:, p * CH : (p + 1) * CH]), 2)):
            grad2[(p + 1) * 32 + l * 16 : (p + 1) * 32 + (l + 1) * 16] = u
    two[0]()
    one[2]()

    def back_norm_one(i):
        at = tile_at(i, TILE)
        grad = nn(wqkv_ref[:, 0:CH], gq_t[:, at]) + jnp.transpose(
            nn(gkv_r[at, :], wqkv_t[CH : 3 * CH, :])
        )
        normed = n1_t[:, at]
        gg_cols[:, 0:1] += jnp.sum(grad * normed, axis=1, keepdims=True)
        back = norm_back_rows(grad * gain_one, normed, inv_rows[0:1, at])
        dx_r[at, :] = jnp.transpose(gm_t[:, at].astype(F32) + back).astype(BF16)

    loop(0, tiles, back_norm_one, 4)
    two[1]()
    gain_start(0, jnp.transpose(gg_cols[...]))

    def give_back(i):
        pick = select_rows((i * TILE).astype(F32), TILE, rank_rows[1:2, :])
        sendr[tile_at(i, TILE // SHARE)] = to_units(nn(pick, dx_r[...]))

    loop(0, tiles, give_back, 4)
    stores = [
        pltpu.make_async_copy(src, dst, store_sems.at[k])
        for k, (src, dst) in enumerate(
            ((grad1, out1_ref), (grad2, out2_ref))
        )
    ]
    a2a_own(sendr, outr_ref, 4)
    cuts = (1, 26, 52, 78, 104)
    a2a_some(sendr, outr_ref, 4, cuts[0], cuts[1])
    gain_start(1, gain_wait(0))
    two[2]()
    one_s3()
    a2a_some(sendr, outr_ref, 4, cuts[1], cuts[2])
    two_s3()
    gain_start(2, gain_wait(1))
    one_s4()
    a2a_some(sendr, outr_ref, 4, cuts[2], cuts[3])
    two_s5()
    gain_start(3, gain_wait(2))
    one_s5()
    a2a_some(sendr, outr_ref, 4, cuts[3], cuts[4])
    two[6]()
    one[6]()
    a2a_some(sendr, outr_ref, 4, cuts[4], n_pts)
    two[7]()
    one[7]()
    one[8]()
    stores[0].start()
    gsum[...] = gain_wait(3)
    keep_gains = pltpu.make_async_copy(gsum, ogain_ref, store_sems.at[3])
    keep_gains.start()
    two[8]()
    stores[1].start()
    a2a_wait_recv(outr_ref, 4)
    a2a_wait_send(sendx, 0)
    a2a_wait_send(sendg, 2)
    a2a_wait_send(sendr, 4)
    for store in stores:
        store.wait()
    keep_ranks.wait()
    keep_gains.wait()


def finish(
    grad_scale,
    u1_hbm,
    u2_hbm,
    ur_hbm,
    ranks_hbm,
    gains_hbm,
    dx_hbm,
    qkv_hbm,
    proj_hbm,
    up_hbm,
    down_hbm,
    gain_one_ref,
    gain_two_ref,
    u1_ref,
    u2_ref,
    ur_ref,
    ranks_ref,
    gains_ref,
    dx_ref,
    oqkv_ref,
    oproj_ref,
    oup_ref,
    odown_ref,
    load_sems,
    sems,
):
    half = 128
    pairs = (
        (u1_hbm.at[pl.ds(half, half)], u1_ref.at[pl.ds(half, half)]),
        (ur_hbm, ur_ref),
        (ranks_hbm, ranks_ref),
        (u1_hbm.at[pl.ds(0, half)], u1_ref.at[pl.ds(0, half)]),
        (u2_hbm, u2_ref),
        (gains_hbm, gains_ref),
    )
    loads = [pltpu.make_async_copy(a, b, load_sems.at[k]) for k, (a, b) in enumerate(pairs)]
    for load in loads:
        load.start()
    stores = [
        pltpu.make_async_copy(src, dst, sems.at[k])
        for k, (src, dst) in enumerate(
            (
                (oup_ref, up_hbm),
                (odown_ref, down_hbm),
                (oqkv_ref, qkv_hbm),
                (oproj_ref, proj_hbm),
                (dx_ref, dx_hbm),
            )
        )
    ]

    def block(ref, first):
        left = ref[first : first + 16].reshape(TILE, 128).astype(F32)
        right = ref[first + 16 : first + 32].reshape(TILE, 128).astype(F32)
        return jnp.concatenate([left, right], axis=1) * grad_scale

    loads[0].wait()
    for f in range(FFN // TILE):
        odown_ref[f * TILE : (f + 1) * TILE, :] = block(u1_ref, 128 + f * 32)
    stores[1].start()
    loads[1].wait()
    loads[2].wait()
    left, right = from_units(ur_ref[...])
    arrived = jnp.concatenate([left, right], axis=1).astype(BF16)
    ranks = jnp.transpose(ranks_ref[...])
    for i in range(ROWS // TILE):
        slot = lax.broadcasted_iota(jnp.int32, (TILE, ROWS), 1).astype(F32)
        pick = jnp.where(ranks[i * TILE : (i + 1) * TILE, 0:1] == slot, 1.0, 0.0).astype(BF16)
        dx_ref[i * TILE : (i + 1) * TILE, :] = nn(pick, arrived).astype(BF16)
    stores[4].start()
    loads[3].wait()
    for f in range(FFN // TILE):
        at = slice(f * TILE, (f + 1) * TILE)
        oup_ref[:, at] = jnp.transpose(block(u1_ref, f * 32))
    stores[0].start()
    loads[4].wait()
    oqkv_ref[:, 0:CH] = jnp.transpose(block(u2_ref, 0))
    oqkv_ref[:, CH : 2 * CH] = block(u2_ref, 32)
    oqkv_ref[:, 2 * CH : 3 * CH] = block(u2_ref, 64)
    stores[2].start()
    oproj_ref[...] = block(u2_ref, 96)
    stores[3].start()
    loads[5].wait()
    gain_one_ref[...] = gains_ref[0:1, :] * grad_scale
    gain_two_ref[...] = gains_ref[1:2, :] * grad_scale
    for store in stores:
        store.wait()


def units(n):
    return pltpu.VMEM((n, 16, 128), BF16)


def shards(
    features,
    cotangent,
    morton_target,
    morton_source,
    counts,
    w_qkv,
    w_proj,
    w_up,
    w_down,
    gain_one,
    gain_two,
):
    n_pts = lax.axis_size("pts")
    grad_scale = 1.0 / math.sqrt(features.shape[0] * n_pts * lax.axis_size("quad"))
    rows = lambda n, kind: pltpu.VMEM((n, ROWS), kind)
    wide = lambda n: pltpu.VMEM((ROWS, n), BF16)
    sem = pltpu.SemaphoreType.DMA
    vmem = pl.BlockSpec(memory_space=pltpu.VMEM)
    anywhere = pl.BlockSpec(memory_space=pl.ANY)
    hbm = pl.BlockSpec(memory_space=pltpu.HBM)
    parts = pl.pallas_call(
        functools.partial(kernel, n_pts),
        out_shape=(
            jax.ShapeDtypeStruct((256, 16, 128), BF16),
            jax.ShapeDtypeStruct((128, 16, 128), BF16),
            jax.ShapeDtypeStruct((n_pts, 16, 128), BF16),
            jax.ShapeDtypeStruct((8, ROWS), F32),
            jax.ShapeDtypeStruct((8, CH), F32),
        ),
        in_specs=[hbm] * 11,
        out_specs=[anywhere] * 5,
        scratch_shapes=[
            pltpu.VMEM((8, 128), jnp.int32),
            pltpu.VMEM((8, 128), jnp.int32),
            pltpu.VMEM((1, WINDOW), jnp.int32),
            pltpu.VMEM((1, CH), F32),
            pltpu.VMEM((1, CH), F32),
            wide(CH),
            wide(CH),
            pltpu.VMEM((CH, 3 * CH), BF16),
            pltpu.VMEM((CH, CH), BF16),
            pltpu.VMEM((CH, FFN), BF16),
            pltpu.VMEM((FFN, CH), BF16),
        ]
        + [units(n_pts)] * 5
        + [
            rows(8, F32),
            pltpu.VMEM((ROWS, 8), F32),
            rows(8, F32),
            pltpu.VMEM((CH, 8), F32),
            pltpu.VMEM((3 * CH, CH), BF16),
            pltpu.VMEM((CH, CH), BF16),
            pltpu.VMEM((FFN, CH), BF16),
            rows(CH, BF16),
            rows(CH, F32),
            rows(CH, BF16),
            wide(CH),
            rows(8, F32),
            rows(3 * CH, BF16),
            wide(3 * CH),
            pltpu.VMEM((ROWS // BLK, WINDOW, HEADS * BLK), F32),
            rows(CH, BF16),
            rows(CH, F32),
            rows(CH, BF16),
            wide(CH),
            rows(FFN, BF16),
            rows(FFN, F32),
            rows(CH, BF16),
            wide(CH),
            rows(FFN, BF16),
            rows(CH, BF16),
            wide(CH),
            rows(CH, BF16),
            wide(CH),
            rows(CH, BF16),
            wide(2 * CH),
            wide(CH),
            pltpu.VMEM((CH, 8), F32),
            units(256),
            units(128),
            units(128),
            pltpu.VMEM((4, 16, 16, 128), BF16),
            pltpu.VMEM((4, 16, 16, 128), BF16),
            units(32),
            pltpu.VMEM((4, 4, 16, 128), BF16),
            pltpu.VMEM((4, 4, 16, 128), BF16),
            units(8),
            units(8),
            units(128),
            units(64),
            units(64),
            pltpu.VMEM((4, 8, 16, 128), BF16),
            pltpu.VMEM((4, 8, 16, 128), BF16),
            units(16),
            pltpu.VMEM((4, 2, 16, 128), BF16),
            pltpu.VMEM((4, 2, 16, 128), BF16),
            pltpu.VMEM((8, 4, 16, 128), BF16),
            pltpu.VMEM((2, 8, CH), F32),
            pltpu.VMEM((4, 8, CH), F32),
            pltpu.VMEM((4, 8, CH), F32),
            pltpu.VMEM((8, 8, CH), F32),
            pltpu.VMEM((8, CH), F32),
            sem((6,)),
            sem((8,)),
            sem((16, 4)),
            sem((16, 4)),
            sem((3, 8)),
            sem((3, 8)),
            sem((2,)),
            sem((2, 4)),
            sem((2, 4)),
            sem((8,)),
            sem((8,)),
            sem((11,)),
            sem((4,)),
        ],
        compiler_params=pltpu.CompilerParams(
            collective_id=0, has_side_effects=True, vmem_limit_bytes=60 * 1024 * 1024
        ),
    )(
        morton_target.reshape(8, 128),
        morton_source.reshape(8, 128),
        counts.reshape(1, WINDOW),
        gain_one.reshape(1, CH),
        gain_two.reshape(1, CH),
        features,
        cotangent,
        w_qkv,
        w_proj,
        w_up,
        w_down,
    )
    shapes = (
        ((ROWS, CH), BF16),
        ((CH, 3 * CH), F32),
        ((CH, CH), F32),
        ((CH, FFN), F32),
        ((FFN, CH), F32),
    )
    out = pl.pallas_call(
        functools.partial(finish, grad_scale),
        out_shape=tuple(jax.ShapeDtypeStruct(*shape) for shape in shapes)
        + (jax.ShapeDtypeStruct((1, CH), F32),) * 2,
        in_specs=[hbm] * 5,
        out_specs=[anywhere] * 5 + [vmem] * 2,
        scratch_shapes=[
            units(256),
            units(128),
            units(n_pts),
            rows(8, F32),
            pltpu.VMEM((8, CH), F32),
        ]
        + [pltpu.VMEM(*shape) for shape in shapes]
        + [sem((6,)), sem((5,))],
        compiler_params=pltpu.CompilerParams(vmem_limit_bytes=60 * 1024 * 1024),
    )(*parts)
    dx, grad_qkv, grad_proj, grad_up, grad_down, gain_one_grad, gain_two_grad = out
    return (
        dx,
        grad_qkv,
        grad_proj,
        grad_up,
        grad_down,
        gain_one_grad.reshape(CH),
        gain_two_grad.reshape(CH),
    )


def solution(mesh):
    placed = (
        P(("pts", "quad"), None),
        P(("pts", "quad"), None),
        P(("pts", "quad")),
        P(("pts", "quad")),
        P(("pts", "quad")),
        P(),
        P(),
        P(),
        P(),
        P(),
        P(),
    )
    return jax.shard_map(
        shards,
        mesh=mesh,
        in_specs=placed,
        out_specs=(P(("pts", "quad"), None), P(), P(), P(), P(), P(), P()),
        check_vma=False,
    )
```

```python
import functools
import math

import jax
import jax.numpy as jnp
from jax import lax
from jax.experimental import pallas as pl
from jax.experimental.pallas import tpu as pltpu
from jax.sharding import PartitionSpec as P

HEADS = 8
WINDOW = 32
DILATION = 4
ROWS = 1024
CH = 256
FFN = 1024
HD = 32
BLK = 128
TILE = 256
SHARE = 8
NEG_FILL = -1e30
SCALE = 1.0 / math.sqrt(HD)

F32 = jnp.float32
BF16 = jnp.bfloat16
MESH = pl.DeviceIdType.MESH

NY, NZ, NX, NC = 4, 8, 4, 2


def nn(a, b):
    return lax.dot_general(a, b, (((1,), (0,)), ((), ())), preferred_element_type=F32)


def nt(a, b):
    return lax.dot_general(a, b, (((1,), (1,)), ((), ())), preferred_element_type=F32)


def tn(a, b):
    return lax.dot_general(a, b, (((0,), (0,)), ((), ())), preferred_element_type=F32)


def loop(start, stop, body, unroll=1):
    def step(i, carry):
        for k in range(unroll):
            body(i * unroll + k)
        return carry

    lax.fori_loop(start // unroll, stop // unroll, step, 0)


def transposed(a):
    return jnp.transpose(a.astype(F32)).astype(a.dtype)


def tile_at(i, size):
    return pl.ds(pl.multiple_of(i * size, size), size)


def norm_rows(values):
    mean = jnp.mean(values, axis=0, keepdims=True)
    centred = values - mean
    inverse = lax.rsqrt(jnp.mean(centred * centred, axis=0, keepdims=True) + 1e-05)
    return centred * inverse, inverse


def norm_back_rows(grad, normed, inverse):
    first = jnp.mean(grad, axis=0, keepdims=True)
    second = jnp.mean(grad * normed, axis=0, keepdims=True)
    return inverse * (grad - first - normed * second)


def pack_windows(dense, window_of_lane):
    packed = dense[3 * WINDOW :]
    for k in (2, 1, 0):
        packed = jnp.where(window_of_lane == k, dense[k * WINDOW : (k + 1) * WINDOW], packed)
    return packed


def spread_windows(packed, diagonal):
    return jnp.concatenate([packed] * DILATION, axis=0) * diagonal


def to_units(y):
    n = y.shape[0] // SHARE
    left = y[:, :128].reshape(n, SHARE, 128)
    right = y[:, 128:].reshape(n, SHARE, 128)
    return jnp.concatenate([left, right], axis=1).astype(BF16)


def from_units(u):
    r = u.astype(F32)
    n = r.shape[0]
    left = r[:, :SHARE, :].reshape(n * SHARE, 128)
    right = r[:, SHARE:, :].reshape(n * SHARE, 128)
    return left, right


def head_columns(t):
    blocks = []
    for h in range(HEADS):
        own = t[h * HD : (h + 1) * HD]
        pieces = [own]
        if h > 0:
            pieces.insert(0, jnp.zeros((h * HD, BLK), t.dtype))
        if h < HEADS - 1:
            pieces.append(jnp.zeros(((HEADS - 1 - h) * HD, BLK), t.dtype))
        blocks.append(jnp.concatenate(pieces, axis=0))
    return jnp.concatenate(blocks, axis=1)


def head_rows(r):
    head = lax.broadcasted_iota(jnp.int32, (1, CH), 1) // HD
    return jnp.concatenate(
        [r * jnp.where(head == h, 1.0, 0.0).astype(r.dtype) for h in range(HEADS)], axis=0
    )


def flip(a):
    return jnp.transpose(a.astype(F32)).astype(BF16)


def kernel(
    n_pts,
    target_hbm,
    source_hbm,
    counts_hbm,
    gain_one_hbm,
    gain_two_hbm,
    x_hbm,
    g_hbm,
    wqkv_hbm,
    wproj_hbm,
    wup_hbm,
    wdown_hbm,
    out1_ref,
    out2_ref,
    outr_ref,
    ranks_ref,
    ogain_ref,
    target_ref,
    source_ref,
    counts_ref,
    gain_one_ref,
    gain_two_ref,
    x_ref,
    g_ref,
    wqkv_ref,
    wproj_ref,
    wup_ref,
    wdown_ref,
    sendx,
    recvx,
    sendg,
    recvg,
    sendr,
    rank_rows,
    rank_cols,
    count_rows,
    gain_cols,
    wqkv_t,
    wproj_t,
    wup_t,
    x_t,
    n1_t,
    h1_t,
    h1_r,
    inv_rows,
    proj_t,
    proj_r,
    w_t,
    att_t,
    n2_t,
    h2_t,
    h2_r,
    act_t,
    dg_t,
    g_t,
    g_r,
    gb_t,
    gm_t,
    gbr_r,
    ga_t,
    ga_r,
    gq_t,
    gkv_r,
    dx_r,
    gg_cols,
    grad1,
    core1,
    cur1,
    ra1,
    rb1,
    mid1,
    rc1,
    rd1,
    zin1,
    rz1,
    grad2,
    core2,
    cur2,
    ra2,
    rb2,
    mid2,
    rc2,
    rd2,
    rz2,
    gcore,
    gx,
    gy,
    gz,
    gsum,
    a2a_sems,
    core_sems,
    four_send,
    four_recv,
    z_send,
    z_recv,
    gcore_sems,
    gfour_send,
    gfour_recv,
    gz_send,
    gz_recv,
    load_sems,
    store_sems,
):
    me = lax.axis_index("pts")
    quad = lax.axis_index("quad")
    core = lax.rem(me, NC)
    x_hi = lax.rem(me // NC, 2)
    z = lax.rem(me // (2 * NC), NZ)
    y = me // (2 * NC * NZ)
    x = x_hi * 2 + quad

    def core_dev():
        return {"pts": me + 1 - 2 * core, "quad": quad}

    def x_dev(other):
        return {"pts": me + (other // 2 - x_hi) * NC, "quad": lax.rem(other, 2)}

    def y_dev(other):
        return {"pts": me + (other - y) * (2 * NC * NZ), "quad": quad}

    def z_dev(other):
        return {"pts": me + (other - z) * (2 * NC), "quad": quad}

    loads = [
        pltpu.make_async_copy(src, dst, load_sems.at[k])
        for k, (src, dst) in enumerate(
            (
                (target_hbm, target_ref),
                (source_hbm, source_ref),
                (counts_hbm, counts_ref),
                (gain_one_hbm, gain_one_ref),
                (gain_two_hbm, gain_two_ref),
                (x_hbm, x_ref),
                (g_hbm, g_ref),
                (wqkv_hbm, wqkv_ref),
                (wproj_hbm, wproj_ref),
                (wup_hbm, wup_ref),
                (wdown_hbm, wdown_ref),
            )
        )
    ]
    for load in loads:
        load.start()

    barrier = pltpu.get_barrier_semaphore()

    def greet(k):
        pl.semaphore_signal(
            barrier, inc=1, device_id={"pts": lax.rem(me + k, n_pts), "quad": quad}, device_id_type=MESH
        )

    loop(1, n_pts, greet)
    for hi in range(2):
        pl.semaphore_signal(
            barrier,
            inc=1,
            device_id={"pts": me + (hi - x_hi) * NC, "quad": 1 - quad},
            device_id_type=MESH,
        )

    for load in loads[:5]:
        load.wait()

    def one_row(a):
        return jnp.concatenate([a[r : r + 1, :] for r in range(8)], axis=1)

    stored = lax.broadcasted_iota(jnp.int32, (8, 128), 0) * 128 + lax.broadcasted_iota(
        jnp.int32, (8, 128), 1
    )
    target_key = one_row(((target_ref[...] >> 11) * ROWS + stored).astype(F32))
    to_lane = lax.broadcasted_iota(jnp.int32, (BLK, BLK), 1)
    from_lane = lax.broadcasted_iota(jnp.int32, (BLK, BLK), 0)
    moved = jnp.where(
        from_lane == lax.rem(to_lane, WINDOW) * DILATION + to_lane // WINDOW, 1.0, 0.0
    ).astype(BF16)
    src = source_ref[...]
    digits = jnp.concatenate([src & 63, (src >> 6) & 63, src >> 12], axis=0)
    digits = nn(digits.astype(F32).astype(BF16), moved)
    source_key = one_row(digits[0:8] + 64.0 * digits[8:16] + 4096.0 * digits[16:24])
    spread = jnp.where(
        lax.broadcasted_iota(jnp.int32, (WINDOW, ROWS), 1) // WINDOW
        == lax.broadcasted_iota(jnp.int32, (WINDOW, ROWS), 0),
        1.0,
        0.0,
    ).astype(BF16)
    wide_counts = jnp.broadcast_to(counts_ref[...].astype(F32), (8, WINDOW)).astype(BF16)
    count_rows[...] = nn(wide_counts, spread)
    pad = jnp.zeros((6, ROWS), F32)
    rank_rows[...] = jnp.concatenate([target_key, source_key, pad], axis=0)
    rank_cols[...] = jnp.transpose(rank_rows[...])

    keys = rank_rows[...]

    def count(i, carry):
        t, s = carry
        cols = rank_cols[tile_at(i, 64), :]
        t = t + jnp.sum(jnp.where(cols[:, 0:1] < keys[0:1, :], 1.0, 0.0), axis=0, keepdims=True)
        s = s + jnp.sum(jnp.where(cols[:, 1:2] < keys[1:2, :], 1.0, 0.0), axis=0, keepdims=True)
        return t, s

    zero_row = jnp.zeros((1, ROWS), F32)
    rank_target, rank_source = lax.fori_loop(0, ROWS // 64, count, (zero_row, zero_row))
    rank_rows[...] = jnp.concatenate([rank_target, rank_source, pad], axis=0)
    rank_cols[...] = jnp.transpose(rank_rows[...])

    def select_rows(first, size, ranks):
        slot = lax.broadcasted_iota(jnp.int32, (size, ranks.shape[1]), 0).astype(F32)
        return jnp.where(slot + first == ranks, 1.0, 0.0).astype(BF16)

    def place(i, source_ref, out):
        pick = select_rows((i * TILE).astype(F32), TILE, rank_rows[0:1, :])
        out[tile_at(i, TILE // SHARE)] = to_units(nn(pick, source_ref[...]))

    def a2a(send, recv, index, k):
        peer = lax.rem(me + k, n_pts)
        return pltpu.make_async_remote_copy(
            src_ref=send.at[peer],
            dst_ref=recv.at[me],
            send_sem=a2a_sems.at[index],
            recv_sem=a2a_sems.at[index + 1],
            device_id={"pts": peer, "quad": quad},
            device_id_type=MESH,
        )

    def a2a_some(send, recv, index, first, stop):
        loop(first, stop, lambda j: a2a(send, recv, index, 1 + lax.rem((j - 1) * 37, n_pts - 1)).start())

    def a2a_own(send, recv, index):
        pltpu.make_async_copy(send.at[me], recv.at[me], a2a_sems.at[index + 1]).start()

    def a2a_start(send, recv, index):
        a2a_own(send, recv, index)
        a2a_some(send, recv, index, 1, n_pts)

    def a2a_wait_recv(recv, index):
        pltpu.make_async_copy(recv, recv, a2a_sems.at[index + 1]).wait()

    def a2a_wait_send(send, index):
        part = send.at[pl.ds(0, n_pts - 1)]
        pltpu.make_async_copy(part, part, a2a_sems.at[index]).wait()

    keep_ranks = pltpu.make_async_copy(rank_rows, ranks_ref, store_sems.at[2])
    keep_ranks.start()
    tiles = ROWS // TILE
    loads[5].wait()
    loop(0, tiles, lambda i: place(i, x_ref, sendx))
    pl.semaphore_wait(barrier, n_pts + 1)
    a2a_start(sendx, recvx, 0)
    loads[6].wait()
    loop(0, tiles, lambda i: place(i, g_ref, sendg))
    a2a_start(sendg, recvg, 2)

    for load in loads[7:]:
        load.wait()
    wqkv_t[...] = transposed(wqkv_ref[...])
    wproj_t[...] = transposed(wproj_ref[...])
    wup_t[...] = transposed(wup_ref[...])
    gain_cols[...] = jnp.transpose(
        jnp.concatenate([gain_one_ref[...], gain_two_ref[...], jnp.zeros((6, CH), F32)], axis=0)
    )
    gain_one = gain_cols[:, 0:1]
    gain_two = gain_cols[:, 1:2]

    span = HEADS * BLK
    sub = lax.broadcasted_iota(jnp.int32, (WINDOW, span), 0).astype(F32)
    window_of_lane = lax.rem(lax.broadcasted_iota(jnp.int32, (WINDOW, span), 1), BLK) // WINDOW
    diagonal = jnp.where(
        lax.broadcasted_iota(jnp.int32, (BLK, span), 0) // WINDOW
        == lax.rem(lax.broadcasted_iota(jnp.int32, (BLK, span), 1), BLK) // WINDOW,
        1.0,
        0.0,
    ).astype(BF16)

    def live_tile(at, size):
        slot = lax.rem(lax.broadcasted_iota(jnp.int32, (1, size), 1), WINDOW).astype(F32)
        return slot < count_rows[0:1, at]

    def arrive(recv, out, out_rows):
        left, right = from_units(recv[...])
        arrived = jnp.concatenate([left, right], axis=1).astype(BF16)

        def one(i):
            at = tile_at(i, TILE)
            slot = lax.broadcasted_iota(jnp.int32, (TILE, ROWS), 1).astype(F32)
            pick = jnp.where(rank_cols[at, 1:2] == slot, 1.0, 0.0).astype(BF16)
            points = nn(pick, arrived)
            out[:, at] = jnp.transpose(points).astype(BF16)
            if out_rows is not None:
                out_rows[at, :] = points.astype(BF16)

        loop(0, tiles, one, 4)

    a2a_wait_recv(recvx, 0)
    arrive(recvx, x_t, None)

    def first_norm(i):
        at = tile_at(i, TILE)
        normed, inverse = norm_rows(x_t[:, at].astype(F32))
        n1_t[:, at] = normed
        inv_rows[0:1, at] = inverse
        scaled = normed * gain_one
        hidden = scaled.astype(BF16)
        hidden_rows = jnp.transpose(scaled).astype(BF16)
        h1_t[:, at] = hidden
        h1_r[at, :] = hidden_rows
        proj_t[:, at] = nn(wqkv_t[...], hidden).astype(BF16)
        proj_r[at, :] = nn(hidden_rows, wqkv_ref[...]).astype(BF16)

    loop(0, tiles, first_norm, 4)

    def attend(b):
        at = tile_at(b, BLK)
        counted = jnp.concatenate([count_rows[0:1, at]] * HEADS, axis=1)
        dense = nn(proj_r[at, CH : 2 * CH], head_columns(proj_t[0:CH, at]))
        scores = pack_windows(dense, window_of_lane) * SCALE
        scores = jnp.where(sub < counted, scores, NEG_FILL)
        powered = jnp.exp(scores - jnp.max(scores, axis=0, keepdims=True))
        weights = powered / jnp.sum(powered, axis=0, keepdims=True)
        w_t[b] = weights
        wide = spread_windows(weights.astype(BF16), diagonal)
        for h in range(HEADS):
            v = proj_t[2 * CH + h * HD : 2 * CH + (h + 1) * HD, at]
            att_t[h * HD : (h + 1) * HD, at] = nn(v, wide[:, h * BLK : (h + 1) * BLK]).astype(BF16)

    loop(0, ROWS // BLK, attend, 8)

    def forward_mlp(i):
        at = tile_at(i, TILE)
        branch = nn(wproj_t[...], att_t[:, at])
        mixed = x_t[:, at].astype(F32) + jnp.where(live_tile(at, TILE), branch, 0.0)
        normed, inverse = norm_rows(mixed.astype(BF16).astype(F32))
        n2_t[:, at] = normed
        inv_rows[1:2, at] = inverse
        scaled = normed * gain_two
        hidden = scaled.astype(BF16)
        h2_t[:, at] = hidden
        h2_r[at, :] = jnp.transpose(scaled).astype(BF16)
        for f in range(FFN // TILE):
            rows = pl.ds(f * TILE, TILE)
            before = nn(wup_t[rows, :], hidden)
            cumulative = 0.5 * (1.0 + lax.erf(before * 0.7071067811865476))
            act_t[rows, at] = (before * cumulative).astype(BF16)
            density = jnp.exp(-0.5 * before * before) * 0.3989422804014327
            dg_t[rows, at] = cumulative + before * density

    loop(0, tiles, forward_mlp)

    a2a_wait_recv(recvg, 2)
    arrive(recvg, g_t, g_r)

    def back_act(i):
        at = tile_at(i, TILE)
        for f in range(FFN // TILE):
            rows = pl.ds(f * TILE, TILE)
            gb_t[rows, at] = (nn(wdown_ref[rows, :], g_t[:, at]) * dg_t[rows, at]).astype(BF16)

    loop(0, tiles, back_act, 4)

    def tiles_of(y, lanes):
        return [y[:, l * 128 : (l + 1) * 128].reshape(16, 16, 128).astype(BF16) for l in range(lanes)]

    def up_down(f):
        rows = tile_at(f, TILE)
        for l, u in enumerate(tiles_of(nn(act_t[rows, :], g_r[...]), 2)):
            grad1[pl.ds(128 + f * 32 + l * 16, 16)] = u
        for l, u in enumerate(tiles_of(nn(gb_t[rows, :], h2_r[...]), 2)):
            grad1[pl.ds(f * 32 + l * 16, 16)] = u

    loop(0, FFN // TILE, up_down, 4)

    def four_copies(src, dst_of, which, mine, dev, sem_base):
        copies = []
        for d in range(1, 4):
            other = lax.rem(mine + d, 4)
            copies.append(
                pltpu.make_async_remote_copy(
                    src_ref=src(other),
                    dst_ref=dst_of,
                    send_sem=four_send.at[sem_base + which, d],
                    recv_sem=four_recv.at[sem_base + which, mine],
                    device_id=dev(other),
                    device_id_type=MESH,
                )
            )
        return copies

    def four_wait(src, dst, which, mine, dev, sem_base):
        for d in range(1, 4):
            other = lax.rem(mine + d, 4)
            got = pltpu.make_async_remote_copy(
                src_ref=src(other),
                dst_ref=dst(other),
                send_sem=four_send.at[sem_base + which, d],
                recv_sem=four_recv.at[sem_base + which, other],
                device_id=dev(other),
                device_id_type=MESH,
            )
            got.wait_recv()
            got.wait_send()

    def group(index, grad, from_core, cur, ra, rb, mid, rc, rd, nk):
        half = nk * 32
        part = half // 2
        quarter = part // 4
        base = index * 4
        cbase = index * 4

        def core_copy(src, dst, sem):
            return pltpu.make_async_remote_copy(
                src_ref=src,
                dst_ref=dst,
                send_sem=core_sems.at[cbase + sem],
                recv_sem=core_sems.at[cbase + sem + 1],
                device_id=core_dev(),
                device_id_type=MESH,
            )

        def first_core():
            return core_copy(grad.at[pl.ds((1 - core) * half, half)], from_core, 0)

        def s0():
            first_core().start()

        def cur_a(o):
            return cur.at[pl.ds(o * quarter, quarter)]

        def cur_b(o):
            return cur.at[pl.ds(part + o * quarter, quarter)]

        def s1():
            first_core().wait()
            total = grad[pl.ds(core * half, half)].astype(F32) + from_core[...].astype(F32)
            cur[...] = total.astype(BF16)
            for c in four_copies(cur_a, ra.at[x], 0, x, x_dev, base):
                c.start()
            for c in four_copies(cur_b, rb.at[y], 1, y, y_dev, base):
                c.start()

        def mid_a(o):
            return mid.at[pl.ds(o * nk, nk)]

        def mid_b(o):
            return mid.at[pl.ds(quarter + o * nk, nk)]

        def add_four(own, slots, mine):
            total = own.astype(F32)
            for d in range(1, 4):
                total = total + slots[lax.rem(mine + d, 4)].astype(F32)
            return total.astype(BF16)

        def s2():
            four_wait(cur_a, lambda o: ra.at[o], 0, x, x_dev, base)
            four_wait(cur_b, lambda o: rb.at[o], 1, y, y_dev, base)
            mid[pl.ds(0, quarter)] = add_four(cur[pl.ds(x * quarter, quarter)], ra, x)
            mid[pl.ds(quarter, quarter)] = add_four(cur[pl.ds(part + y * quarter, quarter)], rb, y)
            for c in four_copies(mid_a, rc.at[y], 2, y, y_dev, base):
                c.start()
            for c in four_copies(mid_b, rd.at[x], 3, x, x_dev, base):
                c.start()

        def s3():
            four_wait(mid_a, lambda o: rc.at[o], 2, y, y_dev, base)
            four_wait(mid_b, lambda o: rd.at[o], 3, x, x_dev, base)
            a = add_four(mid[pl.ds(y * nk, nk)], rc, y)
            b = add_four(mid[pl.ds(quarter + x * nk, nk)], rd, x)
            return a, b

        mine = core * half

        def out_a(xx, yy):
            return grad.at[pl.ds(mine + xx * quarter + yy * nk, nk)]

        def out_b(xx, yy):
            return grad.at[pl.ds(mine + part + yy * quarter + xx * nk, nk)]

        def whole_a(xx):
            return grad.at[pl.ds(mine + xx * quarter, quarter)]

        def whole_b(yy):
            return grad.at[pl.ds(mine + part + yy * quarter, quarter)]

        gbase = 8 + index * 4

        def s5():
            for c in four_copies(lambda o: out_a(x, y), out_a(x, y), 0, y, y_dev, gbase):
                c.start()
            for c in four_copies(lambda o: out_b(x, y), out_b(x, y), 1, x, x_dev, gbase):
                c.start()

        def s6():
            four_wait(lambda o: out_a(x, y), lambda o: out_a(x, o), 0, y, y_dev, gbase)
            four_wait(lambda o: out_b(x, y), lambda o: out_b(o, y), 1, x, x_dev, gbase)
            for c in four_copies(lambda o: whole_a(x), whole_a(x), 2, x, x_dev, gbase):
                c.start()
            for c in four_copies(lambda o: whole_b(y), whole_b(y), 3, y, y_dev, gbase):
                c.start()

        def last_core():
            at = grad.at[pl.ds(mine, half)]
            return core_copy(at, at, 2)

        def s7():
            four_wait(lambda o: whole_a(x), lambda o: whole_a(o), 2, x, x_dev, gbase)
            four_wait(lambda o: whole_b(y), lambda o: whole_b(o), 3, y, y_dev, gbase)
            last_core().start()

        def s8():
            last_core().wait()

        def put(a, b):
            grad[pl.ds(mine + x * quarter + y * nk, nk)] = a
            grad[pl.ds(mine + part + y * quarter + x * nk, nk)] = b

        return s0, s1, s2, s3, put, s5, s6, s7, s8

    def z_copy(src, dst, sems, d, slot):
        other = lax.rem(z + d, NZ)
        return pltpu.make_async_remote_copy(
            src_ref=src,
            dst_ref=dst,
            send_sem=z_send.at[sems, d],
            recv_sem=z_recv.at[sems, slot],
            device_id=z_dev(other),
            device_id_type=MESH,
        )

    one = group(0, grad1, core1, cur1, ra1, rb1, mid1, rc1, rd1, 4)
    two = group(1, grad2, core2, cur2, ra2, rb2, mid2, rc2, rd2, 2)

    def one_s3():
        a, b = one[3]()
        zin1[0:4] = a
        zin1[4:8] = b
        for d in range(1, NZ):
            z_copy(zin1.at[lax.rem(z + d, NZ)], rz1.at[z], 0, d, z).start()

    def one_out(zz):
        p = zz // 4
        k = lax.rem(zz, 4)
        first = x + p * (y - x)
        second = y + p * (x - y)
        return core * 128 + p * 64 + first * 16 + second * 4 + k

    def one_s4():
        total = zin1[z].astype(F32)
        for d in range(1, NZ):
            other = lax.rem(z + d, NZ)
            got = z_copy(zin1.at[other], rz1.at[other], 0, d, other)
            got.wait_recv()
            got.wait_send()
            total = total + rz1[other].astype(F32)
        grad1[one_out(z)] = total.astype(BF16)
        for d in range(1, NZ):
            z_copy(grad1.at[one_out(z)], grad1.at[one_out(z)], 1, d, z).start()

    def one_s5():
        for d in range(1, NZ):
            other = lax.rem(z + d, NZ)
            got = z_copy(grad1.at[one_out(z)], grad1.at[one_out(other)], 1, d, other)
            got.wait_recv()
            got.wait_send()
        one[5]()

    def two_s3():
        a, b = two[3]()
        rz2[z, 0:2] = a
        rz2[z, 2:4] = b
        for d in range(1, NZ):
            z_copy(rz2.at[z], rz2.at[z], 2, d, z).start()

    def two_s5():
        for d in range(1, NZ):
            other = lax.rem(z + d, NZ)
            got = z_copy(rz2.at[z], rz2.at[other], 2, d, other)
            got.wait_recv()
            got.wait_send()
        total = rz2[0].astype(F32)
        for k in range(1, NZ):
            total = total + rz2[k].astype(F32)
        total = total.astype(BF16)
        two[4](total[0:2], total[2:4])
        two[5]()

    def gain_copies(buf, count, mine, dev, send_sem, recv_sem, wait):
        for d in range(1, count):
            other = lax.rem(mine + d, count)
            c = pltpu.make_async_remote_copy(
                src_ref=buf.at[mine],
                dst_ref=buf.at[other] if wait else buf.at[mine],
                send_sem=send_sem(d),
                recv_sem=recv_sem(other) if wait else recv_sem(mine),
                device_id=dev(other),
                device_id_type=MESH,
            )
            if wait:
                c.wait_recv()
                c.wait_send()
            else:
                c.start()

    def add_slots(buf, count):
        total = buf[0]
        for k in range(1, count):
            total = total + buf[k]
        return total

    gain_steps = (
        (gcore, NC, core, lambda o: core_dev(), lambda d: gcore_sems.at[0], lambda o: gcore_sems.at[1]),
        (gx, NX, x, x_dev, lambda d: gfour_send.at[0, d], lambda o: gfour_recv.at[0, o]),
        (gy, NY, y, y_dev, lambda d: gfour_send.at[1, d], lambda o: gfour_recv.at[1, o]),
        (gz, NZ, z, z_dev, lambda d: gz_send.at[d], lambda o: gz_recv.at[o]),
    )

    def gain_start(step, values):
        buf, count, mine, dev, ssem, rsem = gain_steps[step]
        buf[mine] = values
        gain_copies(buf, count, mine, dev, ssem, rsem, False)

    def gain_wait(step):
        buf, count, mine, dev, ssem, rsem = gain_steps[step]
        gain_copies(buf, count, mine, dev, ssem, rsem, True)
        return add_slots(buf, count)

    one[0]()

    gg_cols[...] = jnp.zeros_like(gg_cols)

    def back_norm_two(i):
        at = tile_at(i, TILE)
        grad = nn(wup_ref[...], gb_t[:, at])
        normed = n2_t[:, at]
        gg_cols[:, 1:2] += jnp.sum(grad * normed, axis=1, keepdims=True)
        back = norm_back_rows(grad * gain_two, normed, inv_rows[1:2, at])
        mixed = (g_t[:, at].astype(F32) + back).astype(BF16)
        gm_t[:, at] = mixed
        kept = jnp.where(live_tile(at, TILE), mixed.astype(F32), 0.0)
        kept_rows = jnp.transpose(kept).astype(BF16)
        gbr_r[at, :] = kept_rows
        ga_t[:, at] = nn(wproj_ref[...], kept.astype(BF16)).astype(BF16)
        ga_r[at, :] = nn(kept_rows, wproj_t[...]).astype(BF16)

    loop(0, tiles, back_norm_two, 4)
    one[1]()
    for l, u in enumerate(tiles_of(nn(att_t[...], gbr_r[...]), 2)):
        grad2[96 + l * 16 : 112 + l * 16] = u


    def back_attend(b):
        at = tile_at(b, BLK)
        weights = w_t[b]
        wide = spread_windows(weights.astype(BF16), diagonal)
        gkv_r[at, CH : 2 * CH] = nn(wide, head_rows(ga_r[at, :])).astype(BF16)
        dense = nn(proj_r[at, 2 * CH : 3 * CH], head_columns(ga_t[:, at]))
        grad_w = pack_windows(dense, window_of_lane)
        inner = jnp.sum(weights * grad_w, axis=0, keepdims=True)
        grad_s = (weights * (grad_w - inner) * SCALE).astype(BF16)
        wide_s = spread_windows(grad_s, diagonal)
        gkv_r[at, 0:CH] = nn(wide_s, head_rows(proj_r[at, 0:CH])).astype(BF16)
        for h in range(HEADS):
            k = proj_t[CH + h * HD : CH + (h + 1) * HD, at]
            gq_t[h * HD : (h + 1) * HD, at] = nn(k, wide_s[:, h * BLK : (h + 1) * BLK]).astype(BF16)

    loop(0, ROWS // BLK, back_attend, 8)

    for l, u in enumerate(tiles_of(nn(gq_t[...], h1_r[...]), 2)):
        grad2[l * 16 : (l + 1) * 16] = u
    for p in range(2):
        for l, u in enumerate(tiles_of(nn(h1_t[...], gkv_r[:, p * CH : (p + 1) * CH]), 2)):
            grad2[(p + 1) * 32 + l * 16 : (p + 1) * 32 + (l + 1) * 16] = u
    two[0]()
    one[2]()
    two[1]()

    def back_norm_one(i):
        at = tile_at(i, TILE)
        grad = nn(wqkv_ref[:, 0:CH], gq_t[:, at]) + jnp.transpose(
            nn(gkv_r[at, :], wqkv_t[CH : 3 * CH, :])
        )
        normed = n1_t[:, at]
        gg_cols[:, 0:1] += jnp.sum(grad * normed, axis=1, keepdims=True)
        back = norm_back_rows(grad * gain_one, normed, inv_rows[0:1, at])
        dx_r[at, :] = jnp.transpose(gm_t[:, at].astype(F32) + back).astype(BF16)

    loop(0, tiles, back_norm_one, 4)
    gain_start(0, jnp.transpose(gg_cols[...]))

    def give_back(i):
        pick = select_rows((i * TILE).astype(F32), TILE, rank_rows[1:2, :])
        sendr[tile_at(i, TILE // SHARE)] = to_units(nn(pick, dx_r[...]))

    loop(0, tiles, give_back, 4)
    stores = [
        pltpu.make_async_copy(src, dst, store_sems.at[k])
        for k, (src, dst) in enumerate(
            ((grad1, out1_ref), (grad2, out2_ref))
        )
    ]
    a2a_own(sendr, outr_ref, 4)
    cuts = (1, 26, 52, 78, 104)
    a2a_some(sendr, outr_ref, 4, cuts[0], cuts[1])
    gain_start(1, gain_wait(0))
    two[2]()
    one_s3()
    a2a_some(sendr, outr_ref, 4, cuts[1], cuts[2])
    two_s3()
    gain_start(2, gain_wait(1))
    one_s4()
    a2a_some(sendr, outr_ref, 4, cuts[2], cuts[3])
    two_s5()
    gain_start(3, gain_wait(2))
    one_s5()
    a2a_some(sendr, outr_ref, 4, cuts[3], cuts[4])
    two[6]()
    one[6]()
    a2a_some(sendr, outr_ref, 4, cuts[4], n_pts)
    two[7]()
    one[7]()
    one[8]()
    stores[0].start()
    gsum[...] = gain_wait(3)
    keep_gains = pltpu.make_async_copy(gsum, ogain_ref, store_sems.at[3])
    keep_gains.start()
    two[8]()
    stores[1].start()
    a2a_wait_recv(outr_ref, 4)
    a2a_wait_send(sendx, 0)
    a2a_wait_send(sendg, 2)
    a2a_wait_send(sendr, 4)
    for store in stores:
        store.wait()
    keep_ranks.wait()
    keep_gains.wait()


def finish(
    grad_scale,
    u1_hbm,
    u2_hbm,
    ur_hbm,
    ranks_hbm,
    gains_hbm,
    dx_hbm,
    qkv_hbm,
    proj_hbm,
    up_hbm,
    down_hbm,
    gain_one_ref,
    gain_two_ref,
    u1_ref,
    u2_ref,
    ur_ref,
    ranks_ref,
    gains_ref,
    dx_ref,
    oqkv_ref,
    oproj_ref,
    oup_ref,
    odown_ref,
    load_sems,
    sems,
):
    half = 128
    pairs = (
        (u1_hbm.at[pl.ds(half, half)], u1_ref.at[pl.ds(half, half)]),
        (ur_hbm, ur_ref),
        (ranks_hbm, ranks_ref),
        (u1_hbm.at[pl.ds(0, half)], u1_ref.at[pl.ds(0, half)]),
        (u2_hbm, u2_ref),
        (gains_hbm, gains_ref),
    )
    loads = [pltpu.make_async_copy(a, b, load_sems.at[k]) for k, (a, b) in enumerate(pairs)]
    for load in loads:
        load.start()
    stores = [
        pltpu.make_async_copy(src, dst, sems.at[k])
        for k, (src, dst) in enumerate(
            (
                (oup_ref, up_hbm),
                (odown_ref, down_hbm),
                (oqkv_ref, qkv_hbm),
                (oproj_ref, proj_hbm),
                (dx_ref, dx_hbm),
            )
        )
    ]

    def block(ref, first):
        left = ref[first : first + 16].reshape(TILE, 128).astype(F32)
        right = ref[first + 16 : first + 32].reshape(TILE, 128).astype(F32)
        return jnp.concatenate([left, right], axis=1) * grad_scale

    loads[0].wait()
    for f in range(FFN // TILE):
        odown_ref[f * TILE : (f + 1) * TILE, :] = block(u1_ref, 128 + f * 32)
    stores[1].start()
    loads[1].wait()
    loads[2].wait()
    left, right = from_units(ur_ref[...])
    arrived = jnp.concatenate([left, right], axis=1).astype(BF16)
    ranks = jnp.transpose(ranks_ref[...])
    for i in range(ROWS // TILE):
        slot = lax.broadcasted_iota(jnp.int32, (TILE, ROWS), 1).astype(F32)
        pick = jnp.where(ranks[i * TILE : (i + 1) * TILE, 0:1] == slot, 1.0, 0.0).astype(BF16)
        dx_ref[i * TILE : (i + 1) * TILE, :] = nn(pick, arrived).astype(BF16)
    stores[4].start()
    loads[3].wait()
    for f in range(FFN // TILE):
        at = slice(f * TILE, (f + 1) * TILE)
        oup_ref[:, at] = jnp.transpose(block(u1_ref, f * 32))
    stores[0].start()
    loads[4].wait()
    oqkv_ref[:, 0:CH] = jnp.transpose(block(u2_ref, 0))
    oqkv_ref[:, CH : 2 * CH] = block(u2_ref, 32)
    oqkv_ref[:, 2 * CH : 3 * CH] = block(u2_ref, 64)
    stores[2].start()
    oproj_ref[...] = block(u2_ref, 96)
    stores[3].start()
    loads[5].wait()
    gain_one_ref[...] = gains_ref[0:1, :] * grad_scale
    gain_two_ref[...] = gains_ref[1:2, :] * grad_scale
    for store in stores:
        store.wait()


def units(n):
    return pltpu.VMEM((n, 16, 128), BF16)


def shards(
    features,
    cotangent,
    morton_target,
    morton_source,
    counts,
    w_qkv,
    w_proj,
    w_up,
    w_down,
    gain_one,
    gain_two,
):
    n_pts = lax.axis_size("pts")
    grad_scale = 1.0 / math.sqrt(features.shape[0] * n_pts * lax.axis_size("quad"))
    rows = lambda n, kind: pltpu.VMEM((n, ROWS), kind)
    wide = lambda n: pltpu.VMEM((ROWS, n), BF16)
    sem = pltpu.SemaphoreType.DMA
    vmem = pl.BlockSpec(memory_space=pltpu.VMEM)
    anywhere = pl.BlockSpec(memory_space=pl.ANY)
    hbm = pl.BlockSpec(memory_space=pltpu.HBM)
    parts = pl.pallas_call(
        functools.partial(kernel, n_pts),
        out_shape=(
            jax.ShapeDtypeStruct((256, 16, 128), BF16),
            jax.ShapeDtypeStruct((128, 16, 128), BF16),
            jax.ShapeDtypeStruct((n_pts, 16, 128), BF16),
            jax.ShapeDtypeStruct((8, ROWS), F32),
            jax.ShapeDtypeStruct((8, CH), F32),
        ),
        in_specs=[hbm] * 11,
        out_specs=[anywhere] * 5,
        scratch_shapes=[
            pltpu.VMEM((8, 128), jnp.int32),
            pltpu.VMEM((8, 128), jnp.int32),
            pltpu.VMEM((1, WINDOW), jnp.int32),
            pltpu.VMEM((1, CH), F32),
            pltpu.VMEM((1, CH), F32),
            wide(CH),
            wide(CH),
            pltpu.VMEM((CH, 3 * CH), BF16),
            pltpu.VMEM((CH, CH), BF16),
            pltpu.VMEM((CH, FFN), BF16),
            pltpu.VMEM((FFN, CH), BF16),
        ]
        + [units(n_pts)] * 5
        + [
            rows(8, F32),
            pltpu.VMEM((ROWS, 8), F32),
            rows(8, F32),
            pltpu.VMEM((CH, 8), F32),
            pltpu.VMEM((3 * CH, CH), BF16),
            pltpu.VMEM((CH, CH), BF16),
            pltpu.VMEM((FFN, CH), BF16),
            rows(CH, BF16),
            rows(CH, F32),
            rows(CH, BF16),
            wide(CH),
            rows(8, F32),
            rows(3 * CH, BF16),
            wide(3 * CH),
            pltpu.VMEM((ROWS // BLK, WINDOW, HEADS * BLK), F32),
            rows(CH, BF16),
            rows(CH, F32),
            rows(CH, BF16),
            wide(CH),
            rows(FFN, BF16),
            rows(FFN, F32),
            rows(CH, BF16),
            wide(CH),
            rows(FFN, BF16),
            rows(CH, BF16),
            wide(CH),
            rows(CH, BF16),
            wide(CH),
            rows(CH, BF16),
            wide(2 * CH),
            wide(CH),
            pltpu.VMEM((CH, 8), F32),
            units(256),
            units(128),
            units(128),
            pltpu.VMEM((4, 16, 16, 128), BF16),
            pltpu.VMEM((4, 16, 16, 128), BF16),
            units(32),
            pltpu.VMEM((4, 4, 16, 128), BF16),
            pltpu.VMEM((4, 4, 16, 128), BF16),
            units(8),
            units(8),
            units(128),
            units(64),
            units(64),
            pltpu.VMEM((4, 8, 16, 128), BF16),
            pltpu.VMEM((4, 8, 16, 128), BF16),
            units(16),
            pltpu.VMEM((4, 2, 16, 128), BF16),
            pltpu.VMEM((4, 2, 16, 128), BF16),
            pltpu.VMEM((8, 4, 16, 128), BF16),
            pltpu.VMEM((2, 8, CH), F32),
            pltpu.VMEM((4, 8, CH), F32),
            pltpu.VMEM((4, 8, CH), F32),
            pltpu.VMEM((8, 8, CH), F32),
            pltpu.VMEM((8, CH), F32),
            sem((6,)),
            sem((8,)),
            sem((16, 4)),
            sem((16, 4)),
            sem((3, 8)),
            sem((3, 8)),
            sem((2,)),
            sem((2, 4)),
            sem((2, 4)),
            sem((8,)),
            sem((8,)),
            sem((11,)),
            sem((4,)),
        ],
        compiler_params=pltpu.CompilerParams(
            collective_id=0, has_side_effects=True, vmem_limit_bytes=60 * 1024 * 1024
        ),
    )(
        morton_target.reshape(8, 128),
        morton_source.reshape(8, 128),
        counts.reshape(1, WINDOW),
        gain_one.reshape(1, CH),
        gain_two.reshape(1, CH),
        features,
        cotangent,
        w_qkv,
        w_proj,
        w_up,
        w_down,
    )
    shapes = (
        ((ROWS, CH), BF16),
        ((CH, 3 * CH), F32),
        ((CH, CH), F32),
        ((CH, FFN), F32),
        ((FFN, CH), F32),
    )
    out = pl.pallas_call(
        functools.partial(finish, grad_scale),
        out_shape=tuple(jax.ShapeDtypeStruct(*shape) for shape in shapes)
        + (jax.ShapeDtypeStruct((1, CH), F32),) * 2,
        in_specs=[hbm] * 5,
        out_specs=[anywhere] * 5 + [vmem] * 2,
        scratch_shapes=[
            units(256),
            units(128),
            units(n_pts),
            rows(8, F32),
            pltpu.VMEM((8, CH), F32),
        ]
        + [pltpu.VMEM(*shape) for shape in shapes]
        + [sem((6,)), sem((5,))],
        compiler_params=pltpu.CompilerParams(vmem_limit_bytes=60 * 1024 * 1024),
    )(*parts)
    dx, grad_qkv, grad_proj, grad_up, grad_down, gain_one_grad, gain_two_grad = out
    return (
        dx,
        grad_qkv,
        grad_proj,
        grad_up,
        grad_down,
        gain_one_grad.reshape(CH),
        gain_two_grad.reshape(CH),
    )


def solution(mesh):
    placed = (
        P(("pts", "quad"), None),
        P(("pts", "quad"), None),
        P(("pts", "quad")),
        P(("pts", "quad")),
        P(("pts", "quad")),
        P(),
        P(),
        P(),
        P(),
        P(),
        P(),
    )
    return jax.shard_map(
        shards,
        mesh=mesh,
        in_specs=placed,
        out_specs=(P(("pts", "quad"), None), P(), P(), P(), P(), P(), P()),
        check_vma=False,
    )
```

```python
import functools
import math

import jax
import jax.numpy as jnp
from jax import lax
from jax.experimental import pallas as pl
from jax.experimental.pallas import tpu as pltpu
from jax.sharding import PartitionSpec as P

HEADS = 8
WINDOW = 32
DILATION = 4
ROWS = 1024
CH = 256
FFN = 1024
HD = 32
BLK = 128
TILE = 256
SHARE = 8
NEG_FILL = -1e30
SCALE = 1.0 / math.sqrt(HD)

F32 = jnp.float32
BF16 = jnp.bfloat16
MESH = pl.DeviceIdType.MESH

NY, NZ, NX, NC = 4, 8, 4, 2


def nn(a, b):
    return lax.dot_general(a, b, (((1,), (0,)), ((), ())), preferred_element_type=F32)


def nt(a, b):
    return lax.dot_general(a, b, (((1,), (1,)), ((), ())), preferred_element_type=F32)


def tn(a, b):
    return lax.dot_general(a, b, (((0,), (0,)), ((), ())), preferred_element_type=F32)


def loop(start, stop, body, unroll=1):
    def step(i, carry):
        for k in range(unroll):
            body(i * unroll + k)
        return carry

    lax.fori_loop(start // unroll, stop // unroll, step, 0)


def transposed(a):
    return jnp.transpose(a.astype(F32)).astype(a.dtype)


def tile_at(i, size):
    return pl.ds(pl.multiple_of(i * size, size), size)


def norm_rows(values):
    mean = jnp.mean(values, axis=0, keepdims=True)
    centred = values - mean
    inverse = lax.rsqrt(jnp.mean(centred * centred, axis=0, keepdims=True) + 1e-05)
    return centred * inverse, inverse


def norm_back_rows(grad, normed, inverse):
    first = jnp.mean(grad, axis=0, keepdims=True)
    second = jnp.mean(grad * normed, axis=0, keepdims=True)
    return inverse * (grad - first - normed * second)


def pack_windows(dense, window_of_lane):
    packed = dense[3 * WINDOW :]
    for k in (2, 1, 0):
        packed = jnp.where(window_of_lane == k, dense[k * WINDOW : (k + 1) * WINDOW], packed)
    return packed


def spread_windows(packed, diagonal):
    return jnp.concatenate([packed] * DILATION, axis=0) * diagonal


def to_units(y):
    n = y.shape[0] // SHARE
    left = y[:, :128].reshape(n, SHARE, 128)
    right = y[:, 128:].reshape(n, SHARE, 128)
    return jnp.concatenate([left, right], axis=1).astype(BF16)


def from_units(u):
    r = u.astype(F32)
    n = r.shape[0]
    left = r[:, :SHARE, :].reshape(n * SHARE, 128)
    right = r[:, SHARE:, :].reshape(n * SHARE, 128)
    return left, right


def head_columns(t):
    blocks = []
    for h in range(HEADS):
        own = t[h * HD : (h + 1) * HD]
        pieces = [own]
        if h > 0:
            pieces.insert(0, jnp.zeros((h * HD, BLK), t.dtype))
        if h < HEADS - 1:
            pieces.append(jnp.zeros(((HEADS - 1 - h) * HD, BLK), t.dtype))
        blocks.append(jnp.concatenate(pieces, axis=0))
    return jnp.concatenate(blocks, axis=1)


def head_rows(r):
    head = lax.broadcasted_iota(jnp.int32, (1, CH), 1) // HD
    return jnp.concatenate(
        [r * jnp.where(head == h, 1.0, 0.0).astype(r.dtype) for h in range(HEADS)], axis=0
    )


def flip(a):
    return jnp.transpose(a.astype(F32)).astype(BF16)


def kernel(
    n_pts,
    target_hbm,
    source_hbm,
    counts_hbm,
    gain_one_hbm,
    gain_two_hbm,
    x_hbm,
    g_hbm,
    wqkv_hbm,
    wproj_hbm,
    wup_hbm,
    wdown_hbm,
    out1_ref,
    out2_ref,
    outr_ref,
    ranks_ref,
    ogain_ref,
    target_ref,
    source_ref,
    counts_ref,
    gain_one_ref,
    gain_two_ref,
    x_ref,
    g_ref,
    wqkv_ref,
    wproj_ref,
    wup_ref,
    wdown_ref,
    sendx,
    recvx,
    sendg,
    recvg,
    sendr,
    rank_rows,
    rank_cols,
    count_rows,
    gain_cols,
    wqkv_t,
    wproj_t,
    wup_t,
    x_t,
    n1_t,
    h1_t,
    h1_r,
    inv_rows,
    proj_t,
    proj_r,
    w_t,
    att_t,
    n2_t,
    h2_t,
    h2_r,
    act_t,
    dg_t,
    g_t,
    g_r,
    gb_t,
    gm_t,
    gbr_r,
    ga_t,
    ga_r,
    gq_t,
    gkv_r,
    dx_r,
    gg_cols,
    grad1,
    core1,
    cur1,
    ra1,
    rb1,
    mid1,
    rc1,
    rd1,
    zin1,
    rz1,
    grad2,
    core2,
    cur2,
    ra2,
    rb2,
    mid2,
    rc2,
    rd2,
    rz2,
    gcore,
    gx,
    gy,
    gz,
    gsum,
    a2a_sems,
    core_sems,
    four_send,
    four_recv,
    z_send,
    z_recv,
    gcore_sems,
    gfour_send,
    gfour_recv,
    gz_send,
    gz_recv,
    load_sems,
    store_sems,
):
    me = lax.axis_index("pts")
    quad = lax.axis_index("quad")
    core = lax.rem(me, NC)
    x_hi = lax.rem(me // NC, 2)
    z = lax.rem(me // (2 * NC), NZ)
    y = me // (2 * NC * NZ)
    x = x_hi * 2 + quad

    def core_dev():
        return {"pts": me + 1 - 2 * core, "quad": quad}

    def x_dev(other):
        return {"pts": me + (other // 2 - x_hi) * NC, "quad": lax.rem(other, 2)}

    def y_dev(other):
        return {"pts": me + (other - y) * (2 * NC * NZ), "quad": quad}

    def z_dev(other):
        return {"pts": me + (other - z) * (2 * NC), "quad": quad}

    loads = [
        pltpu.make_async_copy(src, dst, load_sems.at[k])
        for k, (src, dst) in enumerate(
            (
                (target_hbm, target_ref),
                (source_hbm, source_ref),
                (counts_hbm, counts_ref),
                (gain_one_hbm, gain_one_ref),
                (gain_two_hbm, gain_two_ref),
                (x_hbm, x_ref),
                (g_hbm, g_ref),
                (wqkv_hbm, wqkv_ref),
                (wproj_hbm, wproj_ref),
                (wup_hbm, wup_ref),
                (wdown_hbm, wdown_ref),
            )
        )
    ]
    for load in loads:
        load.start()

    barrier = pltpu.get_barrier_semaphore()

    def greet(k):
        pl.semaphore_signal(
            barrier, inc=1, device_id={"pts": lax.rem(me + k, n_pts), "quad": quad}, device_id_type=MESH
        )

    loop(1, n_pts, greet)
    for hi in range(2):
        pl.semaphore_signal(
            barrier,
            inc=1,
            device_id={"pts": me + (hi - x_hi) * NC, "quad": 1 - quad},
            device_id_type=MESH,
        )

    for load in loads[:5]:
        load.wait()

    def one_row(a):
        return jnp.concatenate([a[r : r + 1, :] for r in range(8)], axis=1)

    stored = lax.broadcasted_iota(jnp.int32, (8, 128), 0) * 128 + lax.broadcasted_iota(
        jnp.int32, (8, 128), 1
    )
    target_key = one_row(((target_ref[...] >> 11) * ROWS + stored).astype(F32))
    to_lane = lax.broadcasted_iota(jnp.int32, (BLK, BLK), 1)
    from_lane = lax.broadcasted_iota(jnp.int32, (BLK, BLK), 0)
    moved = jnp.where(
        from_lane == lax.rem(to_lane, WINDOW) * DILATION + to_lane // WINDOW, 1.0, 0.0
    ).astype(BF16)
    src = source_ref[...]
    digits = jnp.concatenate([src & 63, (src >> 6) & 63, src >> 12], axis=0)
    digits = nn(digits.astype(F32).astype(BF16), moved)
    source_key = one_row(digits[0:8] + 64.0 * digits[8:16] + 4096.0 * digits[16:24])
    spread = jnp.where(
        lax.broadcasted_iota(jnp.int32, (WINDOW, ROWS), 1) // WINDOW
        == lax.broadcasted_iota(jnp.int32, (WINDOW, ROWS), 0),
        1.0,
        0.0,
    ).astype(BF16)
    wide_counts = jnp.broadcast_to(counts_ref[...].astype(F32), (8, WINDOW)).astype(BF16)
    count_rows[...] = nn(wide_counts, spread)
    pad = jnp.zeros((6, ROWS), F32)
    rank_rows[...] = jnp.concatenate([target_key, source_key, pad], axis=0)
    rank_cols[...] = jnp.transpose(rank_rows[...])

    keys = rank_rows[...]

    def count(i, carry):
        t, s = carry
        cols = rank_cols[tile_at(i, 64), :]
        t = t + jnp.sum(jnp.where(cols[:, 0:1] < keys[0:1, :], 1.0, 0.0), axis=0, keepdims=True)
        s = s + jnp.sum(jnp.where(cols[:, 1:2] < keys[1:2, :], 1.0, 0.0), axis=0, keepdims=True)
        return t, s

    zero_row = jnp.zeros((1, ROWS), F32)
    rank_target, rank_source = lax.fori_loop(0, ROWS // 64, count, (zero_row, zero_row))
    rank_rows[...] = jnp.concatenate([rank_target, rank_source, pad], axis=0)
    rank_cols[...] = jnp.transpose(rank_rows[...])

    def select_rows(first, size, ranks):
        slot = lax.broadcasted_iota(jnp.int32, (size, ranks.shape[1]), 0).astype(F32)
        return jnp.where(slot + first == ranks, 1.0, 0.0).astype(BF16)

    def place(i, source_ref, out):
        pick = select_rows((i * TILE).astype(F32), TILE, rank_rows[0:1, :])
        out[tile_at(i, TILE // SHARE)] = to_units(nn(pick, source_ref[...]))

    def a2a(send, recv, index, k):
        peer = lax.rem(me + k, n_pts)
        return pltpu.make_async_remote_copy(
            src_ref=send.at[peer],
            dst_ref=recv.at[me],
            send_sem=a2a_sems.at[index],
            recv_sem=a2a_sems.at[index + 1],
            device_id={"pts": peer, "quad": quad},
            device_id_type=MESH,
        )

    def a2a_some(send, recv, index, first, stop):
        loop(first, stop, lambda j: a2a(send, recv, index, 1 + lax.rem((j - 1) * 37, n_pts - 1)).start())

    def a2a_own(send, recv, index):
        pltpu.make_async_copy(send.at[me], recv.at[me], a2a_sems.at[index + 1]).start()

    def a2a_start(send, recv, index):
        a2a_own(send, recv, index)
        a2a_some(send, recv, index, 1, n_pts)

    def a2a_wait_recv(recv, index):
        pltpu.make_async_copy(recv, recv, a2a_sems.at[index + 1]).wait()

    def a2a_wait_send(send, index):
        part = send.at[pl.ds(0, n_pts - 1)]
        pltpu.make_async_copy(part, part, a2a_sems.at[index]).wait()

    keep_ranks = pltpu.make_async_copy(rank_rows, ranks_ref, store_sems.at[2])
    keep_ranks.start()
    tiles = ROWS // TILE
    loads[5].wait()
    loop(0, tiles, lambda i: place(i, x_ref, sendx))
    pl.semaphore_wait(barrier, n_pts + 1)
    a2a_start(sendx, recvx, 0)
    loads[6].wait()
    loop(0, tiles, lambda i: place(i, g_ref, sendg))
    a2a_start(sendg, recvg, 2)

    for load in loads[7:]:
        load.wait()
    wqkv_t[...] = transposed(wqkv_ref[...])
    wproj_t[...] = transposed(wproj_ref[...])
    wup_t[...] = transposed(wup_ref[...])
    gain_cols[...] = jnp.transpose(
        jnp.concatenate([gain_one_ref[...], gain_two_ref[...], jnp.zeros((6, CH), F32)], axis=0)
    )
    gain_one = gain_cols[:, 0:1]
    gain_two = gain_cols[:, 1:2]

    span = HEADS * BLK
    sub = lax.broadcasted_iota(jnp.int32, (WINDOW, span), 0).astype(F32)
    window_of_lane = lax.rem(lax.broadcasted_iota(jnp.int32, (WINDOW, span), 1), BLK) // WINDOW
    diagonal = jnp.where(
        lax.broadcasted_iota(jnp.int32, (BLK, span), 0) // WINDOW
        == lax.rem(lax.broadcasted_iota(jnp.int32, (BLK, span), 1), BLK) // WINDOW,
        1.0,
        0.0,
    ).astype(BF16)

    def live_tile(at, size):
        slot = lax.rem(lax.broadcasted_iota(jnp.int32, (1, size), 1), WINDOW).astype(F32)
        return slot < count_rows[0:1, at]

    def arrive(recv, out, out_rows):
        left, right = from_units(recv[...])
        arrived = jnp.concatenate([left, right], axis=1).astype(BF16)

        def one(i):
            at = tile_at(i, TILE)
            slot = lax.broadcasted_iota(jnp.int32, (TILE, ROWS), 1).astype(F32)
            pick = jnp.where(rank_cols[at, 1:2] == slot, 1.0, 0.0).astype(BF16)
            points = nn(pick, arrived)
            out[:, at] = jnp.transpose(points).astype(BF16)
            if out_rows is not None:
                out_rows[at, :] = points.astype(BF16)

        loop(0, tiles, one, 4)

    a2a_wait_recv(recvx, 0)
    arrive(recvx, x_t, None)

    def first_norm(i):
        at = tile_at(i, TILE)
        normed, inverse = norm_rows(x_t[:, at].astype(F32))
        n1_t[:, at] = normed
        inv_rows[0:1, at] = inverse
        scaled = normed * gain_one
        hidden = scaled.astype(BF16)
        hidden_rows = jnp.transpose(scaled).astype(BF16)
        h1_t[:, at] = hidden
        h1_r[at, :] = hidden_rows
        proj_t[:, at] = nn(wqkv_t[...], hidden).astype(BF16)
        proj_r[at, :] = nn(hidden_rows, wqkv_ref[...]).astype(BF16)

    loop(0, tiles, first_norm, 4)

    def attend(b):
        at = tile_at(b, BLK)
        counted = jnp.concatenate([count_rows[0:1, at]] * HEADS, axis=1)
        dense = nn(proj_r[at, CH : 2 * CH], head_columns(proj_t[0:CH, at]))
        scores = pack_windows(dense, window_of_lane) * SCALE
        scores = jnp.where(sub < counted, scores, NEG_FILL)
        powered = jnp.exp(scores - jnp.max(scores, axis=0, keepdims=True))
        weights = powered / jnp.sum(powered, axis=0, keepdims=True)
        w_t[b] = weights
        wide = spread_windows(weights.astype(BF16), diagonal)
        for h in range(HEADS):
            v = proj_t[2 * CH + h * HD : 2 * CH + (h + 1) * HD, at]
            att_t[h * HD : (h + 1) * HD, at] = nn(v, wide[:, h * BLK : (h + 1) * BLK]).astype(BF16)

    loop(0, ROWS // BLK, attend, 8)

    def forward_mlp(i):
        at = tile_at(i, TILE)
        branch = nn(wproj_t[...], att_t[:, at])
        mixed = x_t[:, at].astype(F32) + jnp.where(live_tile(at, TILE), branch, 0.0)
        normed, inverse = norm_rows(mixed.astype(BF16).astype(F32))
        n2_t[:, at] = normed
        inv_rows[1:2, at] = inverse
        scaled = normed * gain_two
        hidden = scaled.astype(BF16)
        h2_t[:, at] = hidden
        h2_r[at, :] = jnp.transpose(scaled).astype(BF16)
        for f in range(FFN // TILE):
            rows = pl.ds(f * TILE, TILE)
            before = nn(wup_t[rows, :], hidden)
            cumulative = 0.5 * (1.0 + lax.erf(before * 0.7071067811865476))
            act_t[rows, at] = (before * cumulative).astype(BF16)
            density = jnp.exp(-0.5 * before * before) * 0.3989422804014327
            dg_t[rows, at] = cumulative + before * density

    loop(0, tiles, forward_mlp)

    a2a_wait_recv(recvg, 2)
    arrive(recvg, g_t, g_r)

    def back_act(i):
        at = tile_at(i, TILE)
        for f in range(FFN // TILE):
            rows = pl.ds(f * TILE, TILE)
            gb_t[rows, at] = (nn(wdown_ref[rows, :], g_t[:, at]) * dg_t[rows, at]).astype(BF16)

    loop(0, tiles, back_act, 4)

    def tiles_of(y, lanes):
        return [y[:, l * 128 : (l + 1) * 128].reshape(16, 16, 128).astype(BF16) for l in range(lanes)]

    def up_down(f):
        rows = tile_at(f, TILE)
        for l, u in enumerate(tiles_of(nn(act_t[rows, :], g_r[...]), 2)):
            grad1[pl.ds(128 + f * 32 + l * 16, 16)] = u
        for l, u in enumerate(tiles_of(nn(gb_t[rows, :], h2_r[...]), 2)):
            grad1[pl.ds(f * 32 + l * 16, 16)] = u

    loop(0, FFN // TILE, up_down, 4)

    def four_copies(src, dst_of, which, mine, dev, sem_base):
        copies = []
        for d in range(1, 4):
            other = lax.rem(mine + d, 4)
            copies.append(
                pltpu.make_async_remote_copy(
                    src_ref=src(other),
                    dst_ref=dst_of,
                    send_sem=four_send.at[sem_base + which, d],
                    recv_sem=four_recv.at[sem_base + which, mine],
                    device_id=dev(other),
                    device_id_type=MESH,
                )
            )
        return copies

    def four_wait(src, dst, which, mine, dev, sem_base):
        for d in range(1, 4):
            other = lax.rem(mine + d, 4)
            got = pltpu.make_async_remote_copy(
                src_ref=src(other),
                dst_ref=dst(other),
                send_sem=four_send.at[sem_base + which, d],
                recv_sem=four_recv.at[sem_base + which, other],
                device_id=dev(other),
                device_id_type=MESH,
            )
            got.wait_recv()
            got.wait_send()

    def group(index, grad, from_core, cur, ra, rb, mid, rc, rd, nk):
        half = nk * 32
        part = half // 2
        quarter = part // 4
        base = index * 4
        cbase = index * 4

        def core_copy(src, dst, sem):
            return pltpu.make_async_remote_copy(
                src_ref=src,
                dst_ref=dst,
                send_sem=core_sems.at[cbase + sem],
                recv_sem=core_sems.at[cbase + sem + 1],
                device_id=core_dev(),
                device_id_type=MESH,
            )

        def first_core():
            return core_copy(grad.at[pl.ds((1 - core) * half, half)], from_core, 0)

        def s0():
            first_core().start()

        def cur_a(o):
            return cur.at[pl.ds(o * quarter, quarter)]

        def cur_b(o):
            return cur.at[pl.ds(part + o * quarter, quarter)]

        def s1():
            first_core().wait()
            total = grad[pl.ds(core * half, half)].astype(F32) + from_core[...].astype(F32)
            cur[...] = total.astype(BF16)
            for c in four_copies(cur_a, ra.at[x], 0, x, x_dev, base):
                c.start()
            for c in four_copies(cur_b, rb.at[y], 1, y, y_dev, base):
                c.start()

        def mid_a(o):
            return mid.at[pl.ds(o * nk, nk)]

        def mid_b(o):
            return mid.at[pl.ds(quarter + o * nk, nk)]

        def add_four(own, slots, mine):
            total = own.astype(F32)
            for d in range(1, 4):
                total = total + slots[lax.rem(mine + d, 4)].astype(F32)
            return total.astype(BF16)

        def s2():
            four_wait(cur_a, lambda o: ra.at[o], 0, x, x_dev, base)
            four_wait(cur_b, lambda o: rb.at[o], 1, y, y_dev, base)
            mid[pl.ds(0, quarter)] = add_four(cur[pl.ds(x * quarter, quarter)], ra, x)
            mid[pl.ds(quarter, quarter)] = add_four(cur[pl.ds(part + y * quarter, quarter)], rb, y)
            for c in four_copies(mid_a, rc.at[y], 2, y, y_dev, base):
                c.start()
            for c in four_copies(mid_b, rd.at[x], 3, x, x_dev, base):
                c.start()

        def s3():
            four_wait(mid_a, lambda o: rc.at[o], 2, y, y_dev, base)
            four_wait(mid_b, lambda o: rd.at[o], 3, x, x_dev, base)
            a = add_four(mid[pl.ds(y * nk, nk)], rc, y)
            b = add_four(mid[pl.ds(quarter + x * nk, nk)], rd, x)
            return a, b

        mine = core * half

        def out_a(xx, yy):
            return grad.at[pl.ds(mine + xx * quarter + yy * nk, nk)]

        def out_b(xx, yy):
            return grad.at[pl.ds(mine + part + yy * quarter + xx * nk, nk)]

        def whole_a(xx):
            return grad.at[pl.ds(mine + xx * quarter, quarter)]

        def whole_b(yy):
            return grad.at[pl.ds(mine + part + yy * quarter, quarter)]

        gbase = 8 + index * 4

        def s5():
            for c in four_copies(lambda o: out_a(x, y), out_a(x, y), 0, y, y_dev, gbase):
                c.start()
            for c in four_copies(lambda o: out_b(x, y), out_b(x, y), 1, x, x_dev, gbase):
                c.start()

        def s6():
            four_wait(lambda o: out_a(x, y), lambda o: out_a(x, o), 0, y, y_dev, gbase)
            four_wait(lambda o: out_b(x, y), lambda o: out_b(o, y), 1, x, x_dev, gbase)
            for c in four_copies(lambda o: whole_a(x), whole_a(x), 2, x, x_dev, gbase):
                c.start()
            for c in four_copies(lambda o: whole_b(y), whole_b(y), 3, y, y_dev, gbase):
                c.start()

        def last_core():
            at = grad.at[pl.ds(mine, half)]
            return core_copy(at, at, 2)

        def s7():
            four_wait(lambda o: whole_a(x), lambda o: whole_a(o), 2, x, x_dev, gbase)
            four_wait(lambda o: whole_b(y), lambda o: whole_b(o), 3, y, y_dev, gbase)
            last_core().start()

        def s8():
            last_core().wait()

        def put(a, b):
            grad[pl.ds(mine + x * quarter + y * nk, nk)] = a
            grad[pl.ds(mine + part + y * quarter + x * nk, nk)] = b

        return s0, s1, s2, s3, put, s5, s6, s7, s8

    def z_copy(src, dst, sems, d, slot):
        other = lax.rem(z + d, NZ)
        return pltpu.make_async_remote_copy(
            src_ref=src,
            dst_ref=dst,
            send_sem=z_send.at[sems, d],
            recv_sem=z_recv.at[sems, slot],
            device_id=z_dev(other),
            device_id_type=MESH,
        )

    one = group(0, grad1, core1, cur1, ra1, rb1, mid1, rc1, rd1, 4)
    two = group(1, grad2, core2, cur2, ra2, rb2, mid2, rc2, rd2, 2)

    def one_s3():
        a, b = one[3]()
        zin1[0:4] = a
        zin1[4:8] = b
        for d in range(1, NZ):
            z_copy(zin1.at[lax.rem(z + d, NZ)], rz1.at[z], 0, d, z).start()

    def one_out(zz):
        p = zz // 4
        k = lax.rem(zz, 4)
        first = x + p * (y - x)
        second = y + p * (x - y)
        return core * 128 + p * 64 + first * 16 + second * 4 + k

    def one_s4():
        total = zin1[z].astype(F32)
        for d in range(1, NZ):
            other = lax.rem(z + d, NZ)
            got = z_copy(zin1.at[other], rz1.at[other], 0, d, other)
            got.wait_recv()
            got.wait_send()
            total = total + rz1[other].astype(F32)
        grad1[one_out(z)] = total.astype(BF16)
        for d in range(1, NZ):
            z_copy(grad1.at[one_out(z)], grad1.at[one_out(z)], 1, d, z).start()

    def one_s5():
        for d in range(1, NZ):
            other = lax.rem(z + d, NZ)
            got = z_copy(grad1.at[one_out(z)], grad1.at[one_out(other)], 1, d, other)
            got.wait_recv()
            got.wait_send()
        one[5]()

    def two_s3():
        a, b = two[3]()
        rz2[z, 0:2] = a
        rz2[z, 2:4] = b
        for d in range(1, NZ):
            z_copy(rz2.at[z], rz2.at[z], 2, d, z).start()

    def two_s5():
        for d in range(1, NZ):
            other = lax.rem(z + d, NZ)
            got = z_copy(rz2.at[z], rz2.at[other], 2, d, other)
            got.wait_recv()
            got.wait_send()
        total = rz2[0].astype(F32)
        for k in range(1, NZ):
            total = total + rz2[k].astype(F32)
        total = total.astype(BF16)
        two[4](total[0:2], total[2:4])
        two[5]()

    def gain_copies(buf, count, mine, dev, send_sem, recv_sem, wait):
        for d in range(1, count):
            other = lax.rem(mine + d, count)
            c = pltpu.make_async_remote_copy(
                src_ref=buf.at[mine],
                dst_ref=buf.at[other] if wait else buf.at[mine],
                send_sem=send_sem(d),
                recv_sem=recv_sem(other) if wait else recv_sem(mine),
                device_id=dev(other),
                device_id_type=MESH,
            )
            if wait:
                c.wait_recv()
                c.wait_send()
            else:
                c.start()

    def add_slots(buf, count):
        total = buf[0]
        for k in range(1, count):
            total = total + buf[k]
        return total

    gain_steps = (
        (gcore, NC, core, lambda o: core_dev(), lambda d: gcore_sems.at[0], lambda o: gcore_sems.at[1]),
        (gx, NX, x, x_dev, lambda d: gfour_send.at[0, d], lambda o: gfour_recv.at[0, o]),
        (gy, NY, y, y_dev, lambda d: gfour_send.at[1, d], lambda o: gfour_recv.at[1, o]),
        (gz, NZ, z, z_dev, lambda d: gz_send.at[d], lambda o: gz_recv.at[o]),
    )

    def gain_start(step, values):
        buf, count, mine, dev, ssem, rsem = gain_steps[step]
        buf[mine] = values
        gain_copies(buf, count, mine, dev, ssem, rsem, False)

    def gain_wait(step):
        buf, count, mine, dev, ssem, rsem = gain_steps[step]
        gain_copies(buf, count, mine, dev, ssem, rsem, True)
        return add_slots(buf, count)

    one[0]()

    gg_cols[...] = jnp.zeros_like(gg_cols)

    def back_norm_two(i):
        at = tile_at(i, TILE)
        grad = nn(wup_ref[...], gb_t[:, at])
        normed = n2_t[:, at]
        gg_cols[:, 1:2] += jnp.sum(grad * normed, axis=1, keepdims=True)
        back = norm_back_rows(grad * gain_two, normed, inv_rows[1:2, at])
        mixed = (g_t[:, at].astype(F32) + back).astype(BF16)
        gm_t[:, at] = mixed
        kept = jnp.where(live_tile(at, TILE), mixed.astype(F32), 0.0)
        kept_rows = jnp.transpose(kept).astype(BF16)
        gbr_r[at, :] = kept_rows
        ga_t[:, at] = nn(wproj_ref[...], kept.astype(BF16)).astype(BF16)
        ga_r[at, :] = nn(kept_rows, wproj_t[...]).astype(BF16)

    loop(0, tiles, back_norm_two, 4)
    one[1]()
    for l, u in enumerate(tiles_of(nn(att_t[...], gbr_r[...]), 2)):
        grad2[96 + l * 16 : 112 + l * 16] = u


    def back_attend(b):
        at = tile_at(b, BLK)
        weights = w_t[b]
        wide = spread_windows(weights.astype(BF16), diagonal)
        gkv_r[at, CH : 2 * CH] = nn(wide, head_rows(ga_r[at, :])).astype(BF16)
        dense = nn(proj_r[at, 2 * CH : 3 * CH], head_columns(ga_t[:, at]))
        grad_w = pack_windows(dense, window_of_lane)
        inner = jnp.sum(weights * grad_w, axis=0, keepdims=True)
        grad_s = (weights * (grad_w - inner) * SCALE).astype(BF16)
        wide_s = spread_windows(grad_s, diagonal)
        gkv_r[at, 0:CH] = nn(wide_s, head_rows(proj_r[at, 0:CH])).astype(BF16)
        for h in range(HEADS):
            k = proj_t[CH + h * HD : CH + (h + 1) * HD, at]
            gq_t[h * HD : (h + 1) * HD, at] = nn(k, wide_s[:, h * BLK : (h + 1) * BLK]).astype(BF16)

    loop(0, ROWS // BLK, back_attend, 8)

    for l, u in enumerate(tiles_of(nn(gq_t[...], h1_r[...]), 2)):
        grad2[l * 16 : (l + 1) * 16] = u
    for p in range(2):
        for l, u in enumerate(tiles_of(nn(h1_t[...], gkv_r[:, p * CH : (p + 1) * CH]), 2)):
            grad2[(p + 1) * 32 + l * 16 : (p + 1) * 32 + (l + 1) * 16] = u
    two[0]()
    one[2]()
    two[1]()

    def back_norm_one(i):
        at = tile_at(i, TILE)
        grad = nn(wqkv_ref[:, 0:CH], gq_t[:, at]) + jnp.transpose(
            nn(gkv_r[at, :], wqkv_t[CH : 3 * CH, :])
        )
        normed = n1_t[:, at]
        gg_cols[:, 0:1] += jnp.sum(grad * normed, axis=1, keepdims=True)
        back = norm_back_rows(grad * gain_one, normed, inv_rows[0:1, at])
        dx_r[at, :] = jnp.transpose(gm_t[:, at].astype(F32) + back).astype(BF16)

    loop(0, tiles, back_norm_one, 4)
    gain_start(0, jnp.transpose(gg_cols[...]))

    def give_back(i):
        pick = select_rows((i * TILE).astype(F32), TILE, rank_rows[1:2, :])
        sendr[tile_at(i, TILE // SHARE)] = to_units(nn(pick, dx_r[...]))

    loop(0, tiles, give_back, 4)
    stores = [
        pltpu.make_async_copy(src, dst, store_sems.at[k])
        for k, (src, dst) in enumerate(
            ((grad1, out1_ref), (grad2, out2_ref))
        )
    ]
    cuts = (1, 36, 72, 104)
    two[2]()
    a2a_own(sendr, outr_ref, 4)
    a2a_some(sendr, outr_ref, 4, cuts[0], cuts[1])
    gain_start(1, gain_wait(0))
    one_s3()
    two_s3()
    a2a_some(sendr, outr_ref, 4, cuts[1], cuts[2])
    gain_start(2, gain_wait(1))
    one_s4()
    two_s5()
    a2a_some(sendr, outr_ref, 4, cuts[2], cuts[3])
    gain_start(3, gain_wait(2))
    one_s5()
    two[6]()
    a2a_some(sendr, outr_ref, 4, cuts[3], n_pts)
    one[6]()
    two[7]()
    one[7]()
    one[8]()
    stores[0].start()
    gsum[...] = gain_wait(3)
    keep_gains = pltpu.make_async_copy(gsum, ogain_ref, store_sems.at[3])
    keep_gains.start()
    two[8]()
    stores[1].start()
    a2a_wait_recv(outr_ref, 4)
    a2a_wait_send(sendx, 0)
    a2a_wait_send(sendg, 2)
    a2a_wait_send(sendr, 4)
    for store in stores:
        store.wait()
    keep_ranks.wait()
    keep_gains.wait()


def finish(
    grad_scale,
    u1_hbm,
    u2_hbm,
    ur_hbm,
    ranks_hbm,
    gains_hbm,
    dx_hbm,
    qkv_hbm,
    proj_hbm,
    up_hbm,
    down_hbm,
    gain_one_ref,
    gain_two_ref,
    u1_ref,
    u2_ref,
    ur_ref,
    ranks_ref,
    gains_ref,
    dx_ref,
    oqkv_ref,
    oproj_ref,
    oup_ref,
    odown_ref,
    load_sems,
    sems,
):
    half = 128
    pairs = (
        (u1_hbm.at[pl.ds(half, half)], u1_ref.at[pl.ds(half, half)]),
        (ur_hbm, ur_ref),
        (ranks_hbm, ranks_ref),
        (u1_hbm.at[pl.ds(0, half)], u1_ref.at[pl.ds(0, half)]),
        (u2_hbm, u2_ref),
        (gains_hbm, gains_ref),
    )
    loads = [pltpu.make_async_copy(a, b, load_sems.at[k]) for k, (a, b) in enumerate(pairs)]
    for load in loads:
        load.start()
    stores = [
        pltpu.make_async_copy(src, dst, sems.at[k])
        for k, (src, dst) in enumerate(
            (
                (oup_ref, up_hbm),
                (odown_ref, down_hbm),
                (oqkv_ref, qkv_hbm),
                (oproj_ref, proj_hbm),
                (dx_ref, dx_hbm),
            )
        )
    ]

    def block(ref, first):
        left = ref[first : first + 16].reshape(TILE, 128).astype(F32)
        right = ref[first + 16 : first + 32].reshape(TILE, 128).astype(F32)
        return jnp.concatenate([left, right], axis=1) * grad_scale

    loads[0].wait()
    for f in range(FFN // TILE):
        odown_ref[f * TILE : (f + 1) * TILE, :] = block(u1_ref, 128 + f * 32)
    stores[1].start()
    loads[1].wait()
    loads[2].wait()
    left, right = from_units(ur_ref[...])
    arrived = jnp.concatenate([left, right], axis=1).astype(BF16)
    ranks = jnp.transpose(ranks_ref[...])
    for i in range(ROWS // TILE):
        slot = lax.broadcasted_iota(jnp.int32, (TILE, ROWS), 1).astype(F32)
        pick = jnp.where(ranks[i * TILE : (i + 1) * TILE, 0:1] == slot, 1.0, 0.0).astype(BF16)
        dx_ref[i * TILE : (i + 1) * TILE, :] = nn(pick, arrived).astype(BF16)
    stores[4].start()
    loads[3].wait()
    for f in range(FFN // TILE):
        at = slice(f * TILE, (f + 1) * TILE)
        oup_ref[:, at] = jnp.transpose(block(u1_ref, f * 32))
    stores[0].start()
    loads[4].wait()
    oqkv_ref[:, 0:CH] = jnp.transpose(block(u2_ref, 0))
    oqkv_ref[:, CH : 2 * CH] = block(u2_ref, 32)
    oqkv_ref[:, 2 * CH : 3 * CH] = block(u2_ref, 64)
    stores[2].start()
    oproj_ref[...] = block(u2_ref, 96)
    stores[3].start()
    loads[5].wait()
    gain_one_ref[...] = gains_ref[0:1, :] * grad_scale
    gain_two_ref[...] = gains_ref[1:2, :] * grad_scale
    for store in stores:
        store.wait()


def units(n):
    return pltpu.VMEM((n, 16, 128), BF16)


def shards(
    features,
    cotangent,
    morton_target,
    morton_source,
    counts,
    w_qkv,
    w_proj,
    w_up,
    w_down,
    gain_one,
    gain_two,
):
    n_pts = lax.axis_size("pts")
    grad_scale = 1.0 / math.sqrt(features.shape[0] * n_pts * lax.axis_size("quad"))
    rows = lambda n, kind: pltpu.VMEM((n, ROWS), kind)
    wide = lambda n: pltpu.VMEM((ROWS, n), BF16)
    sem = pltpu.SemaphoreType.DMA
    vmem = pl.BlockSpec(memory_space=pltpu.VMEM)
    anywhere = pl.BlockSpec(memory_space=pl.ANY)
    hbm = pl.BlockSpec(memory_space=pltpu.HBM)
    parts = pl.pallas_call(
        functools.partial(kernel, n_pts),
        out_shape=(
            jax.ShapeDtypeStruct((256, 16, 128), BF16),
            jax.ShapeDtypeStruct((128, 16, 128), BF16),
            jax.ShapeDtypeStruct((n_pts, 16, 128), BF16),
            jax.ShapeDtypeStruct((8, ROWS), F32),
            jax.ShapeDtypeStruct((8, CH), F32),
        ),
        in_specs=[hbm] * 11,
        out_specs=[anywhere] * 5,
        scratch_shapes=[
            pltpu.VMEM((8, 128), jnp.int32),
            pltpu.VMEM((8, 128), jnp.int32),
            pltpu.VMEM((1, WINDOW), jnp.int32),
            pltpu.VMEM((1, CH), F32),
            pltpu.VMEM((1, CH), F32),
            wide(CH),
            wide(CH),
            pltpu.VMEM((CH, 3 * CH), BF16),
            pltpu.VMEM((CH, CH), BF16),
            pltpu.VMEM((CH, FFN), BF16),
            pltpu.VMEM((FFN, CH), BF16),
        ]
        + [units(n_pts)] * 5
        + [
            rows(8, F32),
            pltpu.VMEM((ROWS, 8), F32),
            rows(8, F32),
            pltpu.VMEM((CH, 8), F32),
            pltpu.VMEM((3 * CH, CH), BF16),
            pltpu.VMEM((CH, CH), BF16),
            pltpu.VMEM((FFN, CH), BF16),
            rows(CH, BF16),
            rows(CH, F32),
            rows(CH, BF16),
            wide(CH),
            rows(8, F32),
            rows(3 * CH, BF16),
            wide(3 * CH),
            pltpu.VMEM((ROWS // BLK, WINDOW, HEADS * BLK), F32),
            rows(CH, BF16),
            rows(CH, F32),
            rows(CH, BF16),
            wide(CH),
            rows(FFN, BF16),
            rows(FFN, F32),
            rows(CH, BF16),
            wide(CH),
            rows(FFN, BF16),
            rows(CH, BF16),
            wide(CH),
            rows(CH, BF16),
            wide(CH),
            rows(CH, BF16),
            wide(2 * CH),
            wide(CH),
            pltpu.VMEM((CH, 8), F32),
            units(256),
            units(128),
            units(128),
            pltpu.VMEM((4, 16, 16, 128), BF16),
            pltpu.VMEM((4, 16, 16, 128), BF16),
            units(32),
            pltpu.VMEM((4, 4, 16, 128), BF16),
            pltpu.VMEM((4, 4, 16, 128), BF16),
            units(8),
            units(8),
            units(128),
            units(64),
            units(64),
            pltpu.VMEM((4, 8, 16, 128), BF16),
            pltpu.VMEM((4, 8, 16, 128), BF16),
            units(16),
            pltpu.VMEM((4, 2, 16, 128), BF16),
            pltpu.VMEM((4, 2, 16, 128), BF16),
            pltpu.VMEM((8, 4, 16, 128), BF16),
            pltpu.VMEM((2, 8, CH), F32),
            pltpu.VMEM((4, 8, CH), F32),
            pltpu.VMEM((4, 8, CH), F32),
            pltpu.VMEM((8, 8, CH), F32),
            pltpu.VMEM((8, CH), F32),
            sem((6,)),
            sem((8,)),
            sem((16, 4)),
            sem((16, 4)),
            sem((3, 8)),
            sem((3, 8)),
            sem((2,)),
            sem((2, 4)),
            sem((2, 4)),
            sem((8,)),
            sem((8,)),
            sem((11,)),
            sem((4,)),
        ],
        compiler_params=pltpu.CompilerParams(
            collective_id=0, has_side_effects=True, vmem_limit_bytes=60 * 1024 * 1024
        ),
    )(
        morton_target.reshape(8, 128),
        morton_source.reshape(8, 128),
        counts.reshape(1, WINDOW),
        gain_one.reshape(1, CH),
        gain_two.reshape(1, CH),
        features,
        cotangent,
        w_qkv,
        w_proj,
        w_up,
        w_down,
    )
    shapes = (
        ((ROWS, CH), BF16),
        ((CH, 3 * CH), F32),
        ((CH, CH), F32),
        ((CH, FFN), F32),
        ((FFN, CH), F32),
    )
    out = pl.pallas_call(
        functools.partial(finish, grad_scale),
        out_shape=tuple(jax.ShapeDtypeStruct(*shape) for shape in shapes)
        + (jax.ShapeDtypeStruct((1, CH), F32),) * 2,
        in_specs=[hbm] * 5,
        out_specs=[anywhere] * 5 + [vmem] * 2,
        scratch_shapes=[
            units(256),
            units(128),
            units(n_pts),
            rows(8, F32),
            pltpu.VMEM((8, CH), F32),
        ]
        + [pltpu.VMEM(*shape) for shape in shapes]
        + [sem((6,)), sem((5,))],
        compiler_params=pltpu.CompilerParams(vmem_limit_bytes=60 * 1024 * 1024),
    )(*parts)
    dx, grad_qkv, grad_proj, grad_up, grad_down, gain_one_grad, gain_two_grad = out
    return (
        dx,
        grad_qkv,
        grad_proj,
        grad_up,
        grad_down,
        gain_one_grad.reshape(CH),
        gain_two_grad.reshape(CH),
    )


def solution(mesh):
    placed = (
        P(("pts", "quad"), None),
        P(("pts", "quad"), None),
        P(("pts", "quad")),
        P(("pts", "quad")),
        P(("pts", "quad")),
        P(),
        P(),
        P(),
        P(),
        P(),
        P(),
    )
    return jax.shard_map(
        shards,
        mesh=mesh,
        in_specs=placed,
        out_specs=(P(("pts", "quad"), None), P(), P(), P(), P(), P(), P()),
        check_vma=False,
    )
```

```python
import functools
import math

import jax
import jax.numpy as jnp
from jax import lax
from jax.experimental import pallas as pl
from jax.experimental.pallas import tpu as pltpu
from jax.sharding import PartitionSpec as P

HEADS = 8
WINDOW = 32
DILATION = 4
ROWS = 1024
CH = 256
FFN = 1024
HD = 32
BLK = 128
TILE = 256
SHARE = 8
NEG_FILL = -1e30
SCALE = 1.0 / math.sqrt(HD)

F32 = jnp.float32
BF16 = jnp.bfloat16
MESH = pl.DeviceIdType.MESH

NY, NZ, NX, NC = 4, 8, 4, 2


def nn(a, b):
    return lax.dot_general(a, b, (((1,), (0,)), ((), ())), preferred_element_type=F32)


def nt(a, b):
    return lax.dot_general(a, b, (((1,), (1,)), ((), ())), preferred_element_type=F32)


def tn(a, b):
    return lax.dot_general(a, b, (((0,), (0,)), ((), ())), preferred_element_type=F32)


def loop(start, stop, body, unroll=1):
    def step(i, carry):
        for k in range(unroll):
            body(i * unroll + k)
        return carry

    lax.fori_loop(start // unroll, stop // unroll, step, 0)


def transposed(a):
    return jnp.transpose(a.astype(F32)).astype(a.dtype)


def tile_at(i, size):
    return pl.ds(pl.multiple_of(i * size, size), size)


def norm_rows(values):
    mean = jnp.mean(values, axis=0, keepdims=True)
    centred = values - mean
    inverse = lax.rsqrt(jnp.mean(centred * centred, axis=0, keepdims=True) + 1e-05)
    return centred * inverse, inverse


def norm_back_rows(grad, normed, inverse):
    first = jnp.mean(grad, axis=0, keepdims=True)
    second = jnp.mean(grad * normed, axis=0, keepdims=True)
    return inverse * (grad - first - normed * second)


def pack_windows(dense, window_of_lane):
    packed = dense[3 * WINDOW :]
    for k in (2, 1, 0):
        packed = jnp.where(window_of_lane == k, dense[k * WINDOW : (k + 1) * WINDOW], packed)
    return packed


def spread_windows(packed, diagonal):
    return jnp.concatenate([packed] * DILATION, axis=0) * diagonal


def to_units(y):
    n = y.shape[0] // SHARE
    left = y[:, :128].reshape(n, SHARE, 128)
    right = y[:, 128:].reshape(n, SHARE, 128)
    return jnp.concatenate([left, right], axis=1).astype(BF16)


def from_units(u):
    r = u.astype(F32)
    n = r.shape[0]
    left = r[:, :SHARE, :].reshape(n * SHARE, 128)
    right = r[:, SHARE:, :].reshape(n * SHARE, 128)
    return left, right


def head_columns(t):
    blocks = []
    for h in range(HEADS):
        own = t[h * HD : (h + 1) * HD]
        pieces = [own]
        if h > 0:
            pieces.insert(0, jnp.zeros((h * HD, BLK), t.dtype))
        if h < HEADS - 1:
            pieces.append(jnp.zeros(((HEADS - 1 - h) * HD, BLK), t.dtype))
        blocks.append(jnp.concatenate(pieces, axis=0))
    return jnp.concatenate(blocks, axis=1)


def head_rows(r):
    head = lax.broadcasted_iota(jnp.int32, (1, CH), 1) // HD
    return jnp.concatenate(
        [r * jnp.where(head == h, 1.0, 0.0).astype(r.dtype) for h in range(HEADS)], axis=0
    )


def flip(a):
    return jnp.transpose(a.astype(F32)).astype(BF16)


def kernel(
    n_pts,
    target_hbm,
    source_hbm,
    counts_hbm,
    gain_one_hbm,
    gain_two_hbm,
    x_hbm,
    g_hbm,
    wqkv_hbm,
    wproj_hbm,
    wup_hbm,
    wdown_hbm,
    out1_ref,
    out2_ref,
    outr_ref,
    ranks_ref,
    ogain_ref,
    target_ref,
    source_ref,
    counts_ref,
    gain_one_ref,
    gain_two_ref,
    x_ref,
    g_ref,
    wqkv_ref,
    wproj_ref,
    wup_ref,
    wdown_ref,
    sendx,
    recvx,
    sendg,
    recvg,
    sendr,
    rank_rows,
    rank_cols,
    count_rows,
    gain_cols,
    wqkv_t,
    wproj_t,
    wup_t,
    x_t,
    n1_t,
    h1_t,
    h1_r,
    inv_rows,
    proj_t,
    proj_r,
    w_t,
    att_t,
    n2_t,
    h2_t,
    h2_r,
    act_t,
    dg_t,
    g_t,
    g_r,
    gb_t,
    gm_t,
    gbr_r,
    ga_t,
    ga_r,
    gq_t,
    gkv_r,
    dx_r,
    gg_cols,
    grad1,
    core1,
    cur1,
    ra1,
    rb1,
    mid1,
    rc1,
    rd1,
    zin1,
    rz1,
    grad2,
    core2,
    cur2,
    ra2,
    rb2,
    mid2,
    rc2,
    rd2,
    rz2,
    gcore,
    gx,
    gy,
    gz,
    gsum,
    a2a_sems,
    core_sems,
    four_send,
    four_recv,
    z_send,
    z_recv,
    gcore_sems,
    gfour_send,
    gfour_recv,
    gz_send,
    gz_recv,
    load_sems,
    store_sems,
):
    me = lax.axis_index("pts")
    quad = lax.axis_index("quad")
    core = lax.rem(me, NC)
    x_hi = lax.rem(me // NC, 2)
    z = lax.rem(me // (2 * NC), NZ)
    y = me // (2 * NC * NZ)
    x = x_hi * 2 + quad

    def core_dev():
        return {"pts": me + 1 - 2 * core, "quad": quad}

    def x_dev(other):
        return {"pts": me + (other // 2 - x_hi) * NC, "quad": lax.rem(other, 2)}

    def y_dev(other):
        return {"pts": me + (other - y) * (2 * NC * NZ), "quad": quad}

    def z_dev(other):
        return {"pts": me + (other - z) * (2 * NC), "quad": quad}

    loads = [
        pltpu.make_async_copy(src, dst, load_sems.at[k])
        for k, (src, dst) in enumerate(
            (
                (target_hbm, target_ref),
                (source_hbm, source_ref),
                (counts_hbm, counts_ref),
                (gain_one_hbm, gain_one_ref),
                (gain_two_hbm, gain_two_ref),
                (x_hbm, x_ref),
                (g_hbm, g_ref),
                (wqkv_hbm, wqkv_ref),
                (wproj_hbm, wproj_ref),
                (wup_hbm, wup_ref),
                (wdown_hbm, wdown_ref),
            )
        )
    ]
    for load in loads:
        load.start()

    barrier = pltpu.get_barrier_semaphore()

    def greet(k):
        pl.semaphore_signal(
            barrier, inc=1, device_id={"pts": lax.rem(me + k, n_pts), "quad": quad}, device_id_type=MESH
        )

    loop(1, n_pts, greet)
    for hi in range(2):
        pl.semaphore_signal(
            barrier,
            inc=1,
            device_id={"pts": me + (hi - x_hi) * NC, "quad": 1 - quad},
            device_id_type=MESH,
        )

    for load in loads[:5]:
        load.wait()

    def one_row(a):
        return jnp.concatenate([a[r : r + 1, :] for r in range(8)], axis=1)

    stored = lax.broadcasted_iota(jnp.int32, (8, 128), 0) * 128 + lax.broadcasted_iota(
        jnp.int32, (8, 128), 1
    )
    target_key = one_row(((target_ref[...] >> 11) * ROWS + stored).astype(F32))
    to_lane = lax.broadcasted_iota(jnp.int32, (BLK, BLK), 1)
    from_lane = lax.broadcasted_iota(jnp.int32, (BLK, BLK), 0)
    moved = jnp.where(
        from_lane == lax.rem(to_lane, WINDOW) * DILATION + to_lane // WINDOW, 1.0, 0.0
    ).astype(BF16)
    src = source_ref[...]
    digits = jnp.concatenate([src & 63, (src >> 6) & 63, src >> 12], axis=0)
    digits = nn(digits.astype(F32).astype(BF16), moved)
    source_key = one_row(digits[0:8] + 64.0 * digits[8:16] + 4096.0 * digits[16:24])
    spread = jnp.where(
        lax.broadcasted_iota(jnp.int32, (WINDOW, ROWS), 1) // WINDOW
        == lax.broadcasted_iota(jnp.int32, (WINDOW, ROWS), 0),
        1.0,
        0.0,
    ).astype(BF16)
    wide_counts = jnp.broadcast_to(counts_ref[...].astype(F32), (8, WINDOW)).astype(BF16)
    count_rows[...] = nn(wide_counts, spread)
    pad = jnp.zeros((6, ROWS), F32)
    rank_rows[...] = jnp.concatenate([target_key, source_key, pad], axis=0)
    rank_cols[...] = jnp.transpose(rank_rows[...])

    keys = rank_rows[...]

    def count(i, carry):
        t, s = carry
        cols = rank_cols[tile_at(i, 64), :]
        t = t + jnp.sum(jnp.where(cols[:, 0:1] < keys[0:1, :], 1.0, 0.0), axis=0, keepdims=True)
        s = s + jnp.sum(jnp.where(cols[:, 1:2] < keys[1:2, :], 1.0, 0.0), axis=0, keepdims=True)
        return t, s

    zero_row = jnp.zeros((1, ROWS), F32)
    rank_target, rank_source = lax.fori_loop(0, ROWS // 64, count, (zero_row, zero_row))
    rank_rows[...] = jnp.concatenate([rank_target, rank_source, pad], axis=0)
    rank_cols[...] = jnp.transpose(rank_rows[...])

    def select_rows(first, size, ranks):
        slot = lax.broadcasted_iota(jnp.int32, (size, ranks.shape[1]), 0).astype(F32)
        return jnp.where(slot + first == ranks, 1.0, 0.0).astype(BF16)

    def place(i, source_ref, out):
        pick = select_rows((i * TILE).astype(F32), TILE, rank_rows[0:1, :])
        out[tile_at(i, TILE // SHARE)] = to_units(nn(pick, source_ref[...]))

    def a2a(send, recv, index, k):
        peer = lax.rem(me + k, n_pts)
        return pltpu.make_async_remote_copy(
            src_ref=send.at[peer],
            dst_ref=recv.at[me],
            send_sem=a2a_sems.at[index],
            recv_sem=a2a_sems.at[index + 1],
            device_id={"pts": peer, "quad": quad},
            device_id_type=MESH,
        )

    def a2a_some(send, recv, index, first, stop):
        loop(first, stop, lambda j: a2a(send, recv, index, 1 + lax.rem((j - 1) * 37, n_pts - 1)).start())

    def a2a_own(send, recv, index):
        pltpu.make_async_copy(send.at[me], recv.at[me], a2a_sems.at[index + 1]).start()

    def a2a_start(send, recv, index):
        a2a_own(send, recv, index)
        a2a_some(send, recv, index, 1, n_pts)

    def a2a_wait_recv(recv, index):
        pltpu.make_async_copy(recv, recv, a2a_sems.at[index + 1]).wait()

    def a2a_wait_send(send, index):
        part = send.at[pl.ds(0, n_pts - 1)]
        pltpu.make_async_copy(part, part, a2a_sems.at[index]).wait()

    keep_ranks = pltpu.make_async_copy(rank_rows, ranks_ref, store_sems.at[2])
    keep_ranks.start()
    tiles = ROWS // TILE
    loads[5].wait()
    loop(0, tiles, lambda i: place(i, x_ref, sendx))
    pl.semaphore_wait(barrier, n_pts + 1)
    a2a_start(sendx, recvx, 0)
    loads[6].wait()
    loop(0, tiles, lambda i: place(i, g_ref, sendg))
    a2a_start(sendg, recvg, 2)

    for load in loads[7:]:
        load.wait()
    wqkv_t[...] = transposed(wqkv_ref[...])
    wproj_t[...] = transposed(wproj_ref[...])
    wup_t[...] = transposed(wup_ref[...])
    gain_cols[...] = jnp.transpose(
        jnp.concatenate([gain_one_ref[...], gain_two_ref[...], jnp.zeros((6, CH), F32)], axis=0)
    )
    gain_one = gain_cols[:, 0:1]
    gain_two = gain_cols[:, 1:2]

    span = HEADS * BLK
    sub = lax.broadcasted_iota(jnp.int32, (WINDOW, span), 0).astype(F32)
    window_of_lane = lax.rem(lax.broadcasted_iota(jnp.int32, (WINDOW, span), 1), BLK) // WINDOW
    diagonal = jnp.where(
        lax.broadcasted_iota(jnp.int32, (BLK, span), 0) // WINDOW
        == lax.rem(lax.broadcasted_iota(jnp.int32, (BLK, span), 1), BLK) // WINDOW,
        1.0,
        0.0,
    ).astype(BF16)

    def live_tile(at, size):
        slot = lax.rem(lax.broadcasted_iota(jnp.int32, (1, size), 1), WINDOW).astype(F32)
        return slot < count_rows[0:1, at]

    def arrive(recv, out, out_rows):
        left, right = from_units(recv[...])
        arrived = jnp.concatenate([left, right], axis=1).astype(BF16)

        def one(i):
            at = tile_at(i, TILE)
            slot = lax.broadcasted_iota(jnp.int32, (TILE, ROWS), 1).astype(F32)
            pick = jnp.where(rank_cols[at, 1:2] == slot, 1.0, 0.0).astype(BF16)
            points = nn(pick, arrived)
            out[:, at] = jnp.transpose(points).astype(BF16)
            if out_rows is not None:
                out_rows[at, :] = points.astype(BF16)

        loop(0, tiles, one, 4)

    a2a_wait_recv(recvx, 0)
    arrive(recvx, x_t, None)

    def first_norm(i):
        at = tile_at(i, TILE)
        normed, inverse = norm_rows(x_t[:, at].astype(F32))
        n1_t[:, at] = normed
        inv_rows[0:1, at] = inverse
        scaled = normed * gain_one
        hidden = scaled.astype(BF16)
        hidden_rows = jnp.transpose(scaled).astype(BF16)
        h1_t[:, at] = hidden
        h1_r[at, :] = hidden_rows
        proj_t[:, at] = nn(wqkv_t[...], hidden).astype(BF16)
        proj_r[at, :] = nn(hidden_rows, wqkv_ref[...]).astype(BF16)

    loop(0, tiles, first_norm, 4)

    def attend(b):
        at = tile_at(b, BLK)
        counted = jnp.concatenate([count_rows[0:1, at]] * HEADS, axis=1)
        dense = nn(proj_r[at, CH : 2 * CH], head_columns(proj_t[0:CH, at]))
        scores = pack_windows(dense, window_of_lane) * SCALE
        scores = jnp.where(sub < counted, scores, NEG_FILL)
        powered = jnp.exp(scores - jnp.max(scores, axis=0, keepdims=True))
        weights = powered / jnp.sum(powered, axis=0, keepdims=True)
        w_t[b] = weights
        wide = spread_windows(weights.astype(BF16), diagonal)
        for h in range(HEADS):
            v = proj_t[2 * CH + h * HD : 2 * CH + (h + 1) * HD, at]
            att_t[h * HD : (h + 1) * HD, at] = nn(v, wide[:, h * BLK : (h + 1) * BLK]).astype(BF16)

    loop(0, ROWS // BLK, attend, 8)

    def forward_mlp(i):
        at = tile_at(i, TILE)
        branch = nn(wproj_t[...], att_t[:, at])
        mixed = x_t[:, at].astype(F32) + jnp.where(live_tile(at, TILE), branch, 0.0)
        normed, inverse = norm_rows(mixed.astype(BF16).astype(F32))
        n2_t[:, at] = normed
        inv_rows[1:2, at] = inverse
        scaled = normed * gain_two
        hidden = scaled.astype(BF16)
        h2_t[:, at] = hidden
        h2_r[at, :] = jnp.transpose(scaled).astype(BF16)
        for f in range(FFN // TILE):
            rows = pl.ds(f * TILE, TILE)
            before = nn(wup_t[rows, :], hidden)
            cumulative = 0.5 * (1.0 + lax.erf(before * 0.7071067811865476))
            act_t[rows, at] = (before * cumulative).astype(BF16)
            density = jnp.exp(-0.5 * before * before) * 0.3989422804014327
            dg_t[rows, at] = cumulative + before * density

    loop(0, tiles, forward_mlp)

    a2a_wait_recv(recvg, 2)
    arrive(recvg, g_t, g_r)

    def back_act(i):
        at = tile_at(i, TILE)
        for f in range(FFN // TILE):
            rows = pl.ds(f * TILE, TILE)
            gb_t[rows, at] = (nn(wdown_ref[rows, :], g_t[:, at]) * dg_t[rows, at]).astype(BF16)

    loop(0, tiles, back_act, 4)

    def tiles_of(y, lanes):
        return [y[:, l * 128 : (l + 1) * 128].reshape(16, 16, 128).astype(BF16) for l in range(lanes)]

    def up_down(f):
        rows = tile_at(f, TILE)
        for l, u in enumerate(tiles_of(nn(act_t[rows, :], g_r[...]), 2)):
            grad1[pl.ds(128 + f * 32 + l * 16, 16)] = u
        for l, u in enumerate(tiles_of(nn(gb_t[rows, :], h2_r[...]), 2)):
            grad1[pl.ds(f * 32 + l * 16, 16)] = u

    loop(0, FFN // TILE, up_down, 4)

    def four_copies(src, dst_of, which, mine, dev, sem_base):
        copies = []
        for d in range(1, 4):
            other = lax.rem(mine + d, 4)
            copies.append(
                pltpu.make_async_remote_copy(
                    src_ref=src(other),
                    dst_ref=dst_of,
                    send_sem=four_send.at[sem_base + which, d],
                    recv_sem=four_recv.at[sem_base + which, mine],
                    device_id=dev(other),
                    device_id_type=MESH,
                )
            )
        return copies

    def four_wait(src, dst, which, mine, dev, sem_base):
        for d in range(1, 4):
            other = lax.rem(mine + d, 4)
            got = pltpu.make_async_remote_copy(
                src_ref=src(other),
                dst_ref=dst(other),
                send_sem=four_send.at[sem_base + which, d],
                recv_sem=four_recv.at[sem_base + which, other],
                device_id=dev(other),
                device_id_type=MESH,
            )
            got.wait_recv()
            got.wait_send()

    def group(index, grad, from_core, cur, ra, rb, mid, rc, rd, nk):
        half = nk * 32
        part = half // 2
        quarter = part // 4
        base = index * 4
        cbase = index * 4

        def core_copy(src, dst, sem):
            return pltpu.make_async_remote_copy(
                src_ref=src,
                dst_ref=dst,
                send_sem=core_sems.at[cbase + sem],
                recv_sem=core_sems.at[cbase + sem + 1],
                device_id=core_dev(),
                device_id_type=MESH,
            )

        def first_core():
            return core_copy(grad.at[pl.ds((1 - core) * half, half)], from_core, 0)

        def s0():
            first_core().start()

        def cur_a(o):
            return cur.at[pl.ds(o * quarter, quarter)]

        def cur_b(o):
            return cur.at[pl.ds(part + o * quarter, quarter)]

        def s1():
            first_core().wait()
            total = grad[pl.ds(core * half, half)].astype(F32) + from_core[...].astype(F32)
            cur[...] = total.astype(BF16)
            for c in four_copies(cur_a, ra.at[x], 0, x, x_dev, base):
                c.start()
            for c in four_copies(cur_b, rb.at[y], 1, y, y_dev, base):
                c.start()

        def mid_a(o):
            return mid.at[pl.ds(o * nk, nk)]

        def mid_b(o):
            return mid.at[pl.ds(quarter + o * nk, nk)]

        def add_four(own, slots, mine):
            total = own.astype(F32)
            for d in range(1, 4):
                total = total + slots[lax.rem(mine + d, 4)].astype(F32)
            return total.astype(BF16)

        def s2():
            four_wait(cur_a, lambda o: ra.at[o], 0, x, x_dev, base)
            four_wait(cur_b, lambda o: rb.at[o], 1, y, y_dev, base)
            mid[pl.ds(0, quarter)] = add_four(cur[pl.ds(x * quarter, quarter)], ra, x)
            mid[pl.ds(quarter, quarter)] = add_four(cur[pl.ds(part + y * quarter, quarter)], rb, y)
            for c in four_copies(mid_a, rc.at[y], 2, y, y_dev, base):
                c.start()
            for c in four_copies(mid_b, rd.at[x], 3, x, x_dev, base):
                c.start()

        def s3():
            four_wait(mid_a, lambda o: rc.at[o], 2, y, y_dev, base)
            four_wait(mid_b, lambda o: rd.at[o], 3, x, x_dev, base)
            a = add_four(mid[pl.ds(y * nk, nk)], rc, y)
            b = add_four(mid[pl.ds(quarter + x * nk, nk)], rd, x)
            return a, b

        mine = core * half

        def out_a(xx, yy):
            return grad.at[pl.ds(mine + xx * quarter + yy * nk, nk)]

        def out_b(xx, yy):
            return grad.at[pl.ds(mine + part + yy * quarter + xx * nk, nk)]

        def whole_a(xx):
            return grad.at[pl.ds(mine + xx * quarter, quarter)]

        def whole_b(yy):
            return grad.at[pl.ds(mine + part + yy * quarter, quarter)]

        gbase = 8 + index * 4

        def s5():
            for c in four_copies(lambda o: out_a(x, y), out_a(x, y), 0, y, y_dev, gbase):
                c.start()
            for c in four_copies(lambda o: out_b(x, y), out_b(x, y), 1, x, x_dev, gbase):
                c.start()

        def s6():
            four_wait(lambda o: out_a(x, y), lambda o: out_a(x, o), 0, y, y_dev, gbase)
            four_wait(lambda o: out_b(x, y), lambda o: out_b(o, y), 1, x, x_dev, gbase)
            for c in four_copies(lambda o: whole_a(x), whole_a(x), 2, x, x_dev, gbase):
                c.start()
            for c in four_copies(lambda o: whole_b(y), whole_b(y), 3, y, y_dev, gbase):
                c.start()

        def last_core():
            at = grad.at[pl.ds(mine, half)]
            return core_copy(at, at, 2)

        def s7():
            four_wait(lambda o: whole_a(x), lambda o: whole_a(o), 2, x, x_dev, gbase)
            four_wait(lambda o: whole_b(y), lambda o: whole_b(o), 3, y, y_dev, gbase)
            last_core().start()

        def s8():
            last_core().wait()

        def put(a, b):
            grad[pl.ds(mine + x * quarter + y * nk, nk)] = a
            grad[pl.ds(mine + part + y * quarter + x * nk, nk)] = b

        return s0, s1, s2, s3, put, s5, s6, s7, s8

    def z_copy(src, dst, sems, d, slot):
        other = lax.rem(z + d, NZ)
        return pltpu.make_async_remote_copy(
            src_ref=src,
            dst_ref=dst,
            send_sem=z_send.at[sems, d],
            recv_sem=z_recv.at[sems, slot],
            device_id=z_dev(other),
            device_id_type=MESH,
        )

    one = group(0, grad1, core1, cur1, ra1, rb1, mid1, rc1, rd1, 4)
    two = group(1, grad2, core2, cur2, ra2, rb2, mid2, rc2, rd2, 2)

    def one_s3():
        a, b = one[3]()
        zin1[0:4] = a
        zin1[4:8] = b
        for d in range(1, NZ):
            z_copy(zin1.at[lax.rem(z + d, NZ)], rz1.at[z], 0, d, z).start()

    def one_out(zz):
        p = zz // 4
        k = lax.rem(zz, 4)
        first = x + p * (y - x)
        second = y + p * (x - y)
        return core * 128 + p * 64 + first * 16 + second * 4 + k

    def one_s4():
        total = zin1[z].astype(F32)
        for d in range(1, NZ):
            other = lax.rem(z + d, NZ)
            got = z_copy(zin1.at[other], rz1.at[other], 0, d, other)
            got.wait_recv()
            got.wait_send()
            total = total + rz1[other].astype(F32)
        grad1[one_out(z)] = total.astype(BF16)
        for d in range(1, NZ):
            z_copy(grad1.at[one_out(z)], grad1.at[one_out(z)], 1, d, z).start()

    def one_s5():
        for d in range(1, NZ):
            other = lax.rem(z + d, NZ)
            got = z_copy(grad1.at[one_out(z)], grad1.at[one_out(other)], 1, d, other)
            got.wait_recv()
            got.wait_send()
        one[5]()

    def two_s3():
        a, b = two[3]()
        rz2[z, 0:2] = a
        rz2[z, 2:4] = b
        for d in range(1, NZ):
            z_copy(rz2.at[z], rz2.at[z], 2, d, z).start()

    def two_s5():
        for d in range(1, NZ):
            other = lax.rem(z + d, NZ)
            got = z_copy(rz2.at[z], rz2.at[other], 2, d, other)
            got.wait_recv()
            got.wait_send()
        total = rz2[0].astype(F32)
        for k in range(1, NZ):
            total = total + rz2[k].astype(F32)
        total = total.astype(BF16)
        two[4](total[0:2], total[2:4])
        two[5]()

    def gain_copies(buf, count, mine, dev, send_sem, recv_sem, wait):
        for d in range(1, count):
            other = lax.rem(mine + d, count)
            c = pltpu.make_async_remote_copy(
                src_ref=buf.at[mine],
                dst_ref=buf.at[other] if wait else buf.at[mine],
                send_sem=send_sem(d),
                recv_sem=recv_sem(other) if wait else recv_sem(mine),
                device_id=dev(other),
                device_id_type=MESH,
            )
            if wait:
                c.wait_recv()
                c.wait_send()
            else:
                c.start()

    def add_slots(buf, count):
        total = buf[0]
        for k in range(1, count):
            total = total + buf[k]
        return total

    gain_steps = (
        (gcore, NC, core, lambda o: core_dev(), lambda d: gcore_sems.at[0], lambda o: gcore_sems.at[1]),
        (gx, NX, x, x_dev, lambda d: gfour_send.at[0, d], lambda o: gfour_recv.at[0, o]),
        (gy, NY, y, y_dev, lambda d: gfour_send.at[1, d], lambda o: gfour_recv.at[1, o]),
        (gz, NZ, z, z_dev, lambda d: gz_send.at[d], lambda o: gz_recv.at[o]),
    )

    def gain_start(step, values):
        buf, count, mine, dev, ssem, rsem = gain_steps[step]
        buf[mine] = values
        gain_copies(buf, count, mine, dev, ssem, rsem, False)

    def gain_wait(step):
        buf, count, mine, dev, ssem, rsem = gain_steps[step]
        gain_copies(buf, count, mine, dev, ssem, rsem, True)
        return add_slots(buf, count)

    one[0]()

    gg_cols[...] = jnp.zeros_like(gg_cols)

    def back_norm_two(i):
        at = tile_at(i, TILE)
        grad = nn(wup_ref[...], gb_t[:, at])
        normed = n2_t[:, at]
        gg_cols[:, 1:2] += jnp.sum(grad * normed, axis=1, keepdims=True)
        back = norm_back_rows(grad * gain_two, normed, inv_rows[1:2, at])
        mixed = (g_t[:, at].astype(F32) + back).astype(BF16)
        gm_t[:, at] = mixed
        kept = jnp.where(live_tile(at, TILE), mixed.astype(F32), 0.0)
        kept_rows = jnp.transpose(kept).astype(BF16)
        gbr_r[at, :] = kept_rows
        ga_t[:, at] = nn(wproj_ref[...], kept.astype(BF16)).astype(BF16)
        ga_r[at, :] = nn(kept_rows, wproj_t[...]).astype(BF16)

    loop(0, tiles, back_norm_two, 4)
    one[1]()
    for l, u in enumerate(tiles_of(nn(att_t[...], gbr_r[...]), 2)):
        grad2[96 + l * 16 : 112 + l * 16] = u


    def back_attend(b):
        at = tile_at(b, BLK)
        weights = w_t[b]
        wide = spread_windows(weights.astype(BF16), diagonal)
        gkv_r[at, CH : 2 * CH] = nn(wide, head_rows(ga_r[at, :])).astype(BF16)
        dense = nn(proj_r[at, 2 * CH : 3 * CH], head_columns(ga_t[:, at]))
        grad_w = pack_windows(dense, window_of_lane)
        inner = jnp.sum(weights * grad_w, axis=0, keepdims=True)
        grad_s = (weights * (grad_w - inner) * SCALE).astype(BF16)
        wide_s = spread_windows(grad_s, diagonal)
        gkv_r[at, 0:CH] = nn(wide_s, head_rows(proj_r[at, 0:CH])).astype(BF16)
        for h in range(HEADS):
            k = proj_t[CH + h * HD : CH + (h + 1) * HD, at]
            gq_t[h * HD : (h + 1) * HD, at] = nn(k, wide_s[:, h * BLK : (h + 1) * BLK]).astype(BF16)

    loop(0, ROWS // BLK, back_attend, 8)

    for l, u in enumerate(tiles_of(nn(gq_t[...], h1_r[...]), 2)):
        grad2[l * 16 : (l + 1) * 16] = u
    for p in range(2):
        for l, u in enumerate(tiles_of(nn(h1_t[...], gkv_r[:, p * CH : (p + 1) * CH]), 2)):
            grad2[(p + 1) * 32 + l * 16 : (p + 1) * 32 + (l + 1) * 16] = u
    two[0]()
    one[2]()
    two[1]()

    def back_norm_one(i):
        at = tile_at(i, TILE)
        grad = nn(wqkv_ref[:, 0:CH], gq_t[:, at]) + jnp.transpose(
            nn(gkv_r[at, :], wqkv_t[CH : 3 * CH, :])
        )
        normed = n1_t[:, at]
        gg_cols[:, 0:1] += jnp.sum(grad * normed, axis=1, keepdims=True)
        back = norm_back_rows(grad * gain_one, normed, inv_rows[0:1, at])
        dx_r[at, :] = jnp.transpose(gm_t[:, at].astype(F32) + back).astype(BF16)

    loop(0, tiles, back_norm_one, 4)
    gain_start(0, jnp.transpose(gg_cols[...]))

    def give_back(i):
        pick = select_rows((i * TILE).astype(F32), TILE, rank_rows[1:2, :])
        sendr[tile_at(i, TILE // SHARE)] = to_units(nn(pick, dx_r[...]))

    loop(0, tiles, give_back, 4)
    stores = [
        pltpu.make_async_copy(src, dst, store_sems.at[k])
        for k, (src, dst) in enumerate(
            ((grad1, out1_ref), (grad2, out2_ref))
        )
    ]
    a2a_own(sendr, outr_ref, 4)
    def send_slice(k):
        a2a_some(sendr, outr_ref, 4, 1 + 13 * k, min(14 + 13 * k, n_pts))

    send_slice(0)
    gain_start(1, gain_wait(0))
    two[2]()
    send_slice(1)
    one_s3()
    send_slice(2)
    two_s3()
    send_slice(3)
    gain_start(2, gain_wait(1))
    one_s4()
    send_slice(4)
    two_s5()
    send_slice(5)
    gain_start(3, gain_wait(2))
    one_s5()
    send_slice(6)
    two[6]()
    send_slice(7)
    one[6]()
    send_slice(8)
    two[7]()
    send_slice(9)
    one[7]()
    one[8]()
    stores[0].start()
    gsum[...] = gain_wait(3)
    keep_gains = pltpu.make_async_copy(gsum, ogain_ref, store_sems.at[3])
    keep_gains.start()
    two[8]()
    stores[1].start()
    a2a_wait_recv(outr_ref, 4)
    a2a_wait_send(sendx, 0)
    a2a_wait_send(sendg, 2)
    a2a_wait_send(sendr, 4)
    for store in stores:
        store.wait()
    keep_ranks.wait()
    keep_gains.wait()


def finish(
    grad_scale,
    u1_hbm,
    u2_hbm,
    ur_hbm,
    ranks_hbm,
    gains_hbm,
    dx_hbm,
    qkv_hbm,
    proj_hbm,
    up_hbm,
    down_hbm,
    gain_one_ref,
    gain_two_ref,
    u1_ref,
    u2_ref,
    ur_ref,
    ranks_ref,
    gains_ref,
    dx_ref,
    oqkv_ref,
    oproj_ref,
    oup_ref,
    odown_ref,
    load_sems,
    sems,
):
    half = 128
    pairs = (
        (u1_hbm.at[pl.ds(half, half)], u1_ref.at[pl.ds(half, half)]),
        (ur_hbm, ur_ref),
        (ranks_hbm, ranks_ref),
        (u1_hbm.at[pl.ds(0, half)], u1_ref.at[pl.ds(0, half)]),
        (u2_hbm, u2_ref),
        (gains_hbm, gains_ref),
    )
    loads = [pltpu.make_async_copy(a, b, load_sems.at[k]) for k, (a, b) in enumerate(pairs)]
    for load in loads:
        load.start()
    stores = [
        pltpu.make_async_copy(src, dst, sems.at[k])
        for k, (src, dst) in enumerate(
            (
                (oup_ref, up_hbm),
                (odown_ref, down_hbm),
                (oqkv_ref, qkv_hbm),
                (oproj_ref, proj_hbm),
                (dx_ref, dx_hbm),
            )
        )
    ]

    def block(ref, first):
        left = ref[first : first + 16].reshape(TILE, 128).astype(F32)
        right = ref[first + 16 : first + 32].reshape(TILE, 128).astype(F32)
        return jnp.concatenate([left, right], axis=1) * grad_scale

    loads[0].wait()
    for f in range(FFN // TILE):
        odown_ref[f * TILE : (f + 1) * TILE, :] = block(u1_ref, 128 + f * 32)
    stores[1].start()
    loads[1].wait()
    loads[2].wait()
    left, right = from_units(ur_ref[...])
    arrived = jnp.concatenate([left, right], axis=1).astype(BF16)
    ranks = jnp.transpose(ranks_ref[...])
    for i in range(ROWS // TILE):
        slot = lax.broadcasted_iota(jnp.int32, (TILE, ROWS), 1).astype(F32)
        pick = jnp.where(ranks[i * TILE : (i + 1) * TILE, 0:1] == slot, 1.0, 0.0).astype(BF16)
        dx_ref[i * TILE : (i + 1) * TILE, :] = nn(pick, arrived).astype(BF16)
    stores[4].start()
    loads[3].wait()
    for f in range(FFN // TILE):
        at = slice(f * TILE, (f + 1) * TILE)
        oup_ref[:, at] = jnp.transpose(block(u1_ref, f * 32))
    stores[0].start()
    loads[4].wait()
    oqkv_ref[:, 0:CH] = jnp.transpose(block(u2_ref, 0))
    oqkv_ref[:, CH : 2 * CH] = block(u2_ref, 32)
    oqkv_ref[:, 2 * CH : 3 * CH] = block(u2_ref, 64)
    stores[2].start()
    oproj_ref[...] = block(u2_ref, 96)
    stores[3].start()
    loads[5].wait()
    gain_one_ref[...] = gains_ref[0:1, :] * grad_scale
    gain_two_ref[...] = gains_ref[1:2, :] * grad_scale
    for store in stores:
        store.wait()


def units(n):
    return pltpu.VMEM((n, 16, 128), BF16)


def shards(
    features,
    cotangent,
    morton_target,
    morton_source,
    counts,
    w_qkv,
    w_proj,
    w_up,
    w_down,
    gain_one,
    gain_two,
):
    n_pts = lax.axis_size("pts")
    grad_scale = 1.0 / math.sqrt(features.shape[0] * n_pts * lax.axis_size("quad"))
    rows = lambda n, kind: pltpu.VMEM((n, ROWS), kind)
    wide = lambda n: pltpu.VMEM((ROWS, n), BF16)
    sem = pltpu.SemaphoreType.DMA
    vmem = pl.BlockSpec(memory_space=pltpu.VMEM)
    anywhere = pl.BlockSpec(memory_space=pl.ANY)
    hbm = pl.BlockSpec(memory_space=pltpu.HBM)
    parts = pl.pallas_call(
        functools.partial(kernel, n_pts),
        out_shape=(
            jax.ShapeDtypeStruct((256, 16, 128), BF16),
            jax.ShapeDtypeStruct((128, 16, 128), BF16),
            jax.ShapeDtypeStruct((n_pts, 16, 128), BF16),
            jax.ShapeDtypeStruct((8, ROWS), F32),
            jax.ShapeDtypeStruct((8, CH), F32),
        ),
        in_specs=[hbm] * 11,
        out_specs=[anywhere] * 5,
        scratch_shapes=[
            pltpu.VMEM((8, 128), jnp.int32),
            pltpu.VMEM((8, 128), jnp.int32),
            pltpu.VMEM((1, WINDOW), jnp.int32),
            pltpu.VMEM((1, CH), F32),
            pltpu.VMEM((1, CH), F32),
            wide(CH),
            wide(CH),
            pltpu.VMEM((CH, 3 * CH), BF16),
            pltpu.VMEM((CH, CH), BF16),
            pltpu.VMEM((CH, FFN), BF16),
            pltpu.VMEM((FFN, CH), BF16),
        ]
        + [units(n_pts)] * 5
        + [
            rows(8, F32),
            pltpu.VMEM((ROWS, 8), F32),
            rows(8, F32),
            pltpu.VMEM((CH, 8), F32),
            pltpu.VMEM((3 * CH, CH), BF16),
            pltpu.VMEM((CH, CH), BF16),
            pltpu.VMEM((FFN, CH), BF16),
            rows(CH, BF16),
            rows(CH, F32),
            rows(CH, BF16),
            wide(CH),
            rows(8, F32),
            rows(3 * CH, BF16),
            wide(3 * CH),
            pltpu.VMEM((ROWS // BLK, WINDOW, HEADS * BLK), F32),
            rows(CH, BF16),
            rows(CH, F32),
            rows(CH, BF16),
            wide(CH),
            rows(FFN, BF16),
            rows(FFN, F32),
            rows(CH, BF16),
            wide(CH),
            rows(FFN, BF16),
            rows(CH, BF16),
            wide(CH),
            rows(CH, BF16),
            wide(CH),
            rows(CH, BF16),
            wide(2 * CH),
            wide(CH),
            pltpu.VMEM((CH, 8), F32),
            units(256),
            units(128),
            units(128),
            pltpu.VMEM((4, 16, 16, 128), BF16),
            pltpu.VMEM((4, 16, 16, 128), BF16),
            units(32),
            pltpu.VMEM((4, 4, 16, 128), BF16),
            pltpu.VMEM((4, 4, 16, 128), BF16),
            units(8),
            units(8),
            units(128),
            units(64),
            units(64),
            pltpu.VMEM((4, 8, 16, 128), BF16),
            pltpu.VMEM((4, 8, 16, 128), BF16),
            units(16),
            pltpu.VMEM((4, 2, 16, 128), BF16),
            pltpu.VMEM((4, 2, 16, 128), BF16),
            pltpu.VMEM((8, 4, 16, 128), BF16),
            pltpu.VMEM((2, 8, CH), F32),
            pltpu.VMEM((4, 8, CH), F32),
            pltpu.VMEM((4, 8, CH), F32),
            pltpu.VMEM((8, 8, CH), F32),
            pltpu.VMEM((8, CH), F32),
            sem((6,)),
            sem((8,)),
            sem((16, 4)),
            sem((16, 4)),
            sem((3, 8)),
            sem((3, 8)),
            sem((2,)),
            sem((2, 4)),
            sem((2, 4)),
            sem((8,)),
            sem((8,)),
            sem((11,)),
            sem((4,)),
        ],
        compiler_params=pltpu.CompilerParams(
            collective_id=0, has_side_effects=True, vmem_limit_bytes=60 * 1024 * 1024
        ),
    )(
        morton_target.reshape(8, 128),
        morton_source.reshape(8, 128),
        counts.reshape(1, WINDOW),
        gain_one.reshape(1, CH),
        gain_two.reshape(1, CH),
        features,
        cotangent,
        w_qkv,
        w_proj,
        w_up,
        w_down,
    )
    shapes = (
        ((ROWS, CH), BF16),
        ((CH, 3 * CH), F32),
        ((CH, CH), F32),
        ((CH, FFN), F32),
        ((FFN, CH), F32),
    )
    out = pl.pallas_call(
        functools.partial(finish, grad_scale),
        out_shape=tuple(jax.ShapeDtypeStruct(*shape) for shape in shapes)
        + (jax.ShapeDtypeStruct((1, CH), F32),) * 2,
        in_specs=[hbm] * 5,
        out_specs=[anywhere] * 5 + [vmem] * 2,
        scratch_shapes=[
            units(256),
            units(128),
            units(n_pts),
            rows(8, F32),
            pltpu.VMEM((8, CH), F32),
        ]
        + [pltpu.VMEM(*shape) for shape in shapes]
        + [sem((6,)), sem((5,))],
        compiler_params=pltpu.CompilerParams(vmem_limit_bytes=60 * 1024 * 1024),
    )(*parts)
    dx, grad_qkv, grad_proj, grad_up, grad_down, gain_one_grad, gain_two_grad = out
    return (
        dx,
        grad_qkv,
        grad_proj,
        grad_up,
        grad_down,
        gain_one_grad.reshape(CH),
        gain_two_grad.reshape(CH),
    )


def solution(mesh):
    placed = (
        P(("pts", "quad"), None),
        P(("pts", "quad"), None),
        P(("pts", "quad")),
        P(("pts", "quad")),
        P(("pts", "quad")),
        P(),
        P(),
        P(),
        P(),
        P(),
        P(),
    )
    return jax.shard_map(
        shards,
        mesh=mesh,
        in_specs=placed,
        out_specs=(P(("pts", "quad"), None), P(), P(), P(), P(), P(), P()),
        check_vma=False,
    )
```
